1024 devices in a mesh: gx: 16 (over z_hi, y), gy: 4 (over x), gz: 16 (over z_lo, core).
Axes of the slice: x: 4, y: 8, z: 16 (z_hi: 2, z_lo: 8; z = z_hi * 8 + z_lo), core: 2. Of those that a mesh axis runs over, the one named last changes fastest.
Arguments:
- orbitals: float32 [8, 128, 32, 2048], P(None, 'gx', 'gy', 'gz'), may hold values from -6 to 6
- potential: float32 [128, 32, 2048], P('gx', 'gy', 'gz'), may hold values from -3 to 0
- proj_values: float32 [4, 2097152], P(None, ('gx', 'gy', 'gz')), may hold values from -1 to 1
- point_cell: int32 [2097152], P(('gx', 'gy', 'gz')), may hold values from 0 to 8191
- point_owner: int32 [2097152], P(('gx', 'gy', 'gz')), may hold values from 0 to 1023, as said below
- point_slot: int32 [2097152], P(('gx', 'gy', 'gz')), may hold values from 0 to 4
- point_count: int32 [1024], P(('gx', 'gy', 'gz')), may hold values from 1 to 2048, 1310720 in all
- atom_energy: float32 [4, 5120], replicated, may hold values from -2 to 2
Outputs:
- filtered: float32 [8, 128, 32, 2048], P(None, 'gx', 'gy', 'gz')
The draws below stay inside these ranges and needn't reach their ends.
Inputs may be any that keep to these rules, and one draw needn't show every extreme that they name: `point_owner`: the owner of point i's atom differs from domain i // 2048 by at most one index along each of gx, gy and gz, counted periodically. Only the first point_count[d] of domain d's 2048 point slots are live; some domain has all of them live.
All inputs are finite; a program needn't handle non-finite values. No bound on the sum of `point_count` on one device may be relied on, other than what follows from the above.
Results may differ from the reference program's by a relative error of at most 0.0001.
Values sent between devices are 32-bit elements; how exact they have to be, the bound alone decides.
No kernel may reach another device: no remote copies, remote signals or barrier semaphores. Data moves between devices by JAX's collectives and lax.ppermute only.
A program may use at most 64 MiB of HBM per device.

```python
import math
import jax
import jax.numpy as jnp
import numpy as np
from jax import lax

NORB = 8
NPROJ = 4
DEGREE = 3
CX = 8
CY = 8
CZ = 128
PTS_DEV = 2048
ATOM_DEV = 5
NX = 128
NY = 32
NZ = 2048
ATOMS = 5120
POINTS = 2097152
N_GX = 16
N_GY = 4
N_GZ = 16
DEVICES = 1024


def draw_point_owner(key, part):
    key = jax.random.fold_in(key, 7)
    point_total = DEVICES * PTS_DEV
    domain = jnp.arange(point_total, dtype=jnp.int32) // PTS_DEV
    domain_x = domain // (N_GY * N_GZ)
    domain_y = domain // N_GZ % N_GY
    domain_z = domain % N_GZ
    choices_drawn = jax.random.randint(key, (3, point_total), 0, 4)
    moves = jnp.where(choices_drawn < 2, 0, 2 * choices_drawn - 5).astype(jnp.int32)
    owner_x = (domain_x + moves[0]) % N_GX
    owner_y = (domain_y + moves[1]) % N_GY
    owner_z = (domain_z + moves[2]) % N_GZ
    return ((owner_x * N_GY + owner_y) * N_GZ + owner_z).astype(jnp.int32)


def plant(result, own_key, low, top_value):
    longest = result.shape.index(max(result.shape))
    spots = []
    for shift in (0, 1):
        where = [jax.random.randint(jax.random.fold_in(own_key, axis), (), 0, length) for axis, length in enumerate(result.shape)]
        where[longest] = (where[longest] + shift) % result.shape[longest]
        spots.append(tuple(where))
    return result.at[spots[0]].set(low).at[spots[1]].set(top_value)


def levels(key, dims, shards, least, top_value):
    loudness, own = 1.0, jax.random.fold_in(key, 6)
    for position, shards_of in shards:
        heights = jnp.exp(jax.random.uniform(jax.random.fold_in(own, position), (shards_of,), jnp.float32, least / len(shards), top_value / len(shards)))
        loudness = loudness * jnp.repeat(heights, dims[position] // shards_of).reshape([-1 if axis == position else 1 for axis in range(len(dims))])
    return loudness


def split_up(number_of, total, most, lean):
    weights = [(1 << 20) // math.isqrt(grade ** lean) + 1 for grade in range(2, number_of + 1)]
    spare, given = total - most - (number_of - 1), [1] * (number_of - 1)
    while spare > 0:
        free = [i for i in range(number_of - 1) if given[i] < most]
        whole, remaining = sum([weights[i] for i in free]), spare
        for i in free:
            more = min(most - given[i], max(1, remaining * weights[i] // whole), spare)
            given[i] = given[i] + more
            spare = spare - more
    return np.array([most] + given)


def uneven(key, number_of, total, most, skew):
    if number_of == 2:
        one = jax.random.randint(key, (), max(1, total - most), min(most, total - 1) + 1)
        return jnp.stack([one, total - one])
    lengths = jnp.asarray(split_up(number_of, total, most, skew), jnp.int32)
    couples = (number_of - 1) // 2
    giver, sink = lengths[1:1 + 2 * couples:2], lengths[2:2 + 2 * couples:2]
    slack = jnp.minimum(giver - 1, most - sink)
    moved = jax.random.randint(jax.random.fold_in(key, 1), (couples,), 0, 1 << 20) % (slack + 1)
    lengths = lengths.at[1:1 + 2 * couples:2].set(giver - moved).at[2:2 + 2 * couples:2].set(sink + moved)
    return lengths[jax.random.permutation(jax.random.fold_in(key, 2), number_of)]


def scatter_about(key, extent, width, limit, split=(), kind=jnp.bfloat16):
    entries = jax.random.normal(key, extent, jnp.float32) * width
    if len(split) > 0:
        entries = levels(key, extent, split, -0.22, 0.18) * entries
    return jnp.clip(entries, min=-limit, max=limit).astype(kind)


def setup_inputs(seed: int = 0) -> dict:
    key_list = jax.random.split(jax.random.key(seed), 9)
    orbitals = scatter_about(key_list[0], (NORB, NX, NY, NZ), 1.0, 6.0, ((1, 16), (2, 4), (3, 16)), jnp.float32)
    potential = jnp.clip(-3.0 + 3.0 * jax.random.uniform(key_list[1], (NX, NY, NZ), jnp.float32) ** levels(key_list[1], (NX, NY, NZ), ((0, 16), (1, 4), (2, 16)), -0.2, 0.2), -3.0, 0.0)
    proj_values = scatter_about(key_list[2], (NPROJ, POINTS), 0.16, 1.0, ((1, 1024),), jnp.float32)
    point_cell = plant(jax.random.randint(key_list[3], (POINTS,), 0, CX * CY * CZ), jax.random.fold_in(key_list[3], 1), 0, (CX * CY * CZ) - 1).astype(jnp.int32)
    point_owner = draw_point_owner(jax.random.fold_in(key_list[8], 71), 0)
    point_slot = plant(jax.random.randint(key_list[5], (POINTS,), 0, ATOM_DEV), jax.random.fold_in(key_list[5], 1), 0, ATOM_DEV - 1).astype(jnp.int32)
    point_count = uneven(key_list[6], DEVICES, DEVICES * PTS_DEV * 5 // 8, PTS_DEV, 2).astype(jnp.int32)
    atom_energy = jnp.clip(jax.random.uniform(key_list[7], (NPROJ, ATOMS), jnp.float32, -2.0, 2.0), -2.0, 2.0)
    return {"orbitals": orbitals, "potential": potential, "proj_values": proj_values, "point_cell": point_cell, "point_owner": point_owner, "point_slot": point_slot, "point_count": point_count, "atom_energy": atom_energy}


stencil_terms = (-5369.0 / 1800.0, 12.0 / 7.0, -15.0 / 56.0, 10.0 / 189.0, -1.0 / 112.0, 2.0 / 1925.0, -1.0 / 16632.0)
lowest = -3.5
cutoff = 1.5
highest = 13.0


def second_sum(padded, along_dim, length):
    def window(first_index):
        return lax.slice_in_dim(padded, first_index, first_index + length, axis=along_dim)

    summed = stencil_terms[0] * window(6)
    for offset in range(1, 7):
        summed = summed + stencil_terms[offset] * (window(6 + offset) + window(6 - offset))
    return summed


def reference(orbitals, potential, proj_values, point_cell, point_owner, point_slot, point_count, atom_energy):
    point_ids = jnp.arange(POINTS, dtype=jnp.int32)
    domain = point_ids // PTS_DEV
    domain_x = domain // (N_GY * N_GZ)
    domain_y = (domain // N_GZ) % N_GY
    domain_z = domain % N_GZ
    local_x = point_cell // (CY * CZ)
    local_y = (point_cell // CZ) % CY
    local_z = point_cell % CZ
    global_cell = ((domain_x * CX + local_x) * NY + domain_y * CY + local_y) * NZ + domain_z * CZ + local_z
    live_mask = ((point_ids % PTS_DEV) < point_count[domain]).astype(jnp.float32)
    masked = proj_values * live_mask[None, :]
    atom_index = point_owner * ATOM_DEV + point_slot

    def hamiltonian(grid_field):
        laplace = second_sum(jnp.pad(grid_field, ((6, 6), (0, 0), (0, 0)), mode="wrap"), 0, NX)
        laplace = laplace + second_sum(jnp.pad(grid_field, ((0, 0), (6, 6), (0, 0)), mode="wrap"), 1, NY)
        laplace = laplace + second_sum(jnp.pad(grid_field, ((0, 0), (0, 0), (6, 6)), mode="wrap"), 2, NZ)
        flattened = grid_field.reshape(-1)
        sampled = flattened[global_cell]
        contributions = (masked * sampled[None, :]).T
        alphas = jax.ops.segment_sum(contributions, atom_index, num_segments=ATOMS)
        coefficients = alphas * atom_energy.T
        returned = jnp.sum(masked.T * coefficients[atom_index], axis=1)
        nonlocal_term = jnp.zeros_like(flattened).at[global_cell].add(returned).reshape(grid_field.shape)
        return -0.5 * laplace + potential * grid_field + nonlocal_term

    def filter_one(grid_field):
        half_width = (highest - cutoff) / 2.0
        middle = (highest + cutoff) / 2.0
        sigma_first = half_width / (lowest - middle)
        previous = grid_field
        current = (sigma_first / half_width) * (hamiltonian(grid_field) - middle * grid_field)
        sigma_now = sigma_first
        for degree_index in range(1, DEGREE):
            sigma_next = 1.0 / (2.0 / sigma_first - sigma_now)
            following = (2.0 * sigma_next / half_width) * (hamiltonian(current) - middle * current) - (sigma_now * sigma_next) * previous
            previous = current
            current = following
            sigma_now = sigma_next
        return current

    return lax.map(filter_one, orbitals)
```

```python
import jax
import jax.numpy as jnp
from jax import lax
from jax.experimental import pallas as pl
from jax.experimental.pallas import tpu as pltpu
from jax.sharding import PartitionSpec as P

DEGREE = 3
ATOM_DEV = 5
NORB = 8
NPROJ = 4
SIDE = 8
DEPTH = 128
HALO = 6
ROWS = NORB * SIDE * SIDE
PLANES = 9
SEGS = PLANES * 8
CHUNK = 256
POS_Y = 4
VMEM_LIMIT = 56 * 1024 * 1024

stencil_terms = (
    -5369.0 / 1800.0,
    12.0 / 7.0,
    -15.0 / 56.0,
    10.0 / 189.0,
    -1.0 / 112.0,
    2.0 / 1925.0,
    -1.0 / 16632.0,
)
lowest = -3.5
cutoff = 1.5
highest = 13.0

F32 = jnp.float32
BF16 = jnp.bfloat16
LAST = (((1,), (1,)), ((), ()))
FIRST = (((0,), (0,)), ((), ()))


def iota(shape, dim):
    return lax.broadcasted_iota(jnp.int32, shape, dim)


def one_hot(index_row, rows, kind):
    hit = iota((rows, index_row.shape[1]), 0) == index_row
    return jnp.where(hit, 1.0, 0.0).astype(kind)


def split_two(value):
    upper = value.astype(BF16)
    return upper, (value - upper.astype(F32)).astype(BF16)


def sample_partials(cells, idx_ref, wts_ref):
    upper, lower = split_two(cells)
    both = jnp.concatenate([upper, lower], axis=1)
    points = idx_ref.shape[1]
    total = jnp.zeros((SEGS + 8, 128), F32)
    for first in range(0, points, CHUNK):
        span = slice(first, first + CHUNK)
        hot_z = one_hot(idx_ref[0:1, span], DEPTH, BF16)
        picked = jnp.dot(both, jnp.concatenate([hot_z, hot_z], axis=0), preferred_element_type=F32)
        mask = iota((SIDE * SIDE, CHUNK), 0) == idx_ref[1:2, span]
        picked = picked.reshape(NORB, SIDE * SIDE, CHUNK)
        sampled = jnp.sum(jnp.where(mask[None], picked, 0.0), axis=1)
        weights = wts_ref[:, span]
        parts = [weights[k : k + 1] * sampled for k in range(POS_Y * NPROJ)]
        upper_c, lower_c = split_two(jnp.concatenate(parts, axis=0))
        hot_seg = one_hot(idx_ref[2:3, span], SEGS + 8, BF16)
        total = total + lax.dot_general(hot_seg, upper_c, LAST, preferred_element_type=F32)
        total = total + lax.dot_general(hot_seg, lower_c, LAST, preferred_element_type=F32)
    return total[:SEGS]


def scatter_returned(coefs, idx_ref, wts_ref, nonlocal_ref):
    wide = jnp.concatenate([coefs, jnp.zeros((128 - SEGS, 128), F32)], axis=0)
    upper, lower = split_two(wide.T)
    both = jnp.concatenate([upper, lower], axis=1)
    points = idx_ref.shape[1]
    for first in range(0, points, CHUNK):
        span = slice(first, first + CHUNK)
        hot_seg = one_hot(idx_ref[2:3, span], 128, BF16)
        spread = jnp.dot(both, jnp.concatenate([hot_seg, hot_seg], axis=0), preferred_element_type=F32)
        weights = wts_ref[:, span]
        returned = weights[0:1] * spread[0:NORB]
        for k in range(1, POS_Y * NPROJ):
            returned = returned + weights[k : k + 1] * spread[k * NORB : (k + 1) * NORB]
        upper_r = returned.astype(BF16).astype(F32)
        lower_r = returned - upper_r
        mask = iota((SIDE * SIDE, CHUNK), 0) == idx_ref[1:2, span]
        tall = [
            jnp.where(mask, value[o : o + 1], 0.0).astype(BF16)
            for value in (upper_r, lower_r)
            for o in range(NORB)
        ]
        hot_z = one_hot(idx_ref[0:1, span], DEPTH, BF16)
        placed = lax.dot_general(
            jnp.concatenate(tall, axis=0), hot_z, LAST, preferred_element_type=F32
        )
        placed = placed[:ROWS] + placed[ROWS:]
        if first == 0:
            nonlocal_ref[...] = placed
        else:
            nonlocal_ref[...] += placed


def write_sends(coord_ref, cells_ref, xa_ref, xb_ref, za_ref, zb_ref):
    bx, bz = coord_ref[3], coord_ref[5]
    xa_ref[...] = cells_ref[:, pl.ds(2 - 2 * bx, HALO)]
    xb_ref[...] = cells_ref[:, pl.ds(2 * bx, HALO)]
    turned = cells_ref[...].reshape(ROWS, DEPTH).T
    near, far = turned[0:8], turned[DEPTH - 8 : DEPTH]
    to_a = jnp.where(bz == 1, near, far)
    to_b = jnp.where(bz == 1, far, near)
    for k in range(ROWS // 128):
        za_ref[k] = to_a[:, k * 128 : (k + 1) * 128]
        zb_ref[k] = to_b[:, k * 128 : (k + 1) * 128]


def offset_of(place, own, count):
    remain = (place - own) & (count - 1)
    return jnp.where(remain == 0, 1, jnp.where(remain == 1, 2, 0))


def first_kernel(
    sizes, coord_ref, cells_ref, proj_ref, cell_ref, owner_ref, slot_ref,
    part_ref, xa_ref, xb_ref, za_ref, zb_ref, idx_ref, wts_ref,
):
    size_x, size_y, size_z = sizes
    points = proj_ref.shape[1]
    shift_z = size_z.bit_length() - 1
    shift_x = shift_z + size_y.bit_length() - 1
    cell, owner = cell_ref[...], owner_ref[...]
    off_x = offset_of(owner >> shift_x, coord_ref[0], size_x)
    place_y = (owner >> shift_z) & (size_y - 1)
    off_z = offset_of(owner & (size_z - 1), coord_ref[2], size_z)
    idx_ref[0:1, :] = cell & (DEPTH - 1)
    idx_ref[1:2, :] = cell >> 7
    idx_ref[2:3, :] = (off_x * 3 + off_z) * 8 + slot_ref[...]
    idx_ref[3:8, :] = jnp.zeros((5, points), jnp.int32)
    live = iota((1, points), 1) < coord_ref[6]
    for position in range(POS_Y):
        here = jnp.logical_and(live, place_y == position)
        wts_ref[position * NPROJ : (position + 1) * NPROJ, :] = jnp.where(here, proj_ref[...], 0.0)
    part_ref[...] = sample_partials(cells_ref[...].reshape(ROWS, DEPTH), idx_ref, wts_ref)
    write_sends(coord_ref, cells_ref, xa_ref, xb_ref, za_ref, zb_ref)


def band(shape, distance):
    result = jnp.zeros(shape, F32)
    for k in range(1, HALO + 1):
        result = jnp.where(distance == k, stencil_terms[k], result)
    return result


def step_kernel(
    scales, last, coord_ref, cells_ref, *refs
):
    gain, middle, back = scales
    refs = list(refs)
    before_ref = refs.pop(0) if back else None
    (pot_ref, idx_ref, wts_ref, energy_ref, own_ref, px_ref, pz_ref,
     xa_in, xb_in, ya_in, yb_in, za_in, zb_in) = refs[:13]
    outs = refs[13:]
    if last:
        next_ref, nonlocal_ref, z_ref, xext, yext = outs
    else:
        (next_ref, part_ref, xa_ref, xb_ref, za_ref, zb_ref,
         nonlocal_ref, z_ref, xext, yext) = outs
    bx, by, bz = coord_ref[3], coord_ref[4], coord_ref[5]

    odd_x, odd_z = bx == 1, bz == 1
    own0, own1, other = own_ref[0], own_ref[1], px_ref[...]
    rows_x = (
        jnp.where(odd_x, other, own0),
        jnp.where(odd_x, own0, own1),
        jnp.where(odd_x, own1, other),
    )
    planes = []
    for k in range(3):
        low, high, beyond = rows_x[k][0], rows_x[k][1], pz_ref[k]
        planes += [
            jnp.where(odd_z, beyond, low),
            jnp.where(odd_z, low, high),
            jnp.where(odd_z, high, beyond),
        ]
    coefs = jnp.concatenate(planes, axis=0) * energy_ref[...]
    scatter_returned(coefs, idx_ref, wts_ref, nonlocal_ref)

    rows = cells_ref[...].reshape(ROWS, DEPTH)
    along = iota((DEPTH, DEPTH), 1) - iota((DEPTH, DEPTH), 0)
    z_part = jnp.dot(
        rows, band((DEPTH, DEPTH), jnp.abs(along)),
        precision=lax.Precision.HIGHEST, preferred_element_type=F32,
    )
    chunks = ROWS // 128
    from_a = jnp.concatenate([za_in[k] for k in range(chunks)], axis=1)
    from_b = jnp.concatenate([zb_in[k] for k in range(chunks)], axis=1)
    faces = jnp.concatenate(
        [jnp.where(odd_z, from_a, from_b), jnp.where(odd_z, from_b, from_a)], axis=0
    )
    face_row, face_col = iota((16, DEPTH), 0), iota((16, DEPTH), 1)
    distance = jnp.where(face_row < 8, face_col + 8 - face_row, DEPTH + face_row - 8 - face_col)
    z_ref[...] = z_part + jnp.dot(
        faces.T, band((16, DEPTH), distance),
        precision=lax.Precision.HIGHEST, preferred_element_type=F32,
    )

    xext[:, HALO : HALO + SIDE] = cells_ref[...]
    xext[:, pl.ds((1 - bx) * (HALO + SIDE), HALO)] = xa_in[...]
    xext[:, pl.ds(bx * (HALO + SIDE), HALO)] = xb_in[...]
    yext[1] = cells_ref[...]
    yext[2 - 2 * by] = ya_in[...]
    yext[2 * by] = yb_in[...]

    pot = pot_ref[...] - (middle + 1.5 * stencil_terms[0])
    row = iota((SIDE, SIDE, DEPTH), 1)
    for o in range(NORB):
        here = xext[o, HALO : HALO + SIDE]
        left, right = yext[0, o], yext[2, o]
        laplace = z_ref[o * 64 : (o + 1) * 64, :].reshape(SIDE, SIDE, DEPTH)
        for k in range(1, HALO + 1):
            pair = xext[o, HALO + k : HALO + k + SIDE] + xext[o, HALO - k : HALO - k + SIDE]
            up = pltpu.roll(jnp.where(row < k, right, here), SIDE - k, 1)
            down = pltpu.roll(jnp.where(row >= SIDE - k, left, here), k, 1)
            laplace = laplace + stencil_terms[k] * (pair + (up + down))
        nonlocal_part = nonlocal_ref[o * 64 : (o + 1) * 64, :].reshape(SIDE, SIDE, DEPTH)
        result = gain * (pot * here - 0.5 * laplace + nonlocal_part)
        if back:
            result = result - back * before_ref[o]
        next_ref[o] = result
    if not last:
        part_ref[...] = sample_partials(next_ref[...].reshape(ROWS, DEPTH), idx_ref, wts_ref)
        write_sends(coord_ref, next_ref, xa_ref, xb_ref, za_ref, zb_ref)


def energy_kernel(sizes, coord_ref, energy_ref, table_ref):
    size_x, size_y, size_z = sizes
    atoms = energy_ref.shape[1]
    values = jnp.concatenate(
        [jnp.broadcast_to(energy_ref[j : j + 1, :], (NORB, atoms)) for j in range(NPROJ)], axis=0
    )
    upper = values.astype(BF16)
    rest = values - upper.astype(F32)
    middle = rest.astype(BF16)
    lower = (rest - middle.astype(F32)).astype(BF16)
    row = iota((SEGS + 8, 1), 0)
    plane, slot = row >> 3, row & 7
    off_x = jnp.where(plane >= 6, 1, jnp.where(plane >= 3, 0, -1))
    off_z = plane - 3 * (off_x + 1) - 1
    place_x = (coord_ref[0] + off_x) & (size_x - 1)
    place_z = (coord_ref[2] + off_z) & (size_z - 1)
    used = jnp.logical_and(slot < ATOM_DEV, row < SEGS)
    columns = []
    for position in range(POS_Y):
        atom = ((place_x * size_y + position) * size_z + place_z) * ATOM_DEV + slot
        atom = jnp.where(used, atom, -1)
        hot = jnp.where(iota((SEGS + 8, atoms), 1) == atom, 1.0, 0.0).astype(BF16)
        column = lax.dot_general(hot, lower, LAST, preferred_element_type=F32)
        column = column + lax.dot_general(hot, middle, LAST, preferred_element_type=F32)
        columns.append(column + lax.dot_general(hot, upper, LAST, preferred_element_type=F32))
    table_ref[...] = jnp.concatenate(columns, axis=1)[:SEGS]


def in_vmem(count):
    return [pl.BlockSpec(memory_space=pltpu.VMEM)] * count


def call(kernel, shapes, scratch, cost, *operands):
    flops, traffic = cost
    return pl.pallas_call(
        kernel,
        out_shape=[jax.ShapeDtypeStruct(s, k) for s, k in shapes],
        in_specs=[pl.BlockSpec(memory_space=pltpu.SMEM)] + in_vmem(len(operands) - 1),
        out_specs=in_vmem(len(shapes)),
        scratch_shapes=scratch,
        compiler_params=pltpu.CompilerParams(vmem_limit_bytes=VMEM_LIMIT),
        cost_estimate=pl.CostEstimate(flops=flops, bytes_accessed=traffic, transcendentals=0),
    )(*operands)


def swap_inside(value, axis):
    count = lax.axis_size(axis)
    return lax.ppermute(value, axis, [(i, i ^ 1) for i in range(count)])


def swap_across(value, axis):
    count = lax.axis_size(axis)
    pairs = [(i, (i + 1 if i % 2 else i - 1) % count) for i in range(count)]
    return lax.ppermute(value, axis, pairs)


def body(
    orbitals, potential, proj_values, point_cell, point_owner, point_slot, point_count, atom_energy
):
    sizes = tuple(lax.axis_size(axis) for axis in ("gx", "gy", "gz"))
    places = [lax.axis_index(axis) for axis in ("gx", "gy", "gz")]
    points = proj_values.shape[1]
    coord = jnp.stack(
        [p.astype(jnp.int32) for p in places]
        + [(p % 2).astype(jnp.int32) for p in places]
        + [point_count[0], jnp.int32(0)]
    )
    odd_x, odd_z = places[0] % 2 == 1, places[2] % 2 == 1

    cells_shape = orbitals.shape
    x_shape = (NORB, HALO, SIDE, DEPTH)
    z_shape = (ROWS // 128, 8, 128)
    send_shapes = [
        ((SEGS, 128), F32), (x_shape, F32), (x_shape, F32), (z_shape, F32), (z_shape, F32)
    ]

    parts, xa, xb, za, zb, idx, wts = call(
        lambda *refs: first_kernel(sizes, *refs),
        send_shapes + [((8, points), jnp.int32), ((POS_Y * NPROJ, points), F32)],
        [], (600_000_000, 2_000_000),
        coord, orbitals, proj_values,
        point_cell.reshape(1, points), point_owner.reshape(1, points), point_slot.reshape(1, points),
    )
    (energy,) = call(
        lambda *refs: energy_kernel(sizes, *refs), [((SEGS, 128), F32)], [],
        (600_000_000, 200_000), coord, atom_energy,
    )

    def exchange(parts, cells, xa, xb, za, zb):
        table = parts.reshape(3, 3, 8, 128)
        come = swap_inside(jnp.where(odd_x, table[0], table[2]), "gx")
        middle = table[1] + come
        pair = jnp.where(odd_x, jnp.stack([middle, table[2]]), jnp.stack([table[0], middle]))
        pair = pair + swap_across(pair, "gx")
        xb = swap_across(xb, "gx")

        come = swap_inside(
            jnp.concatenate([jnp.where(odd_z, pair[:, 0], pair[:, 2]), za], axis=0), "gz"
        )
        za = come[2:]
        middle = pair[:, 1] + come[:2]
        own = jnp.where(
            odd_z,
            jnp.stack([middle, pair[:, 2]], axis=1),
            jnp.stack([pair[:, 0], middle], axis=1),
        )
        come = swap_across(jnp.concatenate([own.reshape(4, 8, 128), zb], axis=0), "gz")
        zb = come[4:]
        own = own + come[:4].reshape(2, 2, 8, 128)

        own = own + swap_inside(own, "gy")
        own = own + swap_across(own, "gy")
        ya, yb = swap_inside(cells, "gy"), swap_across(cells, "gy")
        xa = swap_inside(xa, "gx")

        beyond_x = swap_inside(jnp.where(odd_x, own[0], own[1]), "gx")
        rows = jnp.where(
            odd_z,
            jnp.where(odd_x, jnp.stack([beyond_x[0], own[0, 0], own[1, 0]]),
                      jnp.stack([own[0, 0], own[1, 0], beyond_x[0]])),
            jnp.where(odd_x, jnp.stack([beyond_x[1], own[0, 1], own[1, 1]]),
                      jnp.stack([own[0, 1], own[1, 1], beyond_x[1]])),
        )
        beyond_z = swap_inside(rows, "gz")
        return own, beyond_x, beyond_z, xa, xb, ya, yb, za, zb

    half_width = (highest - cutoff) / 2.0
    middle = (highest + cutoff) / 2.0
    sigma_first = half_width / (lowest - middle)
    sigma_now = sigma_first
    previous, current = None, orbitals
    scratch = [
        pltpu.VMEM((ROWS, DEPTH), F32),
        pltpu.VMEM((ROWS, DEPTH), F32),
        pltpu.VMEM((NORB, SIDE + 2 * HALO, SIDE, DEPTH), F32),
        pltpu.VMEM((3, NORB, SIDE, SIDE, DEPTH), F32),
    ]
    for degree_index in range(DEGREE):
        if degree_index == 0:
            scales = (sigma_first / half_width, middle, 0.0)
        else:
            sigma_next = 1.0 / (2.0 / sigma_first - sigma_now)
            scales = (2.0 * sigma_next / half_width, middle, sigma_now * sigma_next)
            sigma_now = sigma_next
        last = degree_index == DEGREE - 1
        came = exchange(parts, current, xa, xb, za, zb)
        before = [] if previous is None else [previous]
        results = call(
            lambda *refs, scales=scales, last=last: step_kernel(scales, last, *refs),
            [(cells_shape, F32)] + ([] if last else send_shapes),
            scratch, (1_500_000_000, 4_000_000),
            coord, current, *before, potential, idx, wts, energy, *came,
        )
        previous, current = current, results[0]
        if not last:
            parts, xa, xb, za, zb = results[1:]
    return current


def solution(mesh):
    return jax.shard_map(
        body,
        mesh=mesh,
        in_specs=(
            P(None, "gx", "gy", "gz"),
            P("gx", "gy", "gz"),
            P(None, ("gx", "gy", "gz")),
            P(("gx", "gy", "gz")),
            P(("gx", "gy", "gz")),
            P(("gx", "gy", "gz")),
            P(("gx", "gy", "gz")),
            P(),
        ),
        out_specs=P(None, "gx", "gy", "gz"),
        check_vma=False,
    )
```

```python
import jax
import jax.numpy as jnp
from jax import lax
from jax.experimental import pallas as pl
from jax.experimental.pallas import tpu as pltpu
from jax.sharding import PartitionSpec as P

DEGREE = 3
ATOM_DEV = 5
NORB = 8
NPROJ = 4
SIDE = 8
DEPTH = 128
HALO = 6
FACE = NORB * HALO
ROWS = NORB * SIDE * SIDE
PLANES = 9
SEGS = PLANES * 8
CHUNK = 256
POS_Y = 4
VMEM_LIMIT = 20 * 1024 * 1024

stencil_terms = (
    -5369.0 / 1800.0,
    12.0 / 7.0,
    -15.0 / 56.0,
    10.0 / 189.0,
    -1.0 / 112.0,
    2.0 / 1925.0,
    -1.0 / 16632.0,
)
lowest = -3.5
cutoff = 1.5
highest = 13.0

F32 = jnp.float32
BF16 = jnp.bfloat16
LAST = (((1,), (1,)), ((), ()))
FIRST = (((0,), (0,)), ((), ()))


def iota(shape, dim):
    return lax.broadcasted_iota(jnp.int32, shape, dim)


def one_hot(index_row, rows, kind):
    hit = iota((rows, index_row.shape[1]), 0) == index_row
    return jnp.where(hit, 1.0, 0.0).astype(kind)


def split_two(value):
    upper = value.astype(BF16)
    return upper, (value - upper.astype(F32)).astype(BF16)


def sample_partials(cells, idx_ref, wts_ref):
    upper, lower = split_two(cells)
    both = jnp.concatenate([upper, lower], axis=1)
    points = idx_ref.shape[1]
    total = jnp.zeros((SEGS + 8, 128), F32)
    for first in range(0, points, CHUNK):
        span = slice(first, first + CHUNK)
        hot_z = one_hot(idx_ref[0:1, span], DEPTH, BF16)
        picked = jnp.dot(both, jnp.concatenate([hot_z, hot_z], axis=0), preferred_element_type=F32)
        mask = iota((SIDE * SIDE, CHUNK), 0) == idx_ref[1:2, span]
        picked = picked.reshape(NORB, SIDE * SIDE, CHUNK)
        sampled = jnp.sum(jnp.where(mask[None], picked, 0.0), axis=1)
        weights = wts_ref[:, span]
        parts = [weights[k : k + 1] * sampled for k in range(POS_Y * NPROJ)]
        upper_c, lower_c = split_two(jnp.concatenate(parts, axis=0))
        hot_seg = one_hot(idx_ref[2:3, span], SEGS + 8, BF16)
        total = total + lax.dot_general(hot_seg, upper_c, LAST, preferred_element_type=F32)
        total = total + lax.dot_general(hot_seg, lower_c, LAST, preferred_element_type=F32)
    return total[:SEGS]


def scatter_returned(coefs, idx_ref, wts_ref, nonlocal_ref):
    wide = jnp.concatenate([coefs, jnp.zeros((128 - SEGS, 128), F32)], axis=0)
    upper, lower = split_two(wide.T)
    both = jnp.concatenate([upper, lower], axis=1)
    points = idx_ref.shape[1]
    for first in range(0, points, CHUNK):
        span = slice(first, first + CHUNK)
        hot_seg = one_hot(idx_ref[2:3, span], 128, BF16)
        spread = jnp.dot(both, jnp.concatenate([hot_seg, hot_seg], axis=0), preferred_element_type=F32)
        weights = wts_ref[:, span]
        returned = weights[0:1] * spread[0:NORB]
        for k in range(1, POS_Y * NPROJ):
            returned = returned + weights[k : k + 1] * spread[k * NORB : (k + 1) * NORB]
        upper_r = returned.astype(BF16).astype(F32)
        lower_r = returned - upper_r
        mask = iota((SIDE * SIDE, CHUNK), 0) == idx_ref[1:2, span]
        tall = [
            jnp.where(mask, value[o : o + 1], 0.0).astype(BF16)
            for value in (upper_r, lower_r)
            for o in range(NORB)
        ]
        hot_z = one_hot(idx_ref[0:1, span], DEPTH, BF16)
        placed = lax.dot_general(
            jnp.concatenate(tall, axis=0), hot_z, LAST, preferred_element_type=F32
        )
        placed = placed[:ROWS] + placed[ROWS:]
        if first == 0:
            nonlocal_ref[...] = placed
        else:
            nonlocal_ref[...] += placed


def write_parts(coord_ref, table, send_ref, xb_ref):
    rows = SEGS // 3
    odd_x = coord_ref[3] == 1
    below, same, above = table[:rows], table[rows : 2 * rows], table[2 * rows :]
    send_ref[...] = jnp.where(odd_x, below, above)
    kept = [jnp.where(odd_x, same, below), jnp.where(odd_x, above, same)]
    xb_ref[FACE:] = jnp.concatenate(kept, axis=0).reshape(6, SIDE, DEPTH)


def write_sends(coord_ref, cells_ref, xa_ref, xb_ref, za_ref, zb_ref):
    bx, bz = coord_ref[3], coord_ref[5]
    xa_ref[...] = cells_ref[:, pl.ds(2 - 2 * bx, HALO)]
    xb_ref[:FACE] = cells_ref[:, pl.ds(2 * bx, HALO)].reshape(FACE, SIDE, DEPTH)
    turned = cells_ref[...].reshape(ROWS, DEPTH).T
    near, far = turned[0:8], turned[DEPTH - 8 : DEPTH]
    to_a = jnp.where(bz == 1, near, far)
    to_b = jnp.where(bz == 1, far, near)
    for k in range(ROWS // 128):
        za_ref[k] = to_a[:, k * 128 : (k + 1) * 128]
        zb_ref[k] = to_b[:, k * 128 : (k + 1) * 128]


def offset_of(place, own, count):
    remain = (place - own) & (count - 1)
    return jnp.where(remain == 0, 1, jnp.where(remain == 1, 2, 0))


def first_kernel(
    sizes, coord_ref, cells_ref, proj_ref, cell_ref, owner_ref, slot_ref,
    give_ref, xa_ref, xb_ref, za_ref, zb_ref, idx_ref, wts_ref,
):
    size_x, size_y, size_z = sizes
    points = proj_ref.shape[1]
    shift_z = size_z.bit_length() - 1
    shift_x = shift_z + size_y.bit_length() - 1
    cell, owner = cell_ref[...], owner_ref[...]
    off_x = offset_of(owner >> shift_x, coord_ref[0], size_x)
    place_y = (owner >> shift_z) & (size_y - 1)
    off_z = offset_of(owner & (size_z - 1), coord_ref[2], size_z)
    idx_ref[0:1, :] = cell & (DEPTH - 1)
    idx_ref[1:2, :] = cell >> 7
    idx_ref[2:3, :] = (off_x * 3 + off_z) * 8 + slot_ref[...]
    idx_ref[3:8, :] = jnp.zeros((5, points), jnp.int32)
    live = iota((1, points), 1) < coord_ref[6]
    for position in range(POS_Y):
        here = jnp.logical_and(live, place_y == position)
        wts_ref[position * NPROJ : (position + 1) * NPROJ, :] = jnp.where(here, proj_ref[...], 0.0)
    table = sample_partials(cells_ref[...].reshape(ROWS, DEPTH), idx_ref, wts_ref)
    write_parts(coord_ref, table, give_ref, xb_ref)
    write_sends(coord_ref, cells_ref, xa_ref, xb_ref, za_ref, zb_ref)


def band(shape, distance):
    result = jnp.zeros(shape, F32)
    for k in range(1, HALO + 1):
        result = jnp.where(distance == k, stencil_terms[k], result)
    return result


def step_kernel(
    scales, last, coord_ref, cells_ref, *refs
):
    gain, middle, back = scales
    refs = list(refs)
    before_ref = refs.pop(0) if back else None
    (pot_ref, idx_ref, wts_ref, energy_ref, own_ref, px_ref, pz_ref,
     xa_in, xb_in, ya_in, yb_in, za_in, zb_in) = refs[:13]
    outs = refs[13:]
    if last:
        next_ref, nonlocal_ref, z_ref, xext, yext = outs
    else:
        (next_ref, give_ref, xa_ref, xb_ref, za_ref, zb_ref,
         nonlocal_ref, z_ref, xext, yext) = outs
    bx, by, bz = coord_ref[3], coord_ref[4], coord_ref[5]

    odd_x, odd_z = bx == 1, bz == 1
    own0, own1, other = own_ref[0], own_ref[1], px_ref[...]
    rows_x = (
        jnp.where(odd_x, other, own0),
        jnp.where(odd_x, own0, own1),
        jnp.where(odd_x, own1, other),
    )
    planes = []
    for k in range(3):
        low, high, beyond = rows_x[k][0], rows_x[k][1], pz_ref[k]
        planes += [
            jnp.where(odd_z, beyond, low),
            jnp.where(odd_z, low, high),
            jnp.where(odd_z, high, beyond),
        ]
    coefs = jnp.concatenate(planes, axis=0) * energy_ref[...]
    scatter_returned(coefs, idx_ref, wts_ref, nonlocal_ref)

    rows = cells_ref[...].reshape(ROWS, DEPTH)
    along = iota((DEPTH, DEPTH), 1) - iota((DEPTH, DEPTH), 0)
    z_part = jnp.dot(
        rows, band((DEPTH, DEPTH), jnp.abs(along)),
        precision=lax.Precision.HIGHEST, preferred_element_type=F32,
    )
    chunks = ROWS // 128
    from_a = jnp.concatenate([za_in[k] for k in range(chunks)], axis=1)
    from_b = jnp.concatenate([zb_in[k] for k in range(chunks)], axis=1)
    faces = jnp.concatenate(
        [jnp.where(odd_z, from_a, from_b), jnp.where(odd_z, from_b, from_a)], axis=0
    )
    face_row, face_col = iota((16, DEPTH), 0), iota((16, DEPTH), 1)
    distance = jnp.where(face_row < 8, face_col + 8 - face_row, DEPTH + face_row - 8 - face_col)
    z_ref[...] = z_part + jnp.dot(
        faces.T, band((16, DEPTH), distance),
        precision=lax.Precision.HIGHEST, preferred_element_type=F32,
    )

    xext[:, HALO : HALO + SIDE] = cells_ref[...]
    xext[:, pl.ds((1 - bx) * (HALO + SIDE), HALO)] = xa_in[...]
    xext[:, pl.ds(bx * (HALO + SIDE), HALO)] = xb_in[:FACE].reshape(NORB, HALO, SIDE, DEPTH)
    yext[1] = cells_ref[...]
    yext[2 - 2 * by] = ya_in[...]
    yext[2 * by] = yb_in[...]

    pot = pot_ref[...] - (middle + 1.5 * stencil_terms[0])
    row = iota((SIDE, SIDE, DEPTH), 1)
    for o in range(NORB):
        here = xext[o, HALO : HALO + SIDE]
        left, right = yext[0, o], yext[2, o]
        laplace = z_ref[o * 64 : (o + 1) * 64, :].reshape(SIDE, SIDE, DEPTH)
        for k in range(1, HALO + 1):
            pair = xext[o, HALO + k : HALO + k + SIDE] + xext[o, HALO - k : HALO - k + SIDE]
            up = pltpu.roll(jnp.where(row < k, right, here), SIDE - k, 1)
            down = pltpu.roll(jnp.where(row >= SIDE - k, left, here), k, 1)
            laplace = laplace + stencil_terms[k] * (pair + (up + down))
        nonlocal_part = nonlocal_ref[o * 64 : (o + 1) * 64, :].reshape(SIDE, SIDE, DEPTH)
        result = gain * (pot * here - 0.5 * laplace + nonlocal_part)
        if back:
            result = result - back * before_ref[o]
        next_ref[o] = result
    if not last:
        table = sample_partials(next_ref[...].reshape(ROWS, DEPTH), idx_ref, wts_ref)
        write_parts(coord_ref, table, give_ref, xb_ref)
        write_sends(coord_ref, next_ref, xa_ref, xb_ref, za_ref, zb_ref)


def energy_kernel(sizes, coord_ref, energy_ref, table_ref):
    size_x, size_y, size_z = sizes
    atoms = energy_ref.shape[1]
    values = jnp.concatenate(
        [jnp.broadcast_to(energy_ref[j : j + 1, :], (NORB, atoms)) for j in range(NPROJ)], axis=0
    )
    upper = values.astype(BF16)
    rest = values - upper.astype(F32)
    middle = rest.astype(BF16)
    lower = (rest - middle.astype(F32)).astype(BF16)
    row = iota((SEGS + 8, 1), 0)
    plane, slot = row >> 3, row & 7
    off_x = jnp.where(plane >= 6, 1, jnp.where(plane >= 3, 0, -1))
    off_z = plane - 3 * (off_x + 1) - 1
    place_x = (coord_ref[0] + off_x) & (size_x - 1)
    place_z = (coord_ref[2] + off_z) & (size_z - 1)
    used = jnp.logical_and(slot < ATOM_DEV, row < SEGS)
    columns = []
    for position in range(POS_Y):
        atom = ((place_x * size_y + position) * size_z + place_z) * ATOM_DEV + slot
        atom = jnp.where(used, atom, -1)
        hot = jnp.where(iota((SEGS + 8, atoms), 1) == atom, 1.0, 0.0).astype(BF16)
        column = lax.dot_general(hot, lower, LAST, preferred_element_type=F32)
        column = column + lax.dot_general(hot, middle, LAST, preferred_element_type=F32)
        columns.append(column + lax.dot_general(hot, upper, LAST, preferred_element_type=F32))
    table_ref[...] = jnp.concatenate(columns, axis=1)[:SEGS]


def in_vmem(count):
    return [pl.BlockSpec(memory_space=pltpu.VMEM)] * count


def call(kernel, shapes, scratch, cost, *operands):
    flops, traffic = cost
    return pl.pallas_call(
        kernel,
        out_shape=[jax.ShapeDtypeStruct(s, k) for s, k in shapes],
        in_specs=[pl.BlockSpec(memory_space=pltpu.SMEM)] + in_vmem(len(operands) - 1),
        out_specs=in_vmem(len(shapes)),
        scratch_shapes=scratch,
        compiler_params=pltpu.CompilerParams(vmem_limit_bytes=VMEM_LIMIT),
        cost_estimate=pl.CostEstimate(flops=flops, bytes_accessed=traffic, transcendentals=0),
    )(*operands)


def swap_inside(value, axis):
    count = lax.axis_size(axis)
    return lax.ppermute(value, axis, [(i, i ^ 1) for i in range(count)])


def swap_across(value, axis):
    count = lax.axis_size(axis)
    pairs = [(i, (i + 1 if i % 2 else i - 1) % count) for i in range(count)]
    return lax.ppermute(value, axis, pairs)


def body(
    orbitals, potential, proj_values, point_cell, point_owner, point_slot, point_count, atom_energy
):
    sizes = tuple(lax.axis_size(axis) for axis in ("gx", "gy", "gz"))
    places = [lax.axis_index(axis) for axis in ("gx", "gy", "gz")]
    points = proj_values.shape[1]
    coord = jnp.stack(
        [p.astype(jnp.int32) for p in places]
        + [(p % 2).astype(jnp.int32) for p in places]
        + [point_count[0], jnp.int32(0)]
    )
    odd_x, odd_z = places[0] % 2 == 1, places[2] % 2 == 1

    cells_shape = orbitals.shape
    x_shape = (NORB, HALO, SIDE, DEPTH)
    z_shape = (ROWS // 128, 8, 128)
    send_shapes = [
        ((SEGS // 3, 128), F32), (x_shape, F32), ((FACE + 6, SIDE, DEPTH), F32), (z_shape, F32), (z_shape, F32)
    ]

    *sends, idx, wts = call(
        lambda *refs: first_kernel(sizes, *refs),
        send_shapes + [((8, points), jnp.int32), ((POS_Y * NPROJ, points), F32)],
        [], (600_000_000, 2_000_000),
        coord, orbitals, proj_values,
        point_cell.reshape(1, points), point_owner.reshape(1, points), point_slot.reshape(1, points),
    )
    (energy,) = call(
        lambda *refs: energy_kernel(sizes, *refs), [((SEGS, 128), F32)], [],
        (600_000_000, 200_000), coord, atom_energy,
    )

    def exchange(cells, give, xa, xb, za, zb, energy):
        come = swap_inside(give, "gx").reshape(1, 3, 8, 128)
        place = jnp.arange(2, dtype=jnp.int32)[:, None, None, None]
        pair = xb[FACE:].reshape(2, 3, 8, 128)
        pair = pair + jnp.where(place == 1 - places[0] % 2, come, 0.0)
        xb = lax.dynamic_update_slice(xb, pair.reshape(6, 8, 128), (FACE, 0, 0))
        xb, xa, cells = lax.optimization_barrier((xb, xa, cells))
        across = swap_across(xb, "gx")
        ya, yb = swap_inside(cells, "gy"), swap_across(cells, "gy")
        xa = swap_inside(xa, "gx")
        pair = (xb[FACE:] + across[FACE:]).reshape(2, 3, 8, 128)
        xb = across
        pair, energy, xa, ya, yb = lax.optimization_barrier((pair, energy, xa, ya, yb))
        pair = lax.psum(pair, "gy")

        come = swap_inside(
            jnp.concatenate([jnp.where(odd_z, pair[:, 0], pair[:, 2]), za], axis=0), "gz"
        )
        za = come[2:]
        middle = pair[:, 1] + come[:2]
        own = jnp.where(
            odd_z,
            jnp.stack([middle, pair[:, 2]], axis=1),
            jnp.stack([pair[:, 0], middle], axis=1),
        )
        come = swap_across(jnp.concatenate([own.reshape(4, 8, 128), zb], axis=0), "gz")
        zb = come[4:]
        own = own + come[:4].reshape(2, 2, 8, 128)

        beyond_x = swap_inside(jnp.where(odd_x, own[0], own[1]), "gx")
        rows = jnp.where(
            odd_z,
            jnp.where(odd_x, jnp.stack([beyond_x[0], own[0, 0], own[1, 0]]),
                      jnp.stack([own[0, 0], own[1, 0], beyond_x[0]])),
            jnp.where(odd_x, jnp.stack([beyond_x[1], own[0, 1], own[1, 1]]),
                      jnp.stack([own[0, 1], own[1, 1], beyond_x[1]])),
        )
        beyond_z = swap_inside(rows, "gz")
        return energy, own, beyond_x, beyond_z, xa, xb, ya, yb, za, zb

    half_width = (highest - cutoff) / 2.0
    middle = (highest + cutoff) / 2.0
    sigma_first = half_width / (lowest - middle)
    sigma_now = sigma_first
    previous, current = None, orbitals
    scratch = [
        pltpu.VMEM((ROWS, DEPTH), F32),
        pltpu.VMEM((ROWS, DEPTH), F32),
        pltpu.VMEM((NORB, SIDE + 2 * HALO, SIDE, DEPTH), F32),
        pltpu.VMEM((3, NORB, SIDE, SIDE, DEPTH), F32),
    ]
    for degree_index in range(DEGREE):
        if degree_index == 0:
            scales = (sigma_first / half_width, middle, 0.0)
        else:
            sigma_next = 1.0 / (2.0 / sigma_first - sigma_now)
            scales = (2.0 * sigma_next / half_width, middle, sigma_now * sigma_next)
            sigma_now = sigma_next
        last = degree_index == DEGREE - 1
        came = exchange(current, *sends, energy)
        before = [] if previous is None else [previous]
        results = call(
            lambda *refs, scales=scales, last=last: step_kernel(scales, last, *refs),
            [(cells_shape, F32)] + ([] if last else send_shapes),
            scratch, (1_500_000_000, 4_000_000),
            coord, current, *before, potential, idx, wts, *came,
        )
        previous, current = current, results[0]
        if not last:
            sends = results[1:]
    return current


def solution(mesh):
    return jax.shard_map(
        body,
        mesh=mesh,
        in_specs=(
            P(None, "gx", "gy", "gz"),
            P("gx", "gy", "gz"),
            P(None, ("gx", "gy", "gz")),
            P(("gx", "gy", "gz")),
            P(("gx", "gy", "gz")),
            P(("gx", "gy", "gz")),
            P(("gx", "gy", "gz")),
            P(),
        ),
        out_specs=P(None, "gx", "gy", "gz"),
        check_vma=False,
    )
```

```python
import jax
import jax.numpy as jnp
from jax import lax
from jax.experimental import pallas as pl
from jax.experimental.pallas import tpu as pltpu
from jax.sharding import PartitionSpec as P

DEGREE = 3
ATOM_DEV = 5
NORB = 8
NPROJ = 4
SIDE = 8
DEPTH = 128
HALO = 6
ROWS = NORB * SIDE * SIDE
PLANES = 9
SEGS = PLANES * 8
CHUNK = 256
POS_Y = 4
VMEM_LIMIT = 20 * 1024 * 1024

stencil_terms = (
    -5369.0 / 1800.0,
    12.0 / 7.0,
    -15.0 / 56.0,
    10.0 / 189.0,
    -1.0 / 112.0,
    2.0 / 1925.0,
    -1.0 / 16632.0,
)
lowest = -3.5
cutoff = 1.5
highest = 13.0

F32 = jnp.float32
BF16 = jnp.bfloat16
LAST = (((1,), (1,)), ((), ()))
FIRST = (((0,), (0,)), ((), ()))


def iota(shape, dim):
    return lax.broadcasted_iota(jnp.int32, shape, dim)


def one_hot(index_row, rows, kind):
    hit = iota((rows, index_row.shape[1]), 0) == index_row
    return jnp.where(hit, 1.0, 0.0).astype(kind)


def split_two(value):
    upper = value.astype(BF16)
    return upper, (value - upper.astype(F32)).astype(BF16)


def sample_partials(cells, idx_ref, wts_ref):
    upper, lower = split_two(cells)
    both = jnp.concatenate([upper, lower], axis=1)
    points = idx_ref.shape[1]
    total = jnp.zeros((SEGS + 8, 128), F32)
    for first in range(0, points, CHUNK):
        span = slice(first, first + CHUNK)
        hot_z = one_hot(idx_ref[0:1, span], DEPTH, BF16)
        picked = jnp.dot(both, jnp.concatenate([hot_z, hot_z], axis=0), preferred_element_type=F32)
        mask = iota((SIDE * SIDE, CHUNK), 0) == idx_ref[1:2, span]
        picked = picked.reshape(NORB, SIDE * SIDE, CHUNK)
        sampled = jnp.sum(jnp.where(mask[None], picked, 0.0), axis=1)
        weights = wts_ref[:, span]
        parts = [weights[k : k + 1] * sampled for k in range(POS_Y * NPROJ)]
        upper_c, lower_c = split_two(jnp.concatenate(parts, axis=0))
        hot_seg = one_hot(idx_ref[2:3, span], SEGS + 8, BF16)
        total = total + lax.dot_general(hot_seg, upper_c, LAST, preferred_element_type=F32)
        total = total + lax.dot_general(hot_seg, lower_c, LAST, preferred_element_type=F32)
    return total[:SEGS]


def scatter_returned(coefs, idx_ref, wts_ref, nonlocal_ref):
    wide = jnp.concatenate([coefs, jnp.zeros((128 - SEGS, 128), F32)], axis=0)
    upper, lower = split_two(wide.T)
    both = jnp.concatenate([upper, lower], axis=1)
    points = idx_ref.shape[1]
    for first in range(0, points, CHUNK):
        span = slice(first, first + CHUNK)
        hot_seg = one_hot(idx_ref[2:3, span], 128, BF16)
        spread = jnp.dot(both, jnp.concatenate([hot_seg, hot_seg], axis=0), preferred_element_type=F32)
        weights = wts_ref[:, span]
        returned = weights[0:1] * spread[0:NORB]
        for k in range(1, POS_Y * NPROJ):
            returned = returned + weights[k : k + 1] * spread[k * NORB : (k + 1) * NORB]
        upper_r = returned.astype(BF16).astype(F32)
        lower_r = returned - upper_r
        mask = iota((SIDE * SIDE, CHUNK), 0) == idx_ref[1:2, span]
        tall = [
            jnp.where(mask, value[o : o + 1], 0.0).astype(BF16)
            for value in (upper_r, lower_r)
            for o in range(NORB)
        ]
        hot_z = one_hot(idx_ref[0:1, span], DEPTH, BF16)
        placed = lax.dot_general(
            jnp.concatenate(tall, axis=0), hot_z, LAST, preferred_element_type=F32
        )
        placed = placed[:ROWS] + placed[ROWS:]
        if first == 0:
            nonlocal_ref[...] = placed
        else:
            nonlocal_ref[...] += placed


def write_parts(coord_ref, table, send_ref, keep_ref):
    rows = SEGS // 3
    odd_x = coord_ref[3] == 1
    below, same, above = table[:rows], table[rows : 2 * rows], table[2 * rows :]
    send_ref[...] = jnp.where(odd_x, below, above)
    kept = [jnp.where(odd_x, same, below), jnp.where(odd_x, above, same)]
    keep_ref[...] = jnp.concatenate(kept, axis=0)


def write_sends(coord_ref, cells_ref, xa_ref, xb_ref, za_ref, zb_ref):
    bx, bz = coord_ref[3], coord_ref[5]
    xa_ref[...] = cells_ref[:, pl.ds(2 - 2 * bx, HALO)]
    xb_ref[...] = cells_ref[:, pl.ds(2 * bx, HALO)]
    turned = cells_ref[...].reshape(ROWS, DEPTH).T
    near, far = turned[0:8], turned[DEPTH - 8 : DEPTH]
    to_a = jnp.where(bz == 1, near, far)
    to_b = jnp.where(bz == 1, far, near)
    for k in range(ROWS // 128):
        za_ref[k] = to_a[:, k * 128 : (k + 1) * 128]
        zb_ref[k] = to_b[:, k * 128 : (k + 1) * 128]


def offset_of(place, own, count):
    remain = (place - own) & (count - 1)
    return jnp.where(remain == 0, 1, jnp.where(remain == 1, 2, 0))


def first_kernel(
    sizes, coord_ref, cells_ref, proj_ref, cell_ref, owner_ref, slot_ref,
    give_ref, keep_ref, xa_ref, xb_ref, za_ref, zb_ref, idx_ref, wts_ref,
):
    size_x, size_y, size_z = sizes
    points = proj_ref.shape[1]
    shift_z = size_z.bit_length() - 1
    shift_x = shift_z + size_y.bit_length() - 1
    cell, owner = cell_ref[...], owner_ref[...]
    off_x = offset_of(owner >> shift_x, coord_ref[0], size_x)
    place_y = (owner >> shift_z) & (size_y - 1)
    off_z = offset_of(owner & (size_z - 1), coord_ref[2], size_z)
    idx_ref[0:1, :] = cell & (DEPTH - 1)
    idx_ref[1:2, :] = cell >> 7
    idx_ref[2:3, :] = (off_x * 3 + off_z) * 8 + slot_ref[...]
    idx_ref[3:8, :] = jnp.zeros((5, points), jnp.int32)
    live = iota((1, points), 1) < coord_ref[6]
    for position in range(POS_Y):
        here = jnp.logical_and(live, place_y == position)
        wts_ref[position * NPROJ : (position + 1) * NPROJ, :] = jnp.where(here, proj_ref[...], 0.0)
    table = sample_partials(cells_ref[...].reshape(ROWS, DEPTH), idx_ref, wts_ref)
    write_parts(coord_ref, table, give_ref, keep_ref)
    write_sends(coord_ref, cells_ref, xa_ref, xb_ref, za_ref, zb_ref)


def band(shape, distance):
    result = jnp.zeros(shape, F32)
    for k in range(1, HALO + 1):
        result = jnp.where(distance == k, stencil_terms[k], result)
    return result


def step_kernel(
    scales, last, coord_ref, cells_ref, *refs
):
    gain, middle, back = scales
    refs = list(refs)
    before_ref = refs.pop(0) if back else None
    (pot_ref, idx_ref, wts_ref, energy_ref, own_ref, px_ref, pz_ref,
     xa_in, xb_in, ya_in, yb_in, za_in, zb_in) = refs[:13]
    outs = refs[13:]
    if last:
        next_ref, nonlocal_ref, z_ref, xext, yext = outs
    else:
        (next_ref, give_ref, keep_ref, xa_ref, xb_ref, za_ref, zb_ref,
         nonlocal_ref, z_ref, xext, yext) = outs
    bx, by, bz = coord_ref[3], coord_ref[4], coord_ref[5]

    odd_x, odd_z = bx == 1, bz == 1
    own0, own1, other = own_ref[0], own_ref[1], px_ref[...]
    rows_x = (
        jnp.where(odd_x, other, own0),
        jnp.where(odd_x, own0, own1),
        jnp.where(odd_x, own1, other),
    )
    planes = []
    for k in range(3):
        low, high, beyond = rows_x[k][0], rows_x[k][1], pz_ref[k]
        planes += [
            jnp.where(odd_z, beyond, low),
            jnp.where(odd_z, low, high),
            jnp.where(odd_z, high, beyond),
        ]
    coefs = jnp.concatenate(planes, axis=0) * energy_ref[...]
    scatter_returned(coefs, idx_ref, wts_ref, nonlocal_ref)

    rows = cells_ref[...].reshape(ROWS, DEPTH)
    along = iota((DEPTH, DEPTH), 1) - iota((DEPTH, DEPTH), 0)
    z_part = jnp.dot(
        rows, band((DEPTH, DEPTH), jnp.abs(along)),
        precision=lax.Precision.HIGHEST, preferred_element_type=F32,
    )
    chunks = ROWS // 128
    from_a = jnp.concatenate([za_in[k] for k in range(chunks)], axis=1)
    from_b = jnp.concatenate([zb_in[k] for k in range(chunks)], axis=1)
    faces = jnp.concatenate(
        [jnp.where(odd_z, from_a, from_b), jnp.where(odd_z, from_b, from_a)], axis=0
    )
    face_row, face_col = iota((16, DEPTH), 0), iota((16, DEPTH), 1)
    distance = jnp.where(face_row < 8, face_col + 8 - face_row, DEPTH + face_row - 8 - face_col)
    z_ref[...] = z_part + jnp.dot(
        faces.T, band((16, DEPTH), distance),
        precision=lax.Precision.HIGHEST, preferred_element_type=F32,
    )

    xext[:, HALO : HALO + SIDE] = cells_ref[...]
    xext[:, pl.ds((1 - bx) * (HALO + SIDE), HALO)] = xa_in[...]
    xext[:, pl.ds(bx * (HALO + SIDE), HALO)] = xb_in[...]
    yext[1] = cells_ref[...]
    yext[2 - 2 * by] = ya_in[...]
    yext[2 * by] = yb_in[...]

    pot = pot_ref[...] - (middle + 1.5 * stencil_terms[0])
    row = iota((SIDE, SIDE, DEPTH), 1)
    for o in range(NORB):
        here = xext[o, HALO : HALO + SIDE]
        left, right = yext[0, o], yext[2, o]
        laplace = z_ref[o * 64 : (o + 1) * 64, :].reshape(SIDE, SIDE, DEPTH)
        for k in range(1, HALO + 1):
            pair = xext[o, HALO + k : HALO + k + SIDE] + xext[o, HALO - k : HALO - k + SIDE]
            up = pltpu.roll(jnp.where(row < k, right, here), SIDE - k, 1)
            down = pltpu.roll(jnp.where(row >= SIDE - k, left, here), k, 1)
            laplace = laplace + stencil_terms[k] * (pair + (up + down))
        nonlocal_part = nonlocal_ref[o * 64 : (o + 1) * 64, :].reshape(SIDE, SIDE, DEPTH)
        result = gain * (pot * here - 0.5 * laplace + nonlocal_part)
        if back:
            result = result - back * before_ref[o]
        next_ref[o] = result
    if not last:
        table = sample_partials(next_ref[...].reshape(ROWS, DEPTH), idx_ref, wts_ref)
        write_parts(coord_ref, table, give_ref, keep_ref)
        write_sends(coord_ref, next_ref, xa_ref, xb_ref, za_ref, zb_ref)


def energy_kernel(sizes, coord_ref, energy_ref, table_ref):
    size_x, size_y, size_z = sizes
    atoms = energy_ref.shape[1]
    values = jnp.concatenate(
        [jnp.broadcast_to(energy_ref[j : j + 1, :], (NORB, atoms)) for j in range(NPROJ)], axis=0
    )
    upper = values.astype(BF16)
    rest = values - upper.astype(F32)
    middle = rest.astype(BF16)
    lower = (rest - middle.astype(F32)).astype(BF16)
    row = iota((SEGS + 8, 1), 0)
    plane, slot = row >> 3, row & 7
    off_x = jnp.where(plane >= 6, 1, jnp.where(plane >= 3, 0, -1))
    off_z = plane - 3 * (off_x + 1) - 1
    place_x = (coord_ref[0] + off_x) & (size_x - 1)
    place_z = (coord_ref[2] + off_z) & (size_z - 1)
    used = jnp.logical_and(slot < ATOM_DEV, row < SEGS)
    columns = []
    for position in range(POS_Y):
        atom = ((place_x * size_y + position) * size_z + place_z) * ATOM_DEV + slot
        atom = jnp.where(used, atom, -1)
        hot = jnp.where(iota((SEGS + 8, atoms), 1) == atom, 1.0, 0.0).astype(BF16)
        column = lax.dot_general(hot, lower, LAST, preferred_element_type=F32)
        column = column + lax.dot_general(hot, middle, LAST, preferred_element_type=F32)
        columns.append(column + lax.dot_general(hot, upper, LAST, preferred_element_type=F32))
    table_ref[...] = jnp.concatenate(columns, axis=1)[:SEGS]


def in_vmem(count):
    return [pl.BlockSpec(memory_space=pltpu.VMEM)] * count


def call(kernel, shapes, scratch, cost, *operands):
    flops, traffic = cost
    return pl.pallas_call(
        kernel,
        out_shape=[jax.ShapeDtypeStruct(s, k) for s, k in shapes],
        in_specs=[pl.BlockSpec(memory_space=pltpu.SMEM)] + in_vmem(len(operands) - 1),
        out_specs=in_vmem(len(shapes)),
        scratch_shapes=scratch,
        compiler_params=pltpu.CompilerParams(vmem_limit_bytes=VMEM_LIMIT),
        cost_estimate=pl.CostEstimate(flops=flops, bytes_accessed=traffic, transcendentals=0),
    )(*operands)


def add_kernel(left_ref, right_ref, sum_ref):
    sum_ref[...] = left_ref[...] + right_ref[...]


def total(left, right):
    return pl.pallas_call(
        add_kernel,
        out_shape=jax.ShapeDtypeStruct(left.shape, F32),
        in_specs=in_vmem(2),
        out_specs=in_vmem(1)[0],
        compiler_params=pltpu.CompilerParams(vmem_limit_bytes=VMEM_LIMIT),
        cost_estimate=pl.CostEstimate(flops=4000000000, bytes_accessed=40000000, transcendentals=0),
    )(left, right)


def swap_inside(value, axis):
    count = lax.axis_size(axis)
    return lax.ppermute(value, axis, [(i, i ^ 1) for i in range(count)])


def swap_across(value, axis):
    count = lax.axis_size(axis)
    pairs = [(i, (i + 1 if i % 2 else i - 1) % count) for i in range(count)]
    return lax.ppermute(value, axis, pairs)


def body(
    orbitals, potential, proj_values, point_cell, point_owner, point_slot, point_count, atom_energy
):
    sizes = tuple(lax.axis_size(axis) for axis in ("gx", "gy", "gz"))
    places = [lax.axis_index(axis) for axis in ("gx", "gy", "gz")]
    points = proj_values.shape[1]
    coord = jnp.stack(
        [p.astype(jnp.int32) for p in places]
        + [(p % 2).astype(jnp.int32) for p in places]
        + [point_count[0], jnp.int32(0)]
    )
    odd_x, odd_z = places[0] % 2 == 1, places[2] % 2 == 1
    some = point_count[0] > 0

    cells_shape = orbitals.shape
    x_shape = (NORB, HALO, SIDE, DEPTH)
    z_shape = (ROWS // 128, 8, 128)
    send_shapes = [
        ((SEGS // 3, 128), F32), ((2 * SEGS // 3, 128), F32), (x_shape, F32), (x_shape, F32), (z_shape, F32), (z_shape, F32)
    ]

    *sends, idx, wts = call(
        lambda *refs: first_kernel(sizes, *refs),
        send_shapes + [((8, points), jnp.int32), ((POS_Y * NPROJ, points), F32)],
        [], (600_000_000, 2_000_000),
        coord, orbitals, proj_values,
        point_cell.reshape(1, points), point_owner.reshape(1, points), point_slot.reshape(1, points),
    )
    (energy,) = call(
        lambda *refs: energy_kernel(sizes, *refs), [((SEGS, 128), F32)], [],
        (600_000_000, 200_000), coord, atom_energy,
    )

    def exchange(cells, give, keep, xa, xb, za, zb, energy):
        come = swap_inside(give, "gx").reshape(1, 3, 8, 128)
        place = jnp.arange(2, dtype=jnp.int32)[:, None, None, None]
        pair = keep.reshape(2, 3, 8, 128)
        pair = pair + jnp.where(place == 1 - places[0] % 2, come, 0.0)
        across = swap_across(pair, "gx")
        pair, xb = lax.optimization_barrier((pair, xb))
        xb = swap_across(xb, "gx")
        pair = total(pair, across)
        pair, energy = lax.optimization_barrier((pair, energy))

        def along_yz(pair, cells, xa, za, zb):
            pair = pair + swap_inside(pair, "gy")
            pair = pair + swap_across(pair, "gy")
            come = swap_inside(
                jnp.concatenate([jnp.where(odd_z, pair[:, 0], pair[:, 2]), za], axis=0), "gz"
            )
            za = come[2:]
            middle = pair[:, 1] + come[:2]
            own = jnp.where(
                odd_z,
                jnp.stack([middle, pair[:, 2]], axis=1),
                jnp.stack([pair[:, 0], middle], axis=1),
            )
            own, cells, xa = lax.optimization_barrier((own, cells, xa))
            come = swap_across(jnp.concatenate([own.reshape(4, 8, 128), zb], axis=0), "gz")
            ya, yb = swap_inside(cells, "gy"), swap_across(cells, "gy")
            xa = swap_inside(xa, "gx")
            return own + come[:4].reshape(2, 2, 8, 128), xa, ya, yb, za, come[4:]

        def untouched(pair, cells, xa, za, zb):
            return pair[:, :2], xa, cells, cells, za, zb

        own, xa, ya, yb, za, zb = lax.cond(
            some, along_yz, untouched, pair, cells, xa, za, zb
        )
        own, xb = lax.optimization_barrier((own, xb))

        beyond_x = swap_inside(jnp.where(odd_x, own[0], own[1]), "gx")
        rows = jnp.where(
            odd_z,
            jnp.where(odd_x, jnp.stack([beyond_x[0], own[0, 0], own[1, 0]]),
                      jnp.stack([own[0, 0], own[1, 0], beyond_x[0]])),
            jnp.where(odd_x, jnp.stack([beyond_x[1], own[0, 1], own[1, 1]]),
                      jnp.stack([own[0, 1], own[1, 1], beyond_x[1]])),
        )
        beyond_z = swap_inside(rows, "gz")
        return energy, own, beyond_x, beyond_z, xa, xb, ya, yb, za, zb

    half_width = (highest - cutoff) / 2.0
    middle = (highest + cutoff) / 2.0
    sigma_first = half_width / (lowest - middle)
    sigma_now = sigma_first
    previous, current = None, orbitals
    scratch = [
        pltpu.VMEM((ROWS, DEPTH), F32),
        pltpu.VMEM((ROWS, DEPTH), F32),
        pltpu.VMEM((NORB, SIDE + 2 * HALO, SIDE, DEPTH), F32),
        pltpu.VMEM((3, NORB, SIDE, SIDE, DEPTH), F32),
    ]
    for degree_index in range(DEGREE):
        if degree_index == 0:
            scales = (sigma_first / half_width, middle, 0.0)
        else:
            sigma_next = 1.0 / (2.0 / sigma_first - sigma_now)
            scales = (2.0 * sigma_next / half_width, middle, sigma_now * sigma_next)
            sigma_now = sigma_next
        last = degree_index == DEGREE - 1
        came = exchange(current, *sends, energy)
        before = [] if previous is None else [previous]
        results = call(
            lambda *refs, scales=scales, last=last: step_kernel(scales, last, *refs),
            [(cells_shape, F32)] + ([] if last else send_shapes),
            scratch, (1_500_000_000, 4_000_000),
            coord, current, *before, potential, idx, wts, *came,
        )
        previous, current = current, results[0]
        if not last:
            sends = results[1:]
    return current


def solution(mesh):
    return jax.shard_map(
        body,
        mesh=mesh,
        in_specs=(
            P(None, "gx", "gy", "gz"),
            P("gx", "gy", "gz"),
            P(None, ("gx", "gy", "gz")),
            P(("gx", "gy", "gz")),
            P(("gx", "gy", "gz")),
            P(("gx", "gy", "gz")),
            P(("gx", "gy", "gz")),
            P(),
        ),
        out_specs=P(None, "gx", "gy", "gz"),
        check_vma=False,
    )
```

```python
import jax
import jax.numpy as jnp
from jax import lax
from jax.experimental import pallas as pl
from jax.experimental.pallas import tpu as pltpu
from jax.sharding import PartitionSpec as P

DEGREE = 3
ATOM_DEV = 5
NORB = 8
NPROJ = 4
SIDE = 8
DEPTH = 128
HALO = 6
ROWS = NORB * SIDE * SIDE
PLANES = 9
SEGS = PLANES * 8
CHUNK = 256
POS_Y = 4
VMEM_LIMIT = 20 * 1024 * 1024

stencil_terms = (
    -5369.0 / 1800.0,
    12.0 / 7.0,
    -15.0 / 56.0,
    10.0 / 189.0,
    -1.0 / 112.0,
    2.0 / 1925.0,
    -1.0 / 16632.0,
)
lowest = -3.5
cutoff = 1.5
highest = 13.0

F32 = jnp.float32
BF16 = jnp.bfloat16
LAST = (((1,), (1,)), ((), ()))
FIRST = (((0,), (0,)), ((), ()))


def iota(shape, dim):
    return lax.broadcasted_iota(jnp.int32, shape, dim)


def one_hot(index_row, rows, kind):
    hit = iota((rows, index_row.shape[1]), 0) == index_row
    return jnp.where(hit, 1.0, 0.0).astype(kind)


def split_two(value):
    upper = value.astype(BF16)
    return upper, (value - upper.astype(F32)).astype(BF16)


def sample_partials(cells, idx_ref, wts_ref):
    upper, lower = split_two(cells)
    both = jnp.concatenate([upper, lower], axis=1)
    points = idx_ref.shape[1]
    total = jnp.zeros((SEGS + 8, 128), F32)
    for first in range(0, points, CHUNK):
        span = slice(first, first + CHUNK)
        hot_z = one_hot(idx_ref[0:1, span], DEPTH, BF16)
        picked = jnp.dot(both, jnp.concatenate([hot_z, hot_z], axis=0), preferred_element_type=F32)
        mask = iota((SIDE * SIDE, CHUNK), 0) == idx_ref[1:2, span]
        picked = picked.reshape(NORB, SIDE * SIDE, CHUNK)
        sampled = jnp.sum(jnp.where(mask[None], picked, 0.0), axis=1)
        weights = wts_ref[:, span]
        parts = [weights[k : k + 1] * sampled for k in range(POS_Y * NPROJ)]
        upper_c, lower_c = split_two(jnp.concatenate(parts, axis=0))
        hot_seg = one_hot(idx_ref[2:3, span], SEGS + 8, BF16)
        total = total + lax.dot_general(hot_seg, upper_c, LAST, preferred_element_type=F32)
        total = total + lax.dot_general(hot_seg, lower_c, LAST, preferred_element_type=F32)
    return total[:SEGS]


def scatter_returned(coefs, idx_ref, wts_ref, nonlocal_ref):
    wide = jnp.concatenate([coefs, jnp.zeros((128 - SEGS, 128), F32)], axis=0)
    upper, lower = split_two(wide.T)
    both = jnp.concatenate([upper, lower], axis=1)
    points = idx_ref.shape[1]
    for first in range(0, points, CHUNK):
        span = slice(first, first + CHUNK)
        hot_seg = one_hot(idx_ref[2:3, span], 128, BF16)
        spread = jnp.dot(both, jnp.concatenate([hot_seg, hot_seg], axis=0), preferred_element_type=F32)
        weights = wts_ref[:, span]
        returned = weights[0:1] * spread[0:NORB]
        for k in range(1, POS_Y * NPROJ):
            returned = returned + weights[k : k + 1] * spread[k * NORB : (k + 1) * NORB]
        upper_r = returned.astype(BF16).astype(F32)
        lower_r = returned - upper_r
        mask = iota((SIDE * SIDE, CHUNK), 0) == idx_ref[1:2, span]
        tall = [
            jnp.where(mask, value[o : o + 1], 0.0).astype(BF16)
            for value in (upper_r, lower_r)
            for o in range(NORB)
        ]
        hot_z = one_hot(idx_ref[0:1, span], DEPTH, BF16)
        placed = lax.dot_general(
            jnp.concatenate(tall, axis=0), hot_z, LAST, preferred_element_type=F32
        )
        placed = placed[:ROWS] + placed[ROWS:]
        if first == 0:
            nonlocal_ref[...] = placed
        else:
            nonlocal_ref[...] += placed


def write_parts(coord_ref, table, send_ref, keep_ref):
    rows = SEGS // 3
    odd_x = coord_ref[3] == 1
    below, same, above = table[:rows], table[rows : 2 * rows], table[2 * rows :]
    send_ref[...] = jnp.where(odd_x, below, above)
    kept = [jnp.where(odd_x, same, below), jnp.where(odd_x, above, same)]
    keep_ref[...] = jnp.concatenate(kept, axis=0)


def write_sends(coord_ref, cells_ref, xa_ref, xb_ref, za_ref, zb_ref):
    bx, bz = coord_ref[3], coord_ref[5]
    xa_ref[...] = cells_ref[:, pl.ds(2 - 2 * bx, HALO)]
    xb_ref[...] = cells_ref[:, pl.ds(2 * bx, HALO)]
    turned = cells_ref[...].reshape(ROWS, DEPTH).T
    near, far = turned[0:8], turned[DEPTH - 8 : DEPTH]
    to_a = jnp.where(bz == 1, near, far)
    to_b = jnp.where(bz == 1, far, near)
    for k in range(ROWS // 128):
        za_ref[k] = to_a[:, k * 128 : (k + 1) * 128]
        zb_ref[k] = to_b[:, k * 128 : (k + 1) * 128]


def offset_of(place, own, count):
    remain = (place - own) & (count - 1)
    return jnp.where(remain == 0, 1, jnp.where(remain == 1, 2, 0))


def first_kernel(
    sizes, coord_ref, cells_ref, proj_ref, cell_ref, owner_ref, slot_ref,
    give_ref, keep_ref, xa_ref, xb_ref, za_ref, zb_ref, idx_ref, wts_ref,
):
    size_x, size_y, size_z = sizes
    points = proj_ref.shape[1]
    shift_z = size_z.bit_length() - 1
    shift_x = shift_z + size_y.bit_length() - 1
    cell, owner = cell_ref[...], owner_ref[...]
    off_x = offset_of(owner >> shift_x, coord_ref[0], size_x)
    place_y = (owner >> shift_z) & (size_y - 1)
    off_z = offset_of(owner & (size_z - 1), coord_ref[2], size_z)
    idx_ref[0:1, :] = cell & (DEPTH - 1)
    idx_ref[1:2, :] = cell >> 7
    idx_ref[2:3, :] = (off_x * 3 + off_z) * 8 + slot_ref[...]
    idx_ref[3:8, :] = jnp.zeros((5, points), jnp.int32)
    live = iota((1, points), 1) < coord_ref[6]
    for position in range(POS_Y):
        here = jnp.logical_and(live, place_y == position)
        wts_ref[position * NPROJ : (position + 1) * NPROJ, :] = jnp.where(here, proj_ref[...], 0.0)
    table = sample_partials(cells_ref[...].reshape(ROWS, DEPTH), idx_ref, wts_ref)
    write_parts(coord_ref, table, give_ref, keep_ref)
    write_sends(coord_ref, cells_ref, xa_ref, xb_ref, za_ref, zb_ref)


def band(shape, distance):
    result = jnp.zeros(shape, F32)
    for k in range(1, HALO + 1):
        result = jnp.where(distance == k, stencil_terms[k], result)
    return result


def step_kernel(
    scales, last, coord_ref, cells_ref, *refs
):
    gain, middle, back = scales
    refs = list(refs)
    before_ref = refs.pop(0) if back else None
    (pot_ref, idx_ref, wts_ref, energy_ref, own_ref, px_ref, pz_ref,
     xa_in, xb_in, ya_in, yb_in, za_in, zb_in) = refs[:13]
    outs = refs[13:]
    if last:
        next_ref, nonlocal_ref, z_ref, xext, yext = outs
    else:
        (next_ref, give_ref, keep_ref, xa_ref, xb_ref, za_ref, zb_ref,
         nonlocal_ref, z_ref, xext, yext) = outs
    bx, by, bz = coord_ref[3], coord_ref[4], coord_ref[5]

    odd_x, odd_z = bx == 1, bz == 1
    own0, own1, other = own_ref[0], own_ref[1], px_ref[...]
    rows_x = (
        jnp.where(odd_x, other, own0),
        jnp.where(odd_x, own0, own1),
        jnp.where(odd_x, own1, other),
    )
    planes = []
    for k in range(3):
        low, high, beyond = rows_x[k][0], rows_x[k][1], pz_ref[k]
        planes += [
            jnp.where(odd_z, beyond, low),
            jnp.where(odd_z, low, high),
            jnp.where(odd_z, high, beyond),
        ]
    coefs = jnp.concatenate(planes, axis=0) * energy_ref[...]
    scatter_returned(coefs, idx_ref, wts_ref, nonlocal_ref)

    rows = cells_ref[...].reshape(ROWS, DEPTH)
    along = iota((DEPTH, DEPTH), 1) - iota((DEPTH, DEPTH), 0)
    z_part = jnp.dot(
        rows, band((DEPTH, DEPTH), jnp.abs(along)),
        precision=lax.Precision.HIGHEST, preferred_element_type=F32,
    )
    chunks = ROWS // 128
    from_a = jnp.concatenate([za_in[k] for k in range(chunks)], axis=1)
    from_b = jnp.concatenate([zb_in[k] for k in range(chunks)], axis=1)
    faces = jnp.concatenate(
        [jnp.where(odd_z, from_a, from_b), jnp.where(odd_z, from_b, from_a)], axis=0
    )
    face_row, face_col = iota((16, DEPTH), 0), iota((16, DEPTH), 1)
    distance = jnp.where(face_row < 8, face_col + 8 - face_row, DEPTH + face_row - 8 - face_col)
    z_ref[...] = z_part + jnp.dot(
        faces.T, band((16, DEPTH), distance),
        precision=lax.Precision.HIGHEST, preferred_element_type=F32,
    )

    xext[:, HALO : HALO + SIDE] = cells_ref[...]
    xext[:, pl.ds((1 - bx) * (HALO + SIDE), HALO)] = xa_in[...]
    xext[:, pl.ds(bx * (HALO + SIDE), HALO)] = xb_in[...]
    yext[1] = cells_ref[...]
    yext[2 - 2 * by] = ya_in[...]
    yext[2 * by] = yb_in[...]

    pot = pot_ref[...] - (middle + 1.5 * stencil_terms[0])
    row = iota((SIDE, SIDE, DEPTH), 1)
    for o in range(NORB):
        here = xext[o, HALO : HALO + SIDE]
        left, right = yext[0, o], yext[2, o]
        laplace = z_ref[o * 64 : (o + 1) * 64, :].reshape(SIDE, SIDE, DEPTH)
        for k in range(1, HALO + 1):
            pair = xext[o, HALO + k : HALO + k + SIDE] + xext[o, HALO - k : HALO - k + SIDE]
            up = pltpu.roll(jnp.where(row < k, right, here), SIDE - k, 1)
            down = pltpu.roll(jnp.where(row >= SIDE - k, left, here), k, 1)
            laplace = laplace + stencil_terms[k] * (pair + (up + down))
        nonlocal_part = nonlocal_ref[o * 64 : (o + 1) * 64, :].reshape(SIDE, SIDE, DEPTH)
        result = gain * (pot * here - 0.5 * laplace + nonlocal_part)
        if back:
            result = result - back * before_ref[o]
        next_ref[o] = result
    if not last:
        table = sample_partials(next_ref[...].reshape(ROWS, DEPTH), idx_ref, wts_ref)
        write_parts(coord_ref, table, give_ref, keep_ref)
        write_sends(coord_ref, next_ref, xa_ref, xb_ref, za_ref, zb_ref)


def energy_kernel(sizes, coord_ref, energy_ref, table_ref):
    size_x, size_y, size_z = sizes
    atoms = energy_ref.shape[1]
    values = jnp.concatenate(
        [jnp.broadcast_to(energy_ref[j : j + 1, :], (NORB, atoms)) for j in range(NPROJ)], axis=0
    )
    upper = values.astype(BF16)
    rest = values - upper.astype(F32)
    middle = rest.astype(BF16)
    lower = (rest - middle.astype(F32)).astype(BF16)
    row = iota((SEGS + 8, 1), 0)
    plane, slot = row >> 3, row & 7
    off_x = jnp.where(plane >= 6, 1, jnp.where(plane >= 3, 0, -1))
    off_z = plane - 3 * (off_x + 1) - 1
    place_x = (coord_ref[0] + off_x) & (size_x - 1)
    place_z = (coord_ref[2] + off_z) & (size_z - 1)
    used = jnp.logical_and(slot < ATOM_DEV, row < SEGS)
    columns = []
    for position in range(POS_Y):
        atom = ((place_x * size_y + position) * size_z + place_z) * ATOM_DEV + slot
        atom = jnp.where(used, atom, -1)
        hot = jnp.where(iota((SEGS + 8, atoms), 1) == atom, 1.0, 0.0).astype(BF16)
        column = lax.dot_general(hot, lower, LAST, preferred_element_type=F32)
        column = column + lax.dot_general(hot, middle, LAST, preferred_element_type=F32)
        columns.append(column + lax.dot_general(hot, upper, LAST, preferred_element_type=F32))
    table_ref[...] = jnp.concatenate(columns, axis=1)[:SEGS]


def in_vmem(count):
    return [pl.BlockSpec(memory_space=pltpu.VMEM)] * count


def call(kernel, shapes, scratch, cost, *operands):
    flops, traffic = cost
    return pl.pallas_call(
        kernel,
        out_shape=[jax.ShapeDtypeStruct(s, k) for s, k in shapes],
        in_specs=[pl.BlockSpec(memory_space=pltpu.SMEM)] + in_vmem(len(operands) - 1),
        out_specs=in_vmem(len(shapes)),
        scratch_shapes=scratch,
        compiler_params=pltpu.CompilerParams(vmem_limit_bytes=VMEM_LIMIT),
        cost_estimate=pl.CostEstimate(flops=flops, bytes_accessed=traffic, transcendentals=0),
    )(*operands)


def add_kernel(left_ref, right_ref, sum_ref):
    sum_ref[...] = left_ref[...] + right_ref[...]


def total(left, right):
    return pl.pallas_call(
        add_kernel,
        out_shape=jax.ShapeDtypeStruct(left.shape, F32),
        in_specs=in_vmem(2),
        out_specs=in_vmem(1)[0],
        compiler_params=pltpu.CompilerParams(vmem_limit_bytes=VMEM_LIMIT),
        cost_estimate=pl.CostEstimate(flops=8000000000, bytes_accessed=80000000, transcendentals=0),
    )(left, right)


def swap_inside(value, axis):
    count = lax.axis_size(axis)
    return lax.ppermute(value, axis, [(i, i ^ 1) for i in range(count)])


def swap_across(value, axis):
    count = lax.axis_size(axis)
    pairs = [(i, (i + 1 if i % 2 else i - 1) % count) for i in range(count)]
    return lax.ppermute(value, axis, pairs)


def body(
    orbitals, potential, proj_values, point_cell, point_owner, point_slot, point_count, atom_energy
):
    sizes = tuple(lax.axis_size(axis) for axis in ("gx", "gy", "gz"))
    places = [lax.axis_index(axis) for axis in ("gx", "gy", "gz")]
    points = proj_values.shape[1]
    coord = jnp.stack(
        [p.astype(jnp.int32) for p in places]
        + [(p % 2).astype(jnp.int32) for p in places]
        + [point_count[0], jnp.int32(0)]
    )
    odd_x, odd_z = places[0] % 2 == 1, places[2] % 2 == 1
    some = point_count[0] > 0

    cells_shape = orbitals.shape
    x_shape = (NORB, HALO, SIDE, DEPTH)
    z_shape = (ROWS // 128, 8, 128)
    send_shapes = [
        ((SEGS // 3, 128), F32), ((2 * SEGS // 3, 128), F32), (x_shape, F32), (x_shape, F32), (z_shape, F32), (z_shape, F32)
    ]

    *sends, idx, wts = call(
        lambda *refs: first_kernel(sizes, *refs),
        send_shapes + [((8, points), jnp.int32), ((POS_Y * NPROJ, points), F32)],
        [], (600_000_000, 2_000_000),
        coord, orbitals, proj_values,
        point_cell.reshape(1, points), point_owner.reshape(1, points), point_slot.reshape(1, points),
    )
    def staged(trade, share, halo_trade, halo, finish, rest, otherwise, beside=tuple):
        come, extra = lax.optimization_barrier((trade(share), beside()))
        share, halo = lax.optimization_barrier((share, halo))
        arriving = halo_trade(halo)
        after = lax.cond(some, rest, otherwise, finish(come))
        return lax.optimization_barrier(((*after, *extra), arriving))

    def zeros_like_z(pair):
        z_face = jnp.zeros(z_shape, F32)
        return pair[:, :2], z_face, z_face

    def zeros_like_y(pair):
        return (*zeros_like_z(pair), jnp.zeros(cells_shape, F32))

    def zeros_like_x(pair):
        return (*zeros_like_y(pair), jnp.zeros(x_shape, F32))

    def zeros_like_all(pair):
        return (*zeros_like_x(pair), jnp.zeros(x_shape, F32))

    def zeros_like_first(pair):
        *head, face = zeros_like_all(pair)
        return (*head, jnp.zeros((SEGS, 128), F32), face)

    def energies():
        return call(
            lambda *refs: energy_kernel(sizes, *refs), [((SEGS, 128), F32)], [],
            (600_000_000, 200_000), coord, atom_energy,
        )

    def exchange(cells, give, keep, xa, xb, za, zb, energy):
        first = energy is None
        place = jnp.arange(2, dtype=jnp.int32)[:, None, None, None]

        def along_z(pair):
            come = swap_inside(
                jnp.concatenate([jnp.where(odd_z, pair[:, 0], pair[:, 2]), za], axis=0), "gz"
            )
            middle = pair[:, 1] + come[:2]
            own = jnp.where(
                odd_z,
                jnp.stack([middle, pair[:, 2]], axis=1),
                jnp.stack([pair[:, 0], middle], axis=1),
            )
            far = swap_across(jnp.concatenate([own.reshape(4, 8, 128), zb], axis=0), "gz")
            return own + far[:4].reshape(2, 2, 8, 128), come[2:], far[4:]

        def along_y_across(pair):
            (own, za_in, zb_in), yb_in = staged(
                lambda v: swap_across(v, "gy"), pair, lambda v: swap_across(v, "gy"), cells,
                lambda come: total(pair, come), along_z, zeros_like_z,
            )
            return own, za_in, zb_in, yb_in

        def along_y_inside(pair):
            rest, xa_in = staged(
                lambda v: swap_inside(v, "gy"), pair, lambda v: swap_inside(v, "gx"), xa,
                lambda come: total(pair, come), along_y_across, zeros_like_y,
            )
            return (*rest, xa_in)

        def along_x_across(pair):
            rest, xb_in = staged(
                lambda v: swap_across(v, "gx"), pair, lambda v: swap_across(v, "gx"), xb,
                lambda come: total(pair, come), along_y_inside, zeros_like_x,
                energies if first else tuple,
            )
            return (*rest, xb_in)

        rest, ya_in = staged(
            lambda v: swap_inside(v, "gx"), give, lambda v: swap_inside(v, "gy"), cells,
            lambda come: total(
                keep.reshape(2, 3, 8, 128),
                jnp.where(place == 1 - places[0] % 2, come.reshape(1, 3, 8, 128), 0.0),
            ),
            along_x_across, zeros_like_first if first else zeros_like_all,
        )
        own, za, zb, yb, xa, *made, xb = rest
        energy = made[0] if first else energy
        ya = ya_in

        beyond_x = swap_inside(jnp.where(odd_x, own[0], own[1]), "gx")
        rows = jnp.where(
            odd_z,
            jnp.where(odd_x, jnp.stack([beyond_x[0], own[0, 0], own[1, 0]]),
                      jnp.stack([own[0, 0], own[1, 0], beyond_x[0]])),
            jnp.where(odd_x, jnp.stack([beyond_x[1], own[0, 1], own[1, 1]]),
                      jnp.stack([own[0, 1], own[1, 1], beyond_x[1]])),
        )
        beyond_z = swap_inside(rows, "gz")
        return energy, own, beyond_x, beyond_z, xa, xb, ya, yb, za, zb

    half_width = (highest - cutoff) / 2.0
    middle = (highest + cutoff) / 2.0
    sigma_first = half_width / (lowest - middle)
    sigma_now = sigma_first
    previous, current, energy = None, orbitals, None
    scratch = [
        pltpu.VMEM((ROWS, DEPTH), F32),
        pltpu.VMEM((ROWS, DEPTH), F32),
        pltpu.VMEM((NORB, SIDE + 2 * HALO, SIDE, DEPTH), F32),
        pltpu.VMEM((3, NORB, SIDE, SIDE, DEPTH), F32),
    ]
    for degree_index in range(DEGREE):
        if degree_index == 0:
            scales = (sigma_first / half_width, middle, 0.0)
        else:
            sigma_next = 1.0 / (2.0 / sigma_first - sigma_now)
            scales = (2.0 * sigma_next / half_width, middle, sigma_now * sigma_next)
            sigma_now = sigma_next
        last = degree_index == DEGREE - 1
        came = exchange(current, *sends, energy)
        energy = came[0]
        before = [] if previous is None else [previous]
        results = call(
            lambda *refs, scales=scales, last=last: step_kernel(scales, last, *refs),
            [(cells_shape, F32)] + ([] if last else send_shapes),
            scratch, (1_500_000_000, 4_000_000),
            coord, current, *before, potential, idx, wts, *came,
        )
        previous, current = current, results[0]
        if not last:
            sends = results[1:]
    return current


def solution(mesh):
    return jax.shard_map(
        body,
        mesh=mesh,
        in_specs=(
            P(None, "gx", "gy", "gz"),
            P("gx", "gy", "gz"),
            P(None, ("gx", "gy", "gz")),
            P(("gx", "gy", "gz")),
            P(("gx", "gy", "gz")),
            P(("gx", "gy", "gz")),
            P(("gx", "gy", "gz")),
            P(),
        ),
        out_specs=P(None, "gx", "gy", "gz"),
        check_vma=False,
    )
```

```python
import jax
import jax.numpy as jnp
from jax import lax
from jax.experimental import pallas as pl
from jax.experimental.pallas import tpu as pltpu
from jax.sharding import PartitionSpec as P

DEGREE = 3
ATOM_DEV = 5
NORB = 8
NPROJ = 4
SIDE = 8
DEPTH = 128
HALO = 6
ROWS = NORB * SIDE * SIDE
PLANES = 9
SEGS = PLANES * 8
CHUNK = 256
POS_Y = 4
VMEM_LIMIT = 20 * 1024 * 1024

stencil_terms = (
    -5369.0 / 1800.0,
    12.0 / 7.0,
    -15.0 / 56.0,
    10.0 / 189.0,
    -1.0 / 112.0,
    2.0 / 1925.0,
    -1.0 / 16632.0,
)
lowest = -3.5
cutoff = 1.5
highest = 13.0

F32 = jnp.float32
BF16 = jnp.bfloat16
LAST = (((1,), (1,)), ((), ()))
FIRST = (((0,), (0,)), ((), ()))


def iota(shape, dim):
    return lax.broadcasted_iota(jnp.int32, shape, dim)


def one_hot(index_row, rows, kind):
    hit = iota((rows, index_row.shape[1]), 0) == index_row
    return jnp.where(hit, 1.0, 0.0).astype(kind)


def split_two(value):
    upper = value.astype(BF16)
    return upper, (value - upper.astype(F32)).astype(BF16)


def sample_partials(cells, idx_ref, wts_ref):
    upper, lower = split_two(cells)
    both = jnp.concatenate([upper, lower], axis=1)
    points = idx_ref.shape[1]
    total = jnp.zeros((SEGS + 8, 128), F32)
    for first in range(0, points, CHUNK):
        span = slice(first, first + CHUNK)
        hot_z = one_hot(idx_ref[0:1, span], DEPTH, BF16)
        picked = jnp.dot(both, jnp.concatenate([hot_z, hot_z], axis=0), preferred_element_type=F32)
        mask = iota((SIDE * SIDE, CHUNK), 0) == idx_ref[1:2, span]
        picked = picked.reshape(NORB, SIDE * SIDE, CHUNK)
        sampled = jnp.sum(jnp.where(mask[None], picked, 0.0), axis=1)
        weights = wts_ref[:, span]
        parts = [weights[k : k + 1] * sampled for k in range(POS_Y * NPROJ)]
        upper_c, lower_c = split_two(jnp.concatenate(parts, axis=0))
        hot_seg = one_hot(idx_ref[2:3, span], SEGS + 8, BF16)
        total = total + lax.dot_general(hot_seg, upper_c, LAST, preferred_element_type=F32)
        total = total + lax.dot_general(hot_seg, lower_c, LAST, preferred_element_type=F32)
    return total[:SEGS]


def scatter_returned(coefs, idx_ref, wts_ref, nonlocal_ref):
    wide = jnp.concatenate([coefs, jnp.zeros((128 - SEGS, 128), F32)], axis=0)
    upper, lower = split_two(wide.T)
    both = jnp.concatenate([upper, lower], axis=1)
    points = idx_ref.shape[1]
    for first in range(0, points, CHUNK):
        span = slice(first, first + CHUNK)
        hot_seg = one_hot(idx_ref[2:3, span], 128, BF16)
        spread = jnp.dot(both, jnp.concatenate([hot_seg, hot_seg], axis=0), preferred_element_type=F32)
        weights = wts_ref[:, span]
        returned = weights[0:1] * spread[0:NORB]
        for k in range(1, POS_Y * NPROJ):
            returned = returned + weights[k : k + 1] * spread[k * NORB : (k + 1) * NORB]
        upper_r = returned.astype(BF16).astype(F32)
        lower_r = returned - upper_r
        mask = iota((SIDE * SIDE, CHUNK), 0) == idx_ref[1:2, span]
        tall = [
            jnp.where(mask, value[o : o + 1], 0.0).astype(BF16)
            for value in (upper_r, lower_r)
            for o in range(NORB)
        ]
        hot_z = one_hot(idx_ref[0:1, span], DEPTH, BF16)
        placed = lax.dot_general(
            jnp.concatenate(tall, axis=0), hot_z, LAST, preferred_element_type=F32
        )
        placed = placed[:ROWS] + placed[ROWS:]
        if first == 0:
            nonlocal_ref[...] = placed
        else:
            nonlocal_ref[...] += placed


def write_parts(coord_ref, table, send_ref, keep_ref):
    rows = SEGS // 3
    odd_x = coord_ref[3] == 1
    below, same, above = table[:rows], table[rows : 2 * rows], table[2 * rows :]
    send_ref[...] = jnp.where(odd_x, below, above)
    kept = [jnp.where(odd_x, same, below), jnp.where(odd_x, above, same)]
    keep_ref[...] = jnp.concatenate(kept, axis=0)


def write_sends(coord_ref, cells_ref, xa_ref, xb_ref, za_ref, zb_ref):
    bx, bz = coord_ref[3], coord_ref[5]
    xa_ref[...] = cells_ref[:, pl.ds(2 - 2 * bx, HALO)]
    xb_ref[...] = cells_ref[:, pl.ds(2 * bx, HALO)]
    turned = cells_ref[...].reshape(ROWS, DEPTH).T
    near, far = turned[0:8], turned[DEPTH - 8 : DEPTH]
    to_a = jnp.where(bz == 1, near, far)
    to_b = jnp.where(bz == 1, far, near)
    for k in range(ROWS // 128):
        za_ref[k] = to_a[:, k * 128 : (k + 1) * 128]
        zb_ref[k] = to_b[:, k * 128 : (k + 1) * 128]


def offset_of(place, own, count):
    remain = (place - own) & (count - 1)
    return jnp.where(remain == 0, 1, jnp.where(remain == 1, 2, 0))


def first_kernel(
    sizes, coord_ref, cells_ref, proj_ref, cell_ref, owner_ref, slot_ref,
    give_ref, keep_ref, xa_ref, xb_ref, za_ref, zb_ref, idx_ref, wts_ref,
):
    size_x, size_y, size_z = sizes
    points = proj_ref.shape[1]
    shift_z = size_z.bit_length() - 1
    shift_x = shift_z + size_y.bit_length() - 1
    cell, owner = cell_ref[...], owner_ref[...]
    off_x = offset_of(owner >> shift_x, coord_ref[0], size_x)
    place_y = (owner >> shift_z) & (size_y - 1)
    off_z = offset_of(owner & (size_z - 1), coord_ref[2], size_z)
    idx_ref[0:1, :] = cell & (DEPTH - 1)
    idx_ref[1:2, :] = cell >> 7
    idx_ref[2:3, :] = (off_x * 3 + off_z) * 8 + slot_ref[...]
    idx_ref[3:8, :] = jnp.zeros((5, points), jnp.int32)
    live = iota((1, points), 1) < coord_ref[6]
    for position in range(POS_Y):
        here = jnp.logical_and(live, place_y == position)
        wts_ref[position * NPROJ : (position + 1) * NPROJ, :] = jnp.where(here, proj_ref[...], 0.0)
    table = sample_partials(cells_ref[...].reshape(ROWS, DEPTH), idx_ref, wts_ref)
    write_parts(coord_ref, table, give_ref, keep_ref)
    write_sends(coord_ref, cells_ref, xa_ref, xb_ref, za_ref, zb_ref)


def band(shape, distance):
    result = jnp.zeros(shape, F32)
    for k in range(1, HALO + 1):
        result = jnp.where(distance == k, stencil_terms[k], result)
    return result


def step_kernel(
    scales, last, coord_ref, cells_ref, *refs
):
    gain, middle, back = scales
    refs = list(refs)
    before_ref = refs.pop(0) if back else None
    (pot_ref, idx_ref, wts_ref, energy_ref, own_ref, px_ref, pz_ref,
     xa_in, xb_in, ya_in, yb_in, za_in, zb_in) = refs[:13]
    outs = refs[13:]
    if last:
        next_ref, nonlocal_ref, z_ref, xext, yext = outs
    else:
        (next_ref, give_ref, keep_ref, xa_ref, xb_ref, za_ref, zb_ref,
         nonlocal_ref, z_ref, xext, yext) = outs
    bx, by, bz = coord_ref[3], coord_ref[4], coord_ref[5]

    odd_x, odd_z = bx == 1, bz == 1
    own0, own1, other = own_ref[0], own_ref[1], px_ref[...]
    rows_x = (
        jnp.where(odd_x, other, own0),
        jnp.where(odd_x, own0, own1),
        jnp.where(odd_x, own1, other),
    )
    planes = []
    for k in range(3):
        low, high, beyond = rows_x[k][0], rows_x[k][1], pz_ref[k]
        planes += [
            jnp.where(odd_z, beyond, low),
            jnp.where(odd_z, low, high),
            jnp.where(odd_z, high, beyond),
        ]
    coefs = jnp.concatenate(planes, axis=0) * energy_ref[...]
    scatter_returned(coefs, idx_ref, wts_ref, nonlocal_ref)

    rows = cells_ref[...].reshape(ROWS, DEPTH)
    along = iota((DEPTH, DEPTH), 1) - iota((DEPTH, DEPTH), 0)
    z_part = jnp.dot(
        rows, band((DEPTH, DEPTH), jnp.abs(along)),
        precision=lax.Precision.HIGHEST, preferred_element_type=F32,
    )
    chunks = ROWS // 128
    from_a = jnp.concatenate([za_in[k] for k in range(chunks)], axis=1)
    from_b = jnp.concatenate([zb_in[k] for k in range(chunks)], axis=1)
    faces = jnp.concatenate(
        [jnp.where(odd_z, from_a, from_b), jnp.where(odd_z, from_b, from_a)], axis=0
    )
    face_row, face_col = iota((16, DEPTH), 0), iota((16, DEPTH), 1)
    distance = jnp.where(face_row < 8, face_col + 8 - face_row, DEPTH + face_row - 8 - face_col)
    z_ref[...] = z_part + jnp.dot(
        faces.T, band((16, DEPTH), distance),
        precision=lax.Precision.HIGHEST, preferred_element_type=F32,
    )

    xext[:, HALO : HALO + SIDE] = cells_ref[...]
    xext[:, pl.ds((1 - bx) * (HALO + SIDE), HALO)] = xa_in[...]
    xext[:, pl.ds(bx * (HALO + SIDE), HALO)] = xb_in[...]
    yext[1] = cells_ref[...]
    yext[2 - 2 * by] = ya_in[...]
    yext[2 * by] = yb_in[...]

    pot = pot_ref[...] - (middle + 1.5 * stencil_terms[0])
    row = iota((SIDE, SIDE, DEPTH), 1)
    for o in range(NORB):
        here = xext[o, HALO : HALO + SIDE]
        left, right = yext[0, o], yext[2, o]
        laplace = z_ref[o * 64 : (o + 1) * 64, :].reshape(SIDE, SIDE, DEPTH)
        for k in range(1, HALO + 1):
            pair = xext[o, HALO + k : HALO + k + SIDE] + xext[o, HALO - k : HALO - k + SIDE]
            up = pltpu.roll(jnp.where(row < k, right, here), SIDE - k, 1)
            down = pltpu.roll(jnp.where(row >= SIDE - k, left, here), k, 1)
            laplace = laplace + stencil_terms[k] * (pair + (up + down))
        nonlocal_part = nonlocal_ref[o * 64 : (o + 1) * 64, :].reshape(SIDE, SIDE, DEPTH)
        result = gain * (pot * here - 0.5 * laplace + nonlocal_part)
        if back:
            result = result - back * before_ref[o]
        next_ref[o] = result
    if not last:
        table = sample_partials(next_ref[...].reshape(ROWS, DEPTH), idx_ref, wts_ref)
        write_parts(coord_ref, table, give_ref, keep_ref)
        write_sends(coord_ref, next_ref, xa_ref, xb_ref, za_ref, zb_ref)


def energy_kernel(sizes, coord_ref, energy_ref, table_ref):
    size_x, size_y, size_z = sizes
    atoms = energy_ref.shape[1]
    values = jnp.concatenate(
        [jnp.broadcast_to(energy_ref[j : j + 1, :], (NORB, atoms)) for j in range(NPROJ)], axis=0
    )
    upper = values.astype(BF16)
    rest = values - upper.astype(F32)
    middle = rest.astype(BF16)
    lower = (rest - middle.astype(F32)).astype(BF16)
    row = iota((SEGS + 8, 1), 0)
    plane, slot = row >> 3, row & 7
    off_x = jnp.where(plane >= 6, 1, jnp.where(plane >= 3, 0, -1))
    off_z = plane - 3 * (off_x + 1) - 1
    place_x = (coord_ref[0] + off_x) & (size_x - 1)
    place_z = (coord_ref[2] + off_z) & (size_z - 1)
    used = jnp.logical_and(slot < ATOM_DEV, row < SEGS)
    columns = []
    for position in range(POS_Y):
        atom = ((place_x * size_y + position) * size_z + place_z) * ATOM_DEV + slot
        atom = jnp.where(used, atom, -1)
        hot = jnp.where(iota((SEGS + 8, atoms), 1) == atom, 1.0, 0.0).astype(BF16)
        column = lax.dot_general(hot, lower, LAST, preferred_element_type=F32)
        column = column + lax.dot_general(hot, middle, LAST, preferred_element_type=F32)
        columns.append(column + lax.dot_general(hot, upper, LAST, preferred_element_type=F32))
    table_ref[...] = jnp.concatenate(columns, axis=1)[:SEGS]


def in_vmem(count):
    return [pl.BlockSpec(memory_space=pltpu.VMEM)] * count


def call(kernel, shapes, scratch, cost, *operands):
    flops, traffic = cost
    return pl.pallas_call(
        kernel,
        out_shape=[jax.ShapeDtypeStruct(s, k) for s, k in shapes],
        in_specs=[pl.BlockSpec(memory_space=pltpu.SMEM)] + in_vmem(len(operands) - 1),
        out_specs=in_vmem(len(shapes)),
        scratch_shapes=scratch,
        compiler_params=pltpu.CompilerParams(vmem_limit_bytes=VMEM_LIMIT),
        cost_estimate=pl.CostEstimate(flops=flops, bytes_accessed=traffic, transcendentals=0),
    )(*operands)


def add_kernel(left_ref, right_ref, sum_ref):
    sum_ref[...] = left_ref[...] + right_ref[...]


def total(left, right):
    return pl.pallas_call(
        add_kernel,
        out_shape=jax.ShapeDtypeStruct(left.shape, F32),
        in_specs=in_vmem(2),
        out_specs=in_vmem(1)[0],
        compiler_params=pltpu.CompilerParams(vmem_limit_bytes=VMEM_LIMIT),
        cost_estimate=pl.CostEstimate(flops=8000000000, bytes_accessed=80000000, transcendentals=0),
    )(left, right)


def swap_inside(value, axis):
    count = lax.axis_size(axis)
    return lax.ppermute(value, axis, [(i, i ^ 1) for i in range(count)])


def across(place, count):
    return (place + 1 if place % 2 else place - 1) % count


def swap_across(value, axis):
    count = lax.axis_size(axis)
    return lax.ppermute(value, axis, [(i, across(i, count)) for i in range(count)])


def swap_corners(value):
    count_x, count_z = lax.axis_size("gx"), lax.axis_size("gz")
    pairs = []
    for x in range(count_x):
        for z in range(count_z):
            to_x, to_z = across(x, count_x), z
            turns = (x if x % 2 == 0 else to_x) % (count_x // 2) == 0
            if turns and z in (0, count_z - 1):
                to_z = across(z, count_z)
            pairs.append((x * count_z + z, to_x * count_z + to_z))
    return lax.ppermute(value, ("gx", "gz"), pairs)


def body(
    orbitals, potential, proj_values, point_cell, point_owner, point_slot, point_count, atom_energy
):
    sizes = tuple(lax.axis_size(axis) for axis in ("gx", "gy", "gz"))
    places = [lax.axis_index(axis) for axis in ("gx", "gy", "gz")]
    points = proj_values.shape[1]
    coord = jnp.stack(
        [p.astype(jnp.int32) for p in places]
        + [(p % 2).astype(jnp.int32) for p in places]
        + [point_count[0], jnp.int32(0)]
    )
    odd_x, odd_z = places[0] % 2 == 1, places[2] % 2 == 1
    some = point_count[0] > 0

    cells_shape = orbitals.shape
    x_shape = (NORB, HALO, SIDE, DEPTH)
    z_shape = (ROWS // 128, 8, 128)
    send_shapes = [
        ((SEGS // 3, 128), F32), ((2 * SEGS // 3, 128), F32), (x_shape, F32), (x_shape, F32), (z_shape, F32), (z_shape, F32)
    ]

    *sends, idx, wts = call(
        lambda *refs: first_kernel(sizes, *refs),
        send_shapes + [((8, points), jnp.int32), ((POS_Y * NPROJ, points), F32)],
        [], (600_000_000, 2_000_000),
        coord, orbitals, proj_values,
        point_cell.reshape(1, points), point_owner.reshape(1, points), point_slot.reshape(1, points),
    )
    def staged(trade, share, halo_trade, halo, finish, rest, otherwise, beside=tuple):
        come, extra = lax.optimization_barrier((trade(share), beside()))
        share, halo = lax.optimization_barrier((share, halo))
        arriving = halo_trade(halo)
        after = lax.cond(some, rest, otherwise, finish(come))
        return lax.optimization_barrier(((*after, *extra), arriving))

    def zeros_like_z(own):
        z_face = jnp.zeros(z_shape, F32)
        return own, jnp.zeros((2, 8, 128), F32), jnp.zeros((3, 8, 128), F32), z_face

    def zeros_like_y(own):
        return (*zeros_like_z(own), jnp.zeros(cells_shape, F32))

    def zeros_like_x(own):
        return (*zeros_like_y(own), jnp.zeros(x_shape, F32))

    def zeros_like_all(pair):
        return (*zeros_like_x(pair[:, :2]), jnp.zeros(z_shape, F32), jnp.zeros(x_shape, F32))

    def zeros_like_first(pair):
        return (*zeros_like_all(pair), jnp.zeros((SEGS, 128), F32))

    def energies():
        return call(
            lambda *refs: energy_kernel(sizes, *refs), [((SEGS, 128), F32)], [],
            (600_000_000, 200_000), coord, atom_energy,
        )

    def exchange(cells, give, keep, xa, xb, za, zb, energy):
        first = energy is None
        place = jnp.arange(2, dtype=jnp.int32)[:, None, None, None]

        def along_z_across(own):
            far = swap_across(jnp.concatenate([own.reshape(4, 8, 128), zb], axis=0), "gz")
            own = own + far[:4].reshape(2, 2, 8, 128)
            beyond_x = swap_inside(jnp.where(odd_x, own[0], own[1]), "gx")
            rows = jnp.where(
                odd_z,
                jnp.where(odd_x, jnp.stack([beyond_x[0], own[0, 0], own[1, 0]]),
                          jnp.stack([own[0, 0], own[1, 0], beyond_x[0]])),
                jnp.where(odd_x, jnp.stack([beyond_x[1], own[0, 1], own[1, 1]]),
                          jnp.stack([own[0, 1], own[1, 1], beyond_x[1]])),
            )
            return own, beyond_x, swap_inside(rows, "gz"), far[4:]

        def along_y_across(own):
            rest, yb_in = staged(
                lambda v: swap_across(v, "gy"), own, lambda v: swap_across(v, "gy"), cells,
                lambda come: total(own, come), along_z_across, zeros_like_z,
            )
            return (*rest, yb_in)

        def along_y_inside(own):
            rest, xa_in = staged(
                lambda v: swap_inside(v, "gy"), own, lambda v: swap_inside(v, "gx"), xa,
                lambda come: total(own, come), along_y_across, zeros_like_y,
            )
            return (*rest, xa_in)

        def along_z_inside(pair):
            come = swap_inside(
                jnp.concatenate([jnp.where(odd_z, pair[:, 0], pair[:, 2]), za], axis=0), "gz"
            )
            middle = pair[:, 1] + come[:2]
            own = jnp.where(
                odd_z,
                jnp.stack([middle, pair[:, 2]], axis=1),
                jnp.stack([pair[:, 0], middle], axis=1),
            )
            rest, xb_in = staged(
                swap_corners, own, lambda v: swap_across(v, "gx"), xb,
                lambda come: total(own, come), along_y_inside, zeros_like_x,
                energies if first else tuple,
            )
            made = rest[6:]
            return (*rest[:6], come[2:], xb_in, *made)

        rest, ya_in = staged(
            lambda v: swap_inside(v, "gx"), give, lambda v: swap_inside(v, "gy"), cells,
            lambda come: total(
                keep.reshape(2, 3, 8, 128),
                jnp.where(place == 1 - places[0] % 2, come.reshape(1, 3, 8, 128), 0.0),
            ),
            along_z_inside, zeros_like_first if first else zeros_like_all,
        )
        own, beyond_x, beyond_z, zb_in, yb_in, xa_in, za_in, xb_in, *made = rest
        energy = made[0] if first else energy
        return energy, own, beyond_x, beyond_z, xa_in, xb_in, ya_in, yb_in, za_in, zb_in

    half_width = (highest - cutoff) / 2.0
    middle = (highest + cutoff) / 2.0
    sigma_first = half_width / (lowest - middle)
    sigma_now = sigma_first
    previous, current, energy = None, orbitals, None
    scratch = [
        pltpu.VMEM((ROWS, DEPTH), F32),
        pltpu.VMEM((ROWS, DEPTH), F32),
        pltpu.VMEM((NORB, SIDE + 2 * HALO, SIDE, DEPTH), F32),
        pltpu.VMEM((3, NORB, SIDE, SIDE, DEPTH), F32),
    ]
    for degree_index in range(DEGREE):
        if degree_index == 0:
            scales = (sigma_first / half_width, middle, 0.0)
        else:
            sigma_next = 1.0 / (2.0 / sigma_first - sigma_now)
            scales = (2.0 * sigma_next / half_width, middle, sigma_now * sigma_next)
            sigma_now = sigma_next
        last = degree_index == DEGREE - 1
        came = exchange(current, *sends, energy)
        energy = came[0]
        before = [] if previous is None else [previous]
        results = call(
            lambda *refs, scales=scales, last=last: step_kernel(scales, last, *refs),
            [(cells_shape, F32)] + ([] if last else send_shapes),
            scratch, (1_500_000_000, 4_000_000),
            coord, current, *before, potential, idx, wts, *came,
        )
        previous, current = current, results[0]
        if not last:
            sends = results[1:]
    return current


def solution(mesh):
    return jax.shard_map(
        body,
        mesh=mesh,
        in_specs=(
            P(None, "gx", "gy", "gz"),
            P("gx", "gy", "gz"),
            P(None, ("gx", "gy", "gz")),
            P(("gx", "gy", "gz")),
            P(("gx", "gy", "gz")),
            P(("gx", "gy", "gz")),
            P(("gx", "gy", "gz")),
            P(),
        ),
        out_specs=P(None, "gx", "gy", "gz"),
        check_vma=False,
    )
```

```python
import jax
import jax.numpy as jnp
from jax import lax
from jax.experimental import pallas as pl
from jax.experimental.pallas import tpu as pltpu
from jax.sharding import PartitionSpec as P

DEGREE = 3
ATOM_DEV = 5
NORB = 8
NPROJ = 4
SIDE = 8
DEPTH = 128
HALO = 6
ROWS = NORB * SIDE * SIDE
PLANES = 9
SEGS = PLANES * 8
CHUNK = 256
POS_Y = 4
VMEM_LIMIT = 20 * 1024 * 1024

stencil_terms = (
    -5369.0 / 1800.0,
    12.0 / 7.0,
    -15.0 / 56.0,
    10.0 / 189.0,
    -1.0 / 112.0,
    2.0 / 1925.0,
    -1.0 / 16632.0,
)
lowest = -3.5
cutoff = 1.5
highest = 13.0

F32 = jnp.float32
BF16 = jnp.bfloat16
LAST = (((1,), (1,)), ((), ()))
FIRST = (((0,), (0,)), ((), ()))


def iota(shape, dim):
    return lax.broadcasted_iota(jnp.int32, shape, dim)


def one_hot(index_row, rows, kind):
    hit = iota((rows, index_row.shape[1]), 0) == index_row
    return jnp.where(hit, 1.0, 0.0).astype(kind)


def split_two(value):
    upper = value.astype(BF16)
    return upper, (value - upper.astype(F32)).astype(BF16)


def sample_partials(cells, idx_ref, wts_ref):
    upper, lower = split_two(cells)
    both = jnp.concatenate([upper, lower], axis=1)
    points = idx_ref.shape[1]
    total = jnp.zeros((SEGS + 8, 128), F32)
    for first in range(0, points, CHUNK):
        span = slice(first, first + CHUNK)
        hot_z = one_hot(idx_ref[0:1, span], DEPTH, BF16)
        picked = jnp.dot(both, jnp.concatenate([hot_z, hot_z], axis=0), preferred_element_type=F32)
        mask = iota((SIDE * SIDE, CHUNK), 0) == idx_ref[1:2, span]
        picked = picked.reshape(NORB, SIDE * SIDE, CHUNK)
        sampled = jnp.sum(jnp.where(mask[None], picked, 0.0), axis=1)
        weights = wts_ref[:, span]
        parts = [weights[k : k + 1] * sampled for k in range(POS_Y * NPROJ)]
        upper_c, lower_c = split_two(jnp.concatenate(parts, axis=0))
        hot_seg = one_hot(idx_ref[2:3, span], SEGS + 8, BF16)
        total = total + lax.dot_general(hot_seg, upper_c, LAST, preferred_element_type=F32)
        total = total + lax.dot_general(hot_seg, lower_c, LAST, preferred_element_type=F32)
    return total[:SEGS]


def scatter_returned(coefs, idx_ref, wts_ref, nonlocal_ref):
    wide = jnp.concatenate([coefs, jnp.zeros((128 - SEGS, 128), F32)], axis=0)
    upper, lower = split_two(wide.T)
    both = jnp.concatenate([upper, lower], axis=1)
    points = idx_ref.shape[1]
    for first in range(0, points, CHUNK):
        span = slice(first, first + CHUNK)
        hot_seg = one_hot(idx_ref[2:3, span], 128, BF16)
        spread = jnp.dot(both, jnp.concatenate([hot_seg, hot_seg], axis=0), preferred_element_type=F32)
        weights = wts_ref[:, span]
        returned = weights[0:1] * spread[0:NORB]
        for k in range(1, POS_Y * NPROJ):
            returned = returned + weights[k : k + 1] * spread[k * NORB : (k + 1) * NORB]
        upper_r = returned.astype(BF16).astype(F32)
        lower_r = returned - upper_r
        mask = iota((SIDE * SIDE, CHUNK), 0) == idx_ref[1:2, span]
        tall = [
            jnp.where(mask, value[o : o + 1], 0.0).astype(BF16)
            for value in (upper_r, lower_r)
            for o in range(NORB)
        ]
        hot_z = one_hot(idx_ref[0:1, span], DEPTH, BF16)
        placed = lax.dot_general(
            jnp.concatenate(tall, axis=0), hot_z, LAST, preferred_element_type=F32
        )
        placed = placed[:ROWS] + placed[ROWS:]
        if first == 0:
            nonlocal_ref[...] = placed
        else:
            nonlocal_ref[...] += placed


def write_parts(coord_ref, table, send_ref, keep_ref):
    rows = SEGS // 3
    odd_x = coord_ref[3] == 1
    below, same, above = table[:rows], table[rows : 2 * rows], table[2 * rows :]
    send_ref[...] = jnp.where(odd_x, below, above)
    kept = [jnp.where(odd_x, same, below), jnp.where(odd_x, above, same)]
    keep_ref[...] = jnp.concatenate(kept, axis=0)


def write_sends(coord_ref, cells_ref, xa_ref, xb_ref, za_ref, zb_ref):
    bx, bz = coord_ref[3], coord_ref[5]
    xa_ref[...] = cells_ref[:, pl.ds(2 - 2 * bx, HALO)]
    xb_ref[...] = cells_ref[:, pl.ds(2 * bx, HALO)]
    turned = cells_ref[...].reshape(ROWS, DEPTH).T
    near, far = turned[0:8], turned[DEPTH - 8 : DEPTH]
    to_a = jnp.where(bz == 1, near, far)
    to_b = jnp.where(bz == 1, far, near)
    for k in range(ROWS // 128):
        za_ref[k] = to_a[:, k * 128 : (k + 1) * 128]
        zb_ref[k] = to_b[:, k * 128 : (k + 1) * 128]


def offset_of(place, own, count):
    remain = (place - own) & (count - 1)
    return jnp.where(remain == 0, 1, jnp.where(remain == 1, 2, 0))


def first_kernel(
    sizes, coord_ref, cells_ref, proj_ref, cell_ref, owner_ref, slot_ref,
    give_ref, keep_ref, xa_ref, xb_ref, za_ref, zb_ref, idx_ref, wts_ref,
):
    size_x, size_y, size_z = sizes
    points = proj_ref.shape[1]
    shift_z = size_z.bit_length() - 1
    shift_x = shift_z + size_y.bit_length() - 1
    cell, owner = cell_ref[...], owner_ref[...]
    off_x = offset_of(owner >> shift_x, coord_ref[0], size_x)
    place_y = (owner >> shift_z) & (size_y - 1)
    off_z = offset_of(owner & (size_z - 1), coord_ref[2], size_z)
    idx_ref[0:1, :] = cell & (DEPTH - 1)
    idx_ref[1:2, :] = cell >> 7
    idx_ref[2:3, :] = (off_x * 3 + off_z) * 8 + slot_ref[...]
    idx_ref[3:8, :] = jnp.zeros((5, points), jnp.int32)
    live = iota((1, points), 1) < coord_ref[6]
    for position in range(POS_Y):
        here = jnp.logical_and(live, place_y == position)
        wts_ref[position * NPROJ : (position + 1) * NPROJ, :] = jnp.where(here, proj_ref[...], 0.0)
    table = sample_partials(cells_ref[...].reshape(ROWS, DEPTH), idx_ref, wts_ref)
    write_parts(coord_ref, table, give_ref, keep_ref)
    write_sends(coord_ref, cells_ref, xa_ref, xb_ref, za_ref, zb_ref)


def band(shape, distance):
    result = jnp.zeros(shape, F32)
    for k in range(1, HALO + 1):
        result = jnp.where(distance == k, stencil_terms[k], result)
    return result


def step_kernel(
    scales, last, coord_ref, cells_ref, *refs
):
    gain, middle, back = scales
    refs = list(refs)
    before_ref = refs.pop(0) if back else None
    (pot_ref, idx_ref, wts_ref, energy_ref, table_ref,
     xa_in, xb_in, corner_in, ya_in, yb_in, za_in, zb_in) = refs[:12]
    outs = refs[12:]
    if last:
        next_ref, nonlocal_ref, z_ref, xext, yext = outs
    else:
        (next_ref, give_ref, keep_ref, xa_ref, xb_ref, za_ref, zb_ref,
         nonlocal_ref, z_ref, xext, yext) = outs
    bx, by, bz = coord_ref[3], coord_ref[4], coord_ref[5]
    odd_z = bz == 1

    coefs = table_ref[...] * energy_ref[...]
    scatter_returned(coefs, idx_ref, wts_ref, nonlocal_ref)

    rows = cells_ref[...].reshape(ROWS, DEPTH)
    along = iota((DEPTH, DEPTH), 1) - iota((DEPTH, DEPTH), 0)
    z_part = jnp.dot(
        rows, band((DEPTH, DEPTH), jnp.abs(along)),
        precision=lax.Precision.HIGHEST, preferred_element_type=F32,
    )
    chunks = ROWS // 128
    from_a = jnp.concatenate([za_in[k] for k in range(chunks)], axis=1)
    from_b = jnp.concatenate([zb_in[k] for k in range(chunks)], axis=1)
    faces = jnp.concatenate(
        [jnp.where(odd_z, from_a, from_b), jnp.where(odd_z, from_b, from_a)], axis=0
    )
    face_row, face_col = iota((16, DEPTH), 0), iota((16, DEPTH), 1)
    distance = jnp.where(face_row < 8, face_col + 8 - face_row, DEPTH + face_row - 8 - face_col)
    z_ref[...] = z_part + jnp.dot(
        faces.T, band((16, DEPTH), distance),
        precision=lax.Precision.HIGHEST, preferred_element_type=F32,
    )

    xext[:, HALO : HALO + SIDE] = cells_ref[...]
    xext[:, pl.ds((1 - bx) * (HALO + SIDE), HALO)] = xa_in[...]
    xext[:, pl.ds(bx * (HALO + SIDE), HALO)] = xb_in[...] + corner_in[...]
    yext[1] = cells_ref[...]
    yext[2 - 2 * by] = ya_in[...]
    yext[2 * by] = yb_in[...]

    pot = pot_ref[...] - (middle + 1.5 * stencil_terms[0])
    row = iota((SIDE, SIDE, DEPTH), 1)
    for o in range(NORB):
        here = xext[o, HALO : HALO + SIDE]
        left, right = yext[0, o], yext[2, o]
        laplace = z_ref[o * 64 : (o + 1) * 64, :].reshape(SIDE, SIDE, DEPTH)
        for k in range(1, HALO + 1):
            pair = xext[o, HALO + k : HALO + k + SIDE] + xext[o, HALO - k : HALO - k + SIDE]
            up = pltpu.roll(jnp.where(row < k, right, here), SIDE - k, 1)
            down = pltpu.roll(jnp.where(row >= SIDE - k, left, here), k, 1)
            laplace = laplace + stencil_terms[k] * (pair + (up + down))
        nonlocal_part = nonlocal_ref[o * 64 : (o + 1) * 64, :].reshape(SIDE, SIDE, DEPTH)
        result = gain * (pot * here - 0.5 * laplace + nonlocal_part)
        if back:
            result = result - back * before_ref[o]
        next_ref[o] = result
    if not last:
        table = sample_partials(next_ref[...].reshape(ROWS, DEPTH), idx_ref, wts_ref)
        write_parts(coord_ref, table, give_ref, keep_ref)
        write_sends(coord_ref, next_ref, xa_ref, xb_ref, za_ref, zb_ref)


def table_kernel(coord_ref, own_ref, px_ref, pz_ref, far_ref, table_ref, face_ref):
    odd_x, odd_z = coord_ref[3] == 1, coord_ref[5] == 1
    own0, own1, other = own_ref[0], own_ref[1], px_ref[...]
    rows_x = (
        jnp.where(odd_x, other, own0),
        jnp.where(odd_x, own0, own1),
        jnp.where(odd_x, own1, other),
    )
    planes = []
    for k in range(3):
        low, high, beyond = rows_x[k][0], rows_x[k][1], pz_ref[k]
        planes += [
            jnp.where(odd_z, beyond, low),
            jnp.where(odd_z, low, high),
            jnp.where(odd_z, high, beyond),
        ]
    table_ref[...] = jnp.concatenate(planes, axis=0)
    face_ref[...] = far_ref[4:]


def energy_kernel(sizes, coord_ref, energy_ref, table_ref):
    size_x, size_y, size_z = sizes
    atoms = energy_ref.shape[1]
    values = jnp.concatenate(
        [jnp.broadcast_to(energy_ref[j : j + 1, :], (NORB, atoms)) for j in range(NPROJ)], axis=0
    )
    upper = values.astype(BF16)
    rest = values - upper.astype(F32)
    middle = rest.astype(BF16)
    lower = (rest - middle.astype(F32)).astype(BF16)
    row = iota((SEGS + 8, 1), 0)
    plane, slot = row >> 3, row & 7
    off_x = jnp.where(plane >= 6, 1, jnp.where(plane >= 3, 0, -1))
    off_z = plane - 3 * (off_x + 1) - 1
    place_x = (coord_ref[0] + off_x) & (size_x - 1)
    place_z = (coord_ref[2] + off_z) & (size_z - 1)
    used = jnp.logical_and(slot < ATOM_DEV, row < SEGS)
    columns = []
    for position in range(POS_Y):
        atom = ((place_x * size_y + position) * size_z + place_z) * ATOM_DEV + slot
        atom = jnp.where(used, atom, -1)
        hot = jnp.where(iota((SEGS + 8, atoms), 1) == atom, 1.0, 0.0).astype(BF16)
        column = lax.dot_general(hot, lower, LAST, preferred_element_type=F32)
        column = column + lax.dot_general(hot, middle, LAST, preferred_element_type=F32)
        columns.append(column + lax.dot_general(hot, upper, LAST, preferred_element_type=F32))
    table_ref[...] = jnp.concatenate(columns, axis=1)[:SEGS]


def in_vmem(count):
    return [pl.BlockSpec(memory_space=pltpu.VMEM)] * count


def call(kernel, shapes, scratch, cost, *operands):
    flops, traffic = cost
    return pl.pallas_call(
        kernel,
        out_shape=[jax.ShapeDtypeStruct(s, k) for s, k in shapes],
        in_specs=[pl.BlockSpec(memory_space=pltpu.SMEM)] + in_vmem(len(operands) - 1),
        out_specs=in_vmem(len(shapes)),
        scratch_shapes=scratch,
        compiler_params=pltpu.CompilerParams(vmem_limit_bytes=VMEM_LIMIT),
        cost_estimate=pl.CostEstimate(flops=flops, bytes_accessed=traffic, transcendentals=0),
    )(*operands)


def add_kernel(left_ref, right_ref, sum_ref):
    sum_ref[...] = left_ref[...] + right_ref[...]


def total(left, right):
    return pl.pallas_call(
        add_kernel,
        out_shape=jax.ShapeDtypeStruct(left.shape, F32),
        in_specs=in_vmem(2),
        out_specs=in_vmem(1)[0],
        compiler_params=pltpu.CompilerParams(vmem_limit_bytes=VMEM_LIMIT),
        cost_estimate=pl.CostEstimate(flops=8000000000, bytes_accessed=80000000, transcendentals=0),
    )(left, right)


def swap_inside(value, axis):
    count = lax.axis_size(axis)
    return lax.ppermute(value, axis, [(i, i ^ 1) for i in range(count)])


def across(place, count):
    return (place + 1 if place % 2 else place - 1) % count


def swap_across(value, axis):
    count = lax.axis_size(axis)
    return lax.ppermute(value, axis, [(i, across(i, count)) for i in range(count)])


def is_corner(x, z, count_x, count_z):
    upper = x if x % 2 == 0 else across(x, count_x)
    return upper % (count_x // 2) == 0 and z in (0, count_z - 1)


def swap_corners(value):
    count_x, count_z = lax.axis_size("gx"), lax.axis_size("gz")
    pairs = []
    for x in range(count_x):
        for z in range(count_z):
            corner = is_corner(x, z, count_x, count_z)
            to_z = across(z, count_z) if corner else z
            pairs.append((x * count_z + z, across(x, count_x) * count_z + to_z))
    return lax.ppermute(value, ("gx", "gz"), pairs)


def swap_far_faces(value, corners):
    count_x, count_z = lax.axis_size("gx"), lax.axis_size("gz")
    pairs = [
        (x * count_z + z, across(x, count_x) * count_z + z)
        for x in range(count_x)
        for z in range(count_z)
        if is_corner(x, z, count_x, count_z) == corners
    ]
    return lax.ppermute(value, ("gx", "gz"), pairs)


def body(
    orbitals, potential, proj_values, point_cell, point_owner, point_slot, point_count, atom_energy
):
    sizes = tuple(lax.axis_size(axis) for axis in ("gx", "gy", "gz"))
    places = [lax.axis_index(axis) for axis in ("gx", "gy", "gz")]
    points = proj_values.shape[1]
    coord = jnp.stack(
        [p.astype(jnp.int32) for p in places]
        + [(p % 2).astype(jnp.int32) for p in places]
        + [point_count[0], jnp.int32(0)]
    )
    odd_x, odd_z = places[0] % 2 == 1, places[2] % 2 == 1
    some = point_count[0] > 0

    cells_shape = orbitals.shape
    x_shape = (NORB, HALO, SIDE, DEPTH)
    z_shape = (ROWS // 128, 8, 128)
    send_shapes = [
        ((SEGS // 3, 128), F32), ((2 * SEGS // 3, 128), F32), (x_shape, F32), (x_shape, F32), (z_shape, F32), (z_shape, F32)
    ]

    *sends, idx, wts = call(
        lambda *refs: first_kernel(sizes, *refs),
        send_shapes + [((8, points), jnp.int32), ((POS_Y * NPROJ, points), F32)],
        [], (600_000_000, 2_000_000),
        coord, orbitals, proj_values,
        point_cell.reshape(1, points), point_owner.reshape(1, points), point_slot.reshape(1, points),
    )
    def staged(trade, share, halo_trade, halo, finish, rest, otherwise, beside=tuple):
        come, extra = lax.optimization_barrier((trade(share), beside()))
        share, halo = lax.optimization_barrier((share, halo))
        arriving = halo_trade(halo)
        after = lax.cond(some, rest, otherwise, finish(come))
        return lax.optimization_barrier(((*after, *extra), arriving))

    def zeros_like_last(sums):
        return jnp.zeros((SEGS, 128), F32), jnp.zeros(z_shape, F32)

    def zeros_like_z(own):
        return (*zeros_like_last(own), jnp.zeros(x_shape, F32))

    def zeros_like_y(own):
        return (*zeros_like_z(own), jnp.zeros(cells_shape, F32))

    def zeros_like_x(own):
        return (*zeros_like_y(own), jnp.zeros(x_shape, F32))

    def zeros_like_all(pair):
        return (*zeros_like_x(pair[:, :2]), jnp.zeros(z_shape, F32), jnp.zeros(x_shape, F32))

    def zeros_like_first(pair):
        return (*zeros_like_all(pair), jnp.zeros((SEGS, 128), F32))

    def energies():
        return call(
            lambda *refs: energy_kernel(sizes, *refs), [((SEGS, 128), F32)], [],
            (600_000_000, 200_000), coord, atom_energy,
        )

    def exchange(cells, give, keep, xa, xb, za, zb, energy):
        first = energy is None
        place = jnp.arange(2, dtype=jnp.int32)[:, None, None, None]

        def inside_again(sums):
            own, far = sums
            beyond_x = swap_inside(jnp.where(odd_x, own[0], own[1]), "gx")
            rows = jnp.where(
                odd_z,
                jnp.where(odd_x, jnp.stack([beyond_x[0], own[0, 0], own[1, 0]]),
                          jnp.stack([own[0, 0], own[1, 0], beyond_x[0]])),
                jnp.where(odd_x, jnp.stack([beyond_x[1], own[0, 1], own[1, 1]]),
                          jnp.stack([own[0, 1], own[1, 1], beyond_x[1]])),
            )
            return tuple(call(
                table_kernel, [((SEGS, 128), F32), (z_shape, F32)], [], (100_000, 300_000),
                coord, own, beyond_x, swap_inside(rows, "gz"), far,
            ))

        def along_z_across(own):
            rest, corner_in = staged(
                lambda v: swap_across(v, "gz"),
                jnp.concatenate([own.reshape(4, 8, 128), zb], axis=0),
                lambda v: swap_far_faces(v, True), xb,
                lambda far: (total(own, far[:4].reshape(2, 2, 8, 128)), far),
                inside_again, zeros_like_last,
            )
            return (*rest, corner_in)

        def along_y_across(own):
            rest, yb_in = staged(
                lambda v: swap_across(v, "gy"), own, lambda v: swap_across(v, "gy"), cells,
                lambda come: total(own, come), along_z_across, zeros_like_z,
            )
            return (*rest, yb_in)

        def along_y_inside(own):
            rest, xa_in = staged(
                lambda v: swap_inside(v, "gy"), own, lambda v: swap_inside(v, "gx"), xa,
                lambda come: total(own, come), along_y_across, zeros_like_y,
            )
            return (*rest, xa_in)

        def along_z_inside(pair):
            come = swap_inside(
                jnp.concatenate([jnp.where(odd_z, pair[:, 0], pair[:, 2]), za], axis=0), "gz"
            )
            middle = pair[:, 1] + come[:2]
            own = jnp.where(
                odd_z,
                jnp.stack([middle, pair[:, 2]], axis=1),
                jnp.stack([pair[:, 0], middle], axis=1),
            )
            rest, xb_in = staged(
                swap_corners, own, lambda v: swap_far_faces(v, False), xb,
                lambda come: total(own, come), along_y_inside, zeros_like_x,
                energies if first else tuple,
            )
            return (*rest[:5], come[2:], xb_in, *rest[5:])

        rest, ya_in = staged(
            lambda v: swap_inside(v, "gx"), give, lambda v: swap_inside(v, "gy"), cells,
            lambda come: total(
                keep.reshape(2, 3, 8, 128),
                jnp.where(place == 1 - places[0] % 2, come.reshape(1, 3, 8, 128), 0.0),
            ),
            along_z_inside, zeros_like_first if first else zeros_like_all,
        )
        table, zb_in, corner_in, yb_in, xa_in, za_in, xb_in, *made = rest
        energy = made[0] if first else energy
        return energy, table, xa_in, xb_in, corner_in, ya_in, yb_in, za_in, zb_in

    half_width = (highest - cutoff) / 2.0
    middle = (highest + cutoff) / 2.0
    sigma_first = half_width / (lowest - middle)
    sigma_now = sigma_first
    previous, current, energy = None, orbitals, None
    scratch = [
        pltpu.VMEM((ROWS, DEPTH), F32),
        pltpu.VMEM((ROWS, DEPTH), F32),
        pltpu.VMEM((NORB, SIDE + 2 * HALO, SIDE, DEPTH), F32),
        pltpu.VMEM((3, NORB, SIDE, SIDE, DEPTH), F32),
    ]
    for degree_index in range(DEGREE):
        if degree_index == 0:
            scales = (sigma_first / half_width, middle, 0.0)
        else:
            sigma_next = 1.0 / (2.0 / sigma_first - sigma_now)
            scales = (2.0 * sigma_next / half_width, middle, sigma_now * sigma_next)
            sigma_now = sigma_next
        last = degree_index == DEGREE - 1
        came = exchange(current, *sends, energy)
        energy = came[0]
        before = [] if previous is None else [previous]
        results = call(
            lambda *refs, scales=scales, last=last: step_kernel(scales, last, *refs),
            [(cells_shape, F32)] + ([] if last else send_shapes),
            scratch, (1_500_000_000, 4_000_000),
            coord, current, *before, potential, idx, wts, *came,
        )
        previous, current = current, results[0]
        if not last:
            sends = results[1:]
    return current


def solution(mesh):
    return jax.shard_map(
        body,
        mesh=mesh,
        in_specs=(
            P(None, "gx", "gy", "gz"),
            P("gx", "gy", "gz"),
            P(None, ("gx", "gy", "gz")),
            P(("gx", "gy", "gz")),
            P(("gx", "gy", "gz")),
            P(("gx", "gy", "gz")),
            P(("gx", "gy", "gz")),
            P(),
        ),
        out_specs=P(None, "gx", "gy", "gz"),
        check_vma=False,
    )
```

```python
import jax
import jax.numpy as jnp
from jax import lax
from jax.experimental import pallas as pl
from jax.experimental.pallas import tpu as pltpu
from jax.sharding import PartitionSpec as P

DEGREE = 3
ATOM_DEV = 5
NORB = 8
NPROJ = 4
SIDE = 8
DEPTH = 128
HALO = 6
ROWS = NORB * SIDE * SIDE
PLANES = 9
SEGS = PLANES * 8
CHUNK = 256
POS_Y = 4
VMEM_LIMIT = 20 * 1024 * 1024

stencil_terms = (
    -5369.0 / 1800.0,
    12.0 / 7.0,
    -15.0 / 56.0,
    10.0 / 189.0,
    -1.0 / 112.0,
    2.0 / 1925.0,
    -1.0 / 16632.0,
)
lowest = -3.5
cutoff = 1.5
highest = 13.0

F32 = jnp.float32
BF16 = jnp.bfloat16
LAST = (((1,), (1,)), ((), ()))
FIRST = (((0,), (0,)), ((), ()))


def iota(shape, dim):
    return lax.broadcasted_iota(jnp.int32, shape, dim)


def one_hot(index_row, rows, kind):
    hit = iota((rows, index_row.shape[1]), 0) == index_row
    return jnp.where(hit, 1.0, 0.0).astype(kind)


def split_two(value):
    upper = value.astype(BF16)
    return upper, (value - upper.astype(F32)).astype(BF16)


def sample_partials(cells, idx_ref, wts_ref):
    upper, lower = split_two(cells)
    both = jnp.concatenate([upper, lower], axis=1)
    points = idx_ref.shape[1]
    total = jnp.zeros((SEGS + 8, 128), F32)
    for first in range(0, points, CHUNK):
        span = slice(first, first + CHUNK)
        hot_z = one_hot(idx_ref[0:1, span], DEPTH, BF16)
        picked = jnp.dot(both, jnp.concatenate([hot_z, hot_z], axis=0), preferred_element_type=F32)
        mask = iota((SIDE * SIDE, CHUNK), 0) == idx_ref[1:2, span]
        picked = picked.reshape(NORB, SIDE * SIDE, CHUNK)
        sampled = jnp.sum(jnp.where(mask[None], picked, 0.0), axis=1)
        weights = wts_ref[:, span]
        parts = [weights[k : k + 1] * sampled for k in range(POS_Y * NPROJ)]
        upper_c, lower_c = split_two(jnp.concatenate(parts, axis=0))
        hot_seg = one_hot(idx_ref[2:3, span], SEGS + 8, BF16)
        total = total + lax.dot_general(hot_seg, upper_c, LAST, preferred_element_type=F32)
        total = total + lax.dot_general(hot_seg, lower_c, LAST, preferred_element_type=F32)
    return total[:SEGS]


def scatter_returned(coefs, idx_ref, wts_ref, nonlocal_ref):
    wide = jnp.concatenate([coefs, jnp.zeros((128 - SEGS, 128), F32)], axis=0)
    upper, lower = split_two(wide.T)
    both = jnp.concatenate([upper, lower], axis=1)
    points = idx_ref.shape[1]
    for first in range(0, points, CHUNK):
        span = slice(first, first + CHUNK)
        hot_seg = one_hot(idx_ref[2:3, span], 128, BF16)
        spread = jnp.dot(both, jnp.concatenate([hot_seg, hot_seg], axis=0), preferred_element_type=F32)
        weights = wts_ref[:, span]
        returned = weights[0:1] * spread[0:NORB]
        for k in range(1, POS_Y * NPROJ):
            returned = returned + weights[k : k + 1] * spread[k * NORB : (k + 1) * NORB]
        upper_r = returned.astype(BF16).astype(F32)
        lower_r = returned - upper_r
        mask = iota((SIDE * SIDE, CHUNK), 0) == idx_ref[1:2, span]
        tall = [
            jnp.where(mask, value[o : o + 1], 0.0).astype(BF16)
            for value in (upper_r, lower_r)
            for o in range(NORB)
        ]
        hot_z = one_hot(idx_ref[0:1, span], DEPTH, BF16)
        placed = lax.dot_general(
            jnp.concatenate(tall, axis=0), hot_z, LAST, preferred_element_type=F32
        )
        placed = placed[:ROWS] + placed[ROWS:]
        if first == 0:
            nonlocal_ref[...] = placed
        else:
            nonlocal_ref[...] += placed


def write_parts(coord_ref, table, send_ref, keep_ref):
    rows = SEGS // 3
    odd_x = coord_ref[3] == 1
    below, same, above = table[:rows], table[rows : 2 * rows], table[2 * rows :]
    send_ref[...] = jnp.where(odd_x, below, above)
    kept = [jnp.where(odd_x, same, below), jnp.where(odd_x, above, same)]
    keep_ref[...] = jnp.concatenate(kept, axis=0)


def write_sends(coord_ref, cells_ref, xa_ref, xb_ref, za_ref, zb_ref):
    bx, bz = coord_ref[3], coord_ref[5]
    xa_ref[...] = cells_ref[:, pl.ds(2 - 2 * bx, HALO)]
    xb_ref[...] = cells_ref[:, pl.ds(2 * bx, HALO)]
    turned = cells_ref[...].reshape(ROWS, DEPTH).T
    near, far = turned[0:8], turned[DEPTH - 8 : DEPTH]
    to_a = jnp.where(bz == 1, near, far)
    to_b = jnp.where(bz == 1, far, near)
    for k in range(ROWS // 128):
        za_ref[k] = to_a[:, k * 128 : (k + 1) * 128]
        zb_ref[k] = to_b[:, k * 128 : (k + 1) * 128]


def offset_of(place, own, count):
    remain = (place - own) & (count - 1)
    return jnp.where(remain == 0, 1, jnp.where(remain == 1, 2, 0))


def first_kernel(
    sizes, coord_ref, cells_ref, proj_ref, cell_ref, owner_ref, slot_ref,
    give_ref, keep_ref, xa_ref, xb_ref, za_ref, zb_ref, idx_ref, wts_ref,
):
    size_x, size_y, size_z = sizes
    points = proj_ref.shape[1]
    shift_z = size_z.bit_length() - 1
    shift_x = shift_z + size_y.bit_length() - 1
    cell, owner = cell_ref[...], owner_ref[...]
    off_x = offset_of(owner >> shift_x, coord_ref[0], size_x)
    place_y = (owner >> shift_z) & (size_y - 1)
    off_z = offset_of(owner & (size_z - 1), coord_ref[2], size_z)
    idx_ref[0:1, :] = cell & (DEPTH - 1)
    idx_ref[1:2, :] = cell >> 7
    idx_ref[2:3, :] = (off_x * 3 + off_z) * 8 + slot_ref[...]
    idx_ref[3:8, :] = jnp.zeros((5, points), jnp.int32)
    live = iota((1, points), 1) < coord_ref[6]
    for position in range(POS_Y):
        here = jnp.logical_and(live, place_y == position)
        wts_ref[position * NPROJ : (position + 1) * NPROJ, :] = jnp.where(here, proj_ref[...], 0.0)
    table = sample_partials(cells_ref[...].reshape(ROWS, DEPTH), idx_ref, wts_ref)
    write_parts(coord_ref, table, give_ref, keep_ref)
    write_sends(coord_ref, cells_ref, xa_ref, xb_ref, za_ref, zb_ref)


def band(shape, distance):
    result = jnp.zeros(shape, F32)
    for k in range(1, HALO + 1):
        result = jnp.where(distance == k, stencil_terms[k], result)
    return result


def step_kernel(
    scales, last, coord_ref, cells_ref, *refs
):
    gain, middle, back = scales
    refs = list(refs)
    before_ref = refs.pop(0) if back else None
    (pot_ref, idx_ref, wts_ref, energy_ref, table_ref,
     xa_in, xb_in, corner_in, ya_in, yb_in, za_in, zb_in) = refs[:12]
    outs = refs[12:]
    if last:
        next_ref, nonlocal_ref, z_ref, xext, yext = outs
    else:
        (next_ref, give_ref, keep_ref, xa_ref, xb_ref, za_ref, zb_ref,
         nonlocal_ref, z_ref, xext, yext) = outs
    bx, by, bz = coord_ref[3], coord_ref[4], coord_ref[5]
    odd_z = bz == 1

    coefs = table_ref[...] * energy_ref[...]
    scatter_returned(coefs, idx_ref, wts_ref, nonlocal_ref)

    rows = cells_ref[...].reshape(ROWS, DEPTH)
    along = iota((DEPTH, DEPTH), 1) - iota((DEPTH, DEPTH), 0)
    z_part = jnp.dot(
        rows, band((DEPTH, DEPTH), jnp.abs(along)),
        precision=lax.Precision.HIGHEST, preferred_element_type=F32,
    )
    chunks = ROWS // 128
    from_a = jnp.concatenate([za_in[k] for k in range(chunks)], axis=1)
    from_b = jnp.concatenate([zb_in[k] for k in range(chunks)], axis=1)
    faces = jnp.concatenate(
        [jnp.where(odd_z, from_a, from_b), jnp.where(odd_z, from_b, from_a)], axis=0
    )
    face_row, face_col = iota((16, DEPTH), 0), iota((16, DEPTH), 1)
    distance = jnp.where(face_row < 8, face_col + 8 - face_row, DEPTH + face_row - 8 - face_col)
    z_ref[...] = z_part + jnp.dot(
        faces.T, band((16, DEPTH), distance),
        precision=lax.Precision.HIGHEST, preferred_element_type=F32,
    )

    xext[:, HALO : HALO + SIDE] = cells_ref[...]
    xext[:, pl.ds((1 - bx) * (HALO + SIDE), HALO)] = xa_in[...]
    xext[:, pl.ds(bx * (HALO + SIDE), HALO)] = xb_in[...] + corner_in[...]
    yext[1] = cells_ref[...]
    yext[2 - 2 * by] = ya_in[...]
    yext[2 * by] = yb_in[...]

    pot = pot_ref[...] - (middle + 1.5 * stencil_terms[0])
    row = iota((SIDE, SIDE, DEPTH), 1)
    for o in range(NORB):
        here = xext[o, HALO : HALO + SIDE]
        left, right = yext[0, o], yext[2, o]
        laplace = z_ref[o * 64 : (o + 1) * 64, :].reshape(SIDE, SIDE, DEPTH)
        for k in range(1, HALO + 1):
            pair = xext[o, HALO + k : HALO + k + SIDE] + xext[o, HALO - k : HALO - k + SIDE]
            up = pltpu.roll(jnp.where(row < k, right, here), SIDE - k, 1)
            down = pltpu.roll(jnp.where(row >= SIDE - k, left, here), k, 1)
            laplace = laplace + stencil_terms[k] * (pair + (up + down))
        nonlocal_part = nonlocal_ref[o * 64 : (o + 1) * 64, :].reshape(SIDE, SIDE, DEPTH)
        result = gain * (pot * here - 0.5 * laplace + nonlocal_part)
        if back:
            result = result - back * before_ref[o]
        next_ref[o] = result
    if not last:
        table = sample_partials(next_ref[...].reshape(ROWS, DEPTH), idx_ref, wts_ref)
        write_parts(coord_ref, table, give_ref, keep_ref)
        write_sends(coord_ref, next_ref, xa_ref, xb_ref, za_ref, zb_ref)


def table_kernel(coord_ref, own_ref, px_ref, pz_ref, far_ref, table_ref, face_ref):
    odd_x, odd_z = coord_ref[3] == 1, coord_ref[5] == 1
    own0, own1, other = own_ref[0], own_ref[1], px_ref[...]
    rows_x = (
        jnp.where(odd_x, other, own0),
        jnp.where(odd_x, own0, own1),
        jnp.where(odd_x, own1, other),
    )
    planes = []
    for k in range(3):
        low, high, beyond = rows_x[k][0], rows_x[k][1], pz_ref[k]
        planes += [
            jnp.where(odd_z, beyond, low),
            jnp.where(odd_z, low, high),
            jnp.where(odd_z, high, beyond),
        ]
    table_ref[...] = jnp.concatenate(planes, axis=0)
    face_ref[...] = far_ref[4:]


def energy_kernel(sizes, coord_ref, energy_ref, table_ref):
    size_x, size_y, size_z = sizes
    atoms = energy_ref.shape[1]
    values = jnp.concatenate(
        [jnp.broadcast_to(energy_ref[j : j + 1, :], (NORB, atoms)) for j in range(NPROJ)], axis=0
    )
    upper = values.astype(BF16)
    rest = values - upper.astype(F32)
    middle = rest.astype(BF16)
    lower = (rest - middle.astype(F32)).astype(BF16)
    row = iota((SEGS + 8, 1), 0)
    plane, slot = row >> 3, row & 7
    off_x = jnp.where(plane >= 6, 1, jnp.where(plane >= 3, 0, -1))
    off_z = plane - 3 * (off_x + 1) - 1
    place_x = (coord_ref[0] + off_x) & (size_x - 1)
    place_z = (coord_ref[2] + off_z) & (size_z - 1)
    used = jnp.logical_and(slot < ATOM_DEV, row < SEGS)
    columns = []
    for position in range(POS_Y):
        atom = ((place_x * size_y + position) * size_z + place_z) * ATOM_DEV + slot
        atom = jnp.where(used, atom, -1)
        hot = jnp.where(iota((SEGS + 8, atoms), 1) == atom, 1.0, 0.0).astype(BF16)
        column = lax.dot_general(hot, lower, LAST, preferred_element_type=F32)
        column = column + lax.dot_general(hot, middle, LAST, preferred_element_type=F32)
        columns.append(column + lax.dot_general(hot, upper, LAST, preferred_element_type=F32))
    table_ref[...] = jnp.concatenate(columns, axis=1)[:SEGS]


def in_vmem(count):
    return [pl.BlockSpec(memory_space=pltpu.VMEM)] * count


def call(kernel, shapes, scratch, cost, *operands):
    flops, traffic = cost
    return pl.pallas_call(
        kernel,
        out_shape=[jax.ShapeDtypeStruct(s, k) for s, k in shapes],
        in_specs=[pl.BlockSpec(memory_space=pltpu.SMEM)] + in_vmem(len(operands) - 1),
        out_specs=in_vmem(len(shapes)),
        scratch_shapes=scratch,
        compiler_params=pltpu.CompilerParams(vmem_limit_bytes=VMEM_LIMIT),
        cost_estimate=pl.CostEstimate(flops=flops, bytes_accessed=traffic, transcendentals=0),
    )(*operands)


def add_kernel(left_ref, right_ref, sum_ref):
    sum_ref[...] = left_ref[...] + right_ref[...]


def total(left, right):
    return pl.pallas_call(
        add_kernel,
        out_shape=jax.ShapeDtypeStruct(left.shape, F32),
        in_specs=in_vmem(2),
        out_specs=in_vmem(1)[0],
        compiler_params=pltpu.CompilerParams(vmem_limit_bytes=VMEM_LIMIT),
        cost_estimate=pl.CostEstimate(flops=8000000000, bytes_accessed=80000000, transcendentals=0),
    )(left, right)


def swap_inside(value, axis):
    count = lax.axis_size(axis)
    return lax.ppermute(value, axis, [(i, i ^ 1) for i in range(count)])


def across(place, count):
    return (place + 1 if place % 2 else place - 1) % count


def swap_across(value, axis):
    count = lax.axis_size(axis)
    return lax.ppermute(value, axis, [(i, across(i, count)) for i in range(count)])


def is_corner(x, z, count_x, count_z):
    upper = x if x % 2 == 0 else across(x, count_x)
    return upper % (count_x // 2) == 0 and z in (0, count_z - 1)


def swap_corners(value):
    count_x, count_z = lax.axis_size("gx"), lax.axis_size("gz")
    pairs = []
    for x in range(count_x):
        for z in range(count_z):
            corner = is_corner(x, z, count_x, count_z)
            to_z = across(z, count_z) if corner else z
            pairs.append((x * count_z + z, across(x, count_x) * count_z + to_z))
    return lax.ppermute(value, ("gx", "gz"), pairs)


def swap_far_faces(value, corners):
    count_x, count_z = lax.axis_size("gx"), lax.axis_size("gz")
    pairs = [
        (x * count_z + z, across(x, count_x) * count_z + z)
        for x in range(count_x)
        for z in range(count_z)
        if is_corner(x, z, count_x, count_z) == corners
    ]
    return lax.ppermute(value, ("gx", "gz"), pairs)


def body(
    orbitals, potential, proj_values, point_cell, point_owner, point_slot, point_count, atom_energy
):
    sizes = tuple(lax.axis_size(axis) for axis in ("gx", "gy", "gz"))
    places = [lax.axis_index(axis) for axis in ("gx", "gy", "gz")]
    points = proj_values.shape[1]
    coord = jnp.stack(
        [p.astype(jnp.int32) for p in places]
        + [(p % 2).astype(jnp.int32) for p in places]
        + [point_count[0], jnp.int32(0)]
    )
    odd_x, odd_z = places[0] % 2 == 1, places[2] % 2 == 1
    some = point_count[0] > 0

    cells_shape = orbitals.shape
    x_shape = (NORB, HALO, SIDE, DEPTH)
    z_shape = (ROWS // 128, 8, 128)
    send_shapes = [
        ((SEGS // 3, 128), F32), ((2 * SEGS // 3, 128), F32), (x_shape, F32), (x_shape, F32), (z_shape, F32), (z_shape, F32)
    ]

    *sends, idx, wts = call(
        lambda *refs: first_kernel(sizes, *refs),
        send_shapes + [((8, points), jnp.int32), ((POS_Y * NPROJ, points), F32)],
        [], (600_000_000, 2_000_000),
        coord, orbitals, proj_values,
        point_cell.reshape(1, points), point_owner.reshape(1, points), point_slot.reshape(1, points),
    )
    def staged(trade, share, halo_trade, halo, finish, rest, otherwise, beside=tuple):
        come, extra = lax.optimization_barrier((trade(share), beside()))
        share, halo = lax.optimization_barrier((share, halo))
        arriving = halo_trade(halo)
        after = lax.cond(some, rest, otherwise, finish(come))
        return lax.optimization_barrier(((*after, *extra), arriving))

    def zeros_like_last(sums):
        return jnp.zeros((SEGS, 128), F32), jnp.zeros(z_shape, F32)

    def zeros_like_z(own):
        return (*zeros_like_last(own), jnp.zeros(x_shape, F32))

    def zeros_like_y(own):
        return (*zeros_like_z(own), jnp.zeros(cells_shape, F32))

    def zeros_like_x(own):
        return (*zeros_like_y(own), jnp.zeros(x_shape, F32))

    def energies():
        return call(
            lambda *refs: energy_kernel(sizes, *refs), [((SEGS, 128), F32)], [],
            (600_000_000, 200_000), coord, atom_energy,
        )

    def exchange(cells, give, keep, xa, xb, za, zb, energy):
        first = energy is None
        place = jnp.arange(2, dtype=jnp.int32)[:, None, None, None]

        def inside_again(sums):
            own, far = sums
            beyond_x = swap_inside(jnp.where(odd_x, own[0], own[1]), "gx")
            rows = jnp.where(
                odd_z,
                jnp.where(odd_x, jnp.stack([beyond_x[0], own[0, 0], own[1, 0]]),
                          jnp.stack([own[0, 0], own[1, 0], beyond_x[0]])),
                jnp.where(odd_x, jnp.stack([beyond_x[1], own[0, 1], own[1, 1]]),
                          jnp.stack([own[0, 1], own[1, 1], beyond_x[1]])),
            )
            return tuple(call(
                table_kernel, [((SEGS, 128), F32), (z_shape, F32)], [], (100_000, 300_000),
                coord, own, beyond_x, swap_inside(rows, "gz"), far,
            ))

        def along_z_across(own):
            rest, corner_in = staged(
                lambda v: swap_across(v, "gz"),
                jnp.concatenate([own.reshape(4, 8, 128), zb], axis=0),
                lambda v: swap_far_faces(v, True), xb,
                lambda far: (total(own, far[:4].reshape(2, 2, 8, 128)), far),
                inside_again, zeros_like_last,
            )
            return (*rest, corner_in)

        def along_y_across(own):
            rest, yb_in = staged(
                lambda v: swap_across(v, "gy"), own, lambda v: swap_across(v, "gy"), cells,
                lambda come: total(own, come), along_z_across, zeros_like_z,
            )
            return (*rest, yb_in)

        def along_y_inside(own):
            rest, xa_in = staged(
                lambda v: swap_inside(v, "gy"), own, lambda v: swap_inside(v, "gx"), xa,
                lambda come: total(own, come), along_y_across, zeros_like_y,
            )
            return (*rest, xa_in)

        cells, give = lax.optimization_barrier((cells, give))
        come = swap_inside(give, "gx").reshape(1, 3, 8, 128)
        pair = total(
            keep.reshape(2, 3, 8, 128), jnp.where(place == 1 - places[0] % 2, come, 0.0)
        )
        come = swap_inside(
            jnp.concatenate([jnp.where(odd_z, pair[:, 0], pair[:, 2]), za], axis=0), "gz"
        )
        za_in = come[2:]
        middle = pair[:, 1] + come[:2]
        own = jnp.where(
            odd_z,
            jnp.stack([middle, pair[:, 2]], axis=1),
            jnp.stack([pair[:, 0], middle], axis=1),
        )
        ya_in = swap_inside(cells, "gy")
        rest, xb_in = staged(
            swap_corners, own, lambda v: swap_far_faces(v, False), xb,
            lambda come: total(own, come), along_y_inside, zeros_like_x,
            lambda: (ya_in, *(energies() if first else ())),
        )
        table, zb_in, corner_in, yb_in, xa_in, ya_in, *made = rest
        energy = made[0] if first else energy
        return energy, table, xa_in, xb_in, corner_in, ya_in, yb_in, za_in, zb_in

    half_width = (highest - cutoff) / 2.0
    middle = (highest + cutoff) / 2.0
    sigma_first = half_width / (lowest - middle)
    sigma_now = sigma_first
    previous, current, energy = None, orbitals, None
    scratch = [
        pltpu.VMEM((ROWS, DEPTH), F32),
        pltpu.VMEM((ROWS, DEPTH), F32),
        pltpu.VMEM((NORB, SIDE + 2 * HALO, SIDE, DEPTH), F32),
        pltpu.VMEM((3, NORB, SIDE, SIDE, DEPTH), F32),
    ]
    for degree_index in range(DEGREE):
        if degree_index == 0:
            scales = (sigma_first / half_width, middle, 0.0)
        else:
            sigma_next = 1.0 / (2.0 / sigma_first - sigma_now)
            scales = (2.0 * sigma_next / half_width, middle, sigma_now * sigma_next)
            sigma_now = sigma_next
        last = degree_index == DEGREE - 1
        came = exchange(current, *sends, energy)
        energy = came[0]
        before = [] if previous is None else [previous]
        results = call(
            lambda *refs, scales=scales, last=last: step_kernel(scales, last, *refs),
            [(cells_shape, F32)] + ([] if last else send_shapes),
            scratch, (1_500_000_000, 4_000_000),
            coord, current, *before, potential, idx, wts, *came,
        )
        previous, current = current, results[0]
        if not last:
            sends = results[1:]
    return current


def solution(mesh):
    return jax.shard_map(
        body,
        mesh=mesh,
        in_specs=(
            P(None, "gx", "gy", "gz"),
            P("gx", "gy", "gz"),
            P(None, ("gx", "gy", "gz")),
            P(("gx", "gy", "gz")),
            P(("gx", "gy", "gz")),
            P(("gx", "gy", "gz")),
            P(("gx", "gy", "gz")),
            P(),
        ),
        out_specs=P(None, "gx", "gy", "gz"),
        check_vma=False,
    )
```

```python
import jax
import jax.numpy as jnp
from jax import lax
from jax.experimental import pallas as pl
from jax.experimental.pallas import tpu as pltpu
from jax.sharding import PartitionSpec as P

DEGREE = 3
ATOM_DEV = 5
NORB = 8
NPROJ = 4
SIDE = 8
DEPTH = 128
HALO = 6
ROWS = NORB * SIDE * SIDE
PLANES = 9
SEGS = PLANES * 8
CHUNK = 1024
POS_Y = 4
VMEM_LIMIT = 20 * 1024 * 1024

stencil_terms = (
    -5369.0 / 1800.0,
    12.0 / 7.0,
    -15.0 / 56.0,
    10.0 / 189.0,
    -1.0 / 112.0,
    2.0 / 1925.0,
    -1.0 / 16632.0,
)
lowest = -3.5
cutoff = 1.5
highest = 13.0

F32 = jnp.float32
BF16 = jnp.bfloat16
LAST = (((1,), (1,)), ((), ()))
FIRST = (((0,), (0,)), ((), ()))


def iota(shape, dim):
    return lax.broadcasted_iota(jnp.int32, shape, dim)


def one_hot(index_row, rows, kind):
    hit = iota((rows, index_row.shape[1]), 0) == index_row
    return jnp.where(hit, 1.0, 0.0).astype(kind)


def split_two(value):
    upper = value.astype(BF16)
    return upper, (value - upper.astype(F32)).astype(BF16)


def sample_partials(cells, idx_ref, wts_ref):
    upper, lower = split_two(cells)
    both = jnp.concatenate([upper, lower], axis=1)
    points = idx_ref.shape[1]
    total = jnp.zeros((SEGS + 8, 128), F32)
    for first in range(0, points, CHUNK):
        span = slice(first, first + CHUNK)
        hot_z = one_hot(idx_ref[0:1, span], DEPTH, BF16)
        picked = jnp.dot(both, jnp.concatenate([hot_z, hot_z], axis=0), preferred_element_type=F32)
        mask = iota((SIDE * SIDE, CHUNK), 0) == idx_ref[1:2, span]
        picked = picked.reshape(NORB, SIDE * SIDE, CHUNK)
        sampled = jnp.sum(jnp.where(mask[None], picked, 0.0), axis=1)
        weights = wts_ref[:, span]
        parts = [weights[k : k + 1] * sampled for k in range(POS_Y * NPROJ)]
        upper_c, lower_c = split_two(jnp.concatenate(parts, axis=0))
        hot_seg = one_hot(idx_ref[2:3, span], SEGS + 8, BF16)
        total = total + lax.dot_general(hot_seg, upper_c, LAST, preferred_element_type=F32)
        total = total + lax.dot_general(hot_seg, lower_c, LAST, preferred_element_type=F32)
    return total[:SEGS]


def scatter_returned(coefs, idx_ref, wts_ref, nonlocal_ref):
    wide = jnp.concatenate([coefs, jnp.zeros((128 - SEGS, 128), F32)], axis=0)
    upper, lower = split_two(wide.T)
    both = jnp.concatenate([upper, lower], axis=1)
    points = idx_ref.shape[1]
    sums = []
    for first in range(0, points, CHUNK):
        span = slice(first, first + CHUNK)
        hot_seg = one_hot(idx_ref[2:3, span], 128, BF16)
        spread = jnp.dot(both, jnp.concatenate([hot_seg, hot_seg], axis=0), preferred_element_type=F32)
        weights = wts_ref[:, span]
        returned = weights[0:1] * spread[0:NORB]
        for k in range(1, POS_Y * NPROJ):
            returned = returned + weights[k : k + 1] * spread[k * NORB : (k + 1) * NORB]
        upper_r, lower_r = split_two(returned)
        hot_xy = one_hot(idx_ref[1:2, span], SIDE * SIDE, BF16)
        tall = jnp.concatenate(
            [
                jnp.concatenate([hot_xy * value[o : o + 1] for o in range(NORB)], axis=0)
                for value in (upper_r, lower_r)
            ],
            axis=1,
        )
        hot_z = one_hot(idx_ref[0:1, span], DEPTH, BF16)
        placed = lax.dot_general(
            tall, jnp.concatenate([hot_z, hot_z], axis=1), LAST, preferred_element_type=F32
        )
        sums.append(placed)
    nonlocal_ref[...] = sum(sums[1:], sums[0])


def write_parts(coord_ref, table, send_ref, keep_ref):
    rows = SEGS // 3
    odd_x = coord_ref[3] == 1
    below, same, above = table[:rows], table[rows : 2 * rows], table[2 * rows :]
    send_ref[...] = jnp.where(odd_x, below, above)
    kept = [jnp.where(odd_x, same, below), jnp.where(odd_x, above, same)]
    keep_ref[...] = jnp.concatenate(kept, axis=0)


def write_sends(coord_ref, cells_ref, xa_ref, xb_ref, za_ref, zb_ref):
    bx, bz = coord_ref[3], coord_ref[5]
    xa_ref[...] = cells_ref[:, pl.ds(2 - 2 * bx, HALO)]
    xb_ref[...] = cells_ref[:, pl.ds(2 * bx, HALO)]
    turned = cells_ref[...].reshape(ROWS, DEPTH).T
    near, far = turned[0:8], turned[DEPTH - 8 : DEPTH]
    to_a = jnp.where(bz == 1, near, far)
    to_b = jnp.where(bz == 1, far, near)
    for k in range(ROWS // 128):
        za_ref[k] = to_a[:, k * 128 : (k + 1) * 128]
        zb_ref[k] = to_b[:, k * 128 : (k + 1) * 128]


def offset_of(place, own, count):
    remain = (place - own) & (count - 1)
    return jnp.where(remain == 0, 1, jnp.where(remain == 1, 2, 0))


def first_kernel(
    sizes, coord_ref, cells_ref, proj_ref, cell_ref, owner_ref, slot_ref,
    give_ref, keep_ref, xa_ref, xb_ref, za_ref, zb_ref, idx_ref, wts_ref,
):
    size_x, size_y, size_z = sizes
    points = proj_ref.shape[1]
    shift_z = size_z.bit_length() - 1
    shift_x = shift_z + size_y.bit_length() - 1
    cell, owner = cell_ref[...], owner_ref[...]
    off_x = offset_of(owner >> shift_x, coord_ref[0], size_x)
    place_y = (owner >> shift_z) & (size_y - 1)
    off_z = offset_of(owner & (size_z - 1), coord_ref[2], size_z)
    idx_ref[0:1, :] = cell & (DEPTH - 1)
    idx_ref[1:2, :] = cell >> 7
    idx_ref[2:3, :] = (off_x * 3 + off_z) * 8 + slot_ref[...]
    idx_ref[3:8, :] = jnp.zeros((5, points), jnp.int32)
    live = iota((1, points), 1) < coord_ref[6]
    for position in range(POS_Y):
        here = jnp.logical_and(live, place_y == position)
        wts_ref[position * NPROJ : (position + 1) * NPROJ, :] = jnp.where(here, proj_ref[...], 0.0)
    table = sample_partials(cells_ref[...].reshape(ROWS, DEPTH), idx_ref, wts_ref)
    write_parts(coord_ref, table, give_ref, keep_ref)
    write_sends(coord_ref, cells_ref, xa_ref, xb_ref, za_ref, zb_ref)


def band(shape, distance):
    result = jnp.zeros(shape, F32)
    for k in range(1, HALO + 1):
        result = jnp.where(distance == k, stencil_terms[k], result)
    return result


def step_kernel(
    scales, last, coord_ref, cells_ref, *refs
):
    gain, middle, back = scales
    refs = list(refs)
    before_ref = refs.pop(0) if back else None
    (pot_ref, idx_ref, wts_ref, energy_ref, table_ref,
     xa_in, xb_in, corner_in, ya_in, yb_in, za_in, zb_in) = refs[:12]
    outs = refs[12:]
    if last:
        next_ref, nonlocal_ref, z_ref, xext, yext = outs
    else:
        (next_ref, give_ref, keep_ref, xa_ref, xb_ref, za_ref, zb_ref,
         nonlocal_ref, z_ref, xext, yext) = outs
    bx, by, bz = coord_ref[3], coord_ref[4], coord_ref[5]
    odd_z = bz == 1

    coefs = table_ref[...] * energy_ref[...]
    scatter_returned(coefs, idx_ref, wts_ref, nonlocal_ref)

    rows = cells_ref[...].reshape(ROWS, DEPTH)
    along = iota((DEPTH, DEPTH), 1) - iota((DEPTH, DEPTH), 0)
    z_part = jnp.dot(
        rows, band((DEPTH, DEPTH), jnp.abs(along)),
        precision=lax.Precision.HIGHEST, preferred_element_type=F32,
    )
    chunks = ROWS // 128
    from_a = jnp.concatenate([za_in[k] for k in range(chunks)], axis=1)
    from_b = jnp.concatenate([zb_in[k] for k in range(chunks)], axis=1)
    faces = jnp.concatenate(
        [jnp.where(odd_z, from_a, from_b), jnp.where(odd_z, from_b, from_a)], axis=0
    )
    face_row, face_col = iota((16, DEPTH), 0), iota((16, DEPTH), 1)
    distance = jnp.where(face_row < 8, face_col + 8 - face_row, DEPTH + face_row - 8 - face_col)
    z_ref[...] = z_part + jnp.dot(
        faces.T, band((16, DEPTH), distance),
        precision=lax.Precision.HIGHEST, preferred_element_type=F32,
    )

    xext[:, HALO : HALO + SIDE] = cells_ref[...]
    xext[:, pl.ds((1 - bx) * (HALO + SIDE), HALO)] = xa_in[...]
    xext[:, pl.ds(bx * (HALO + SIDE), HALO)] = xb_in[...] + corner_in[...]
    yext[1] = cells_ref[...]
    yext[2 - 2 * by] = ya_in[...]
    yext[2 * by] = yb_in[...]

    pot = pot_ref[...] - (middle + 1.5 * stencil_terms[0])
    row = iota((SIDE, SIDE, DEPTH), 1)
    for o in range(NORB):
        here = xext[o, HALO : HALO + SIDE]
        left, right = yext[0, o], yext[2, o]
        laplace = z_ref[o * 64 : (o + 1) * 64, :].reshape(SIDE, SIDE, DEPTH)
        for k in range(1, HALO + 1):
            pair = xext[o, HALO + k : HALO + k + SIDE] + xext[o, HALO - k : HALO - k + SIDE]
            up = pltpu.roll(jnp.where(row < k, right, here), SIDE - k, 1)
            down = pltpu.roll(jnp.where(row >= SIDE - k, left, here), k, 1)
            laplace = laplace + stencil_terms[k] * (pair + (up + down))
        nonlocal_part = nonlocal_ref[o * 64 : (o + 1) * 64, :].reshape(SIDE, SIDE, DEPTH)
        result = gain * (pot * here - 0.5 * laplace + nonlocal_part)
        if back:
            result = result - back * before_ref[o]
        next_ref[o] = result
    if not last:
        table = sample_partials(next_ref[...].reshape(ROWS, DEPTH), idx_ref, wts_ref)
        write_parts(coord_ref, table, give_ref, keep_ref)
        write_sends(coord_ref, next_ref, xa_ref, xb_ref, za_ref, zb_ref)


def table_kernel(coord_ref, own_ref, px_ref, pz_ref, far_ref, table_ref, face_ref):
    odd_x, odd_z = coord_ref[3] == 1, coord_ref[5] == 1
    own0, own1, other = own_ref[0], own_ref[1], px_ref[...]
    rows_x = (
        jnp.where(odd_x, other, own0),
        jnp.where(odd_x, own0, own1),
        jnp.where(odd_x, own1, other),
    )
    planes = []
    for k in range(3):
        low, high, beyond = rows_x[k][0], rows_x[k][1], pz_ref[k]
        planes += [
            jnp.where(odd_z, beyond, low),
            jnp.where(odd_z, low, high),
            jnp.where(odd_z, high, beyond),
        ]
    table_ref[...] = jnp.concatenate(planes, axis=0)
    face_ref[...] = far_ref[4:]


def energy_kernel(sizes, coord_ref, energy_ref, table_ref):
    size_x, size_y, size_z = sizes
    atoms = energy_ref.shape[1]
    values = jnp.concatenate(
        [jnp.broadcast_to(energy_ref[j : j + 1, :], (NORB, atoms)) for j in range(NPROJ)], axis=0
    )
    upper = values.astype(BF16)
    rest = values - upper.astype(F32)
    middle = rest.astype(BF16)
    lower = (rest - middle.astype(F32)).astype(BF16)
    row = iota((SEGS + 8, 1), 0)
    plane, slot = row >> 3, row & 7
    off_x = jnp.where(plane >= 6, 1, jnp.where(plane >= 3, 0, -1))
    off_z = plane - 3 * (off_x + 1) - 1
    place_x = (coord_ref[0] + off_x) & (size_x - 1)
    place_z = (coord_ref[2] + off_z) & (size_z - 1)
    used = jnp.logical_and(slot < ATOM_DEV, row < SEGS)
    columns = []
    for position in range(POS_Y):
        atom = ((place_x * size_y + position) * size_z + place_z) * ATOM_DEV + slot
        atom = jnp.where(used, atom, -1)
        hot = jnp.where(iota((SEGS + 8, atoms), 1) == atom, 1.0, 0.0).astype(BF16)
        column = lax.dot_general(hot, lower, LAST, preferred_element_type=F32)
        column = column + lax.dot_general(hot, middle, LAST, preferred_element_type=F32)
        columns.append(column + lax.dot_general(hot, upper, LAST, preferred_element_type=F32))
    table_ref[...] = jnp.concatenate(columns, axis=1)[:SEGS]


def in_vmem(count):
    return [pl.BlockSpec(memory_space=pltpu.VMEM)] * count


def call(kernel, shapes, scratch, cost, *operands):
    flops, traffic = cost
    return pl.pallas_call(
        kernel,
        out_shape=[jax.ShapeDtypeStruct(s, k) for s, k in shapes],
        in_specs=[pl.BlockSpec(memory_space=pltpu.SMEM)] + in_vmem(len(operands) - 1),
        out_specs=in_vmem(len(shapes)),
        scratch_shapes=scratch,
        compiler_params=pltpu.CompilerParams(vmem_limit_bytes=VMEM_LIMIT),
        cost_estimate=pl.CostEstimate(flops=flops, bytes_accessed=traffic, transcendentals=0),
    )(*operands)


def add_kernel(*refs):
    *parts, sum_ref = refs
    sum_ref[...] = sum((part[...] for part in parts[1:]), parts[0][...])


def total(*parts):
    return pl.pallas_call(
        add_kernel,
        out_shape=jax.ShapeDtypeStruct(parts[0].shape, F32),
        in_specs=in_vmem(len(parts)),
        out_specs=in_vmem(1)[0],
        compiler_params=pltpu.CompilerParams(vmem_limit_bytes=VMEM_LIMIT),
        cost_estimate=pl.CostEstimate(flops=8000000000, bytes_accessed=80000000, transcendentals=0),
    )(*parts)


def swap_inside(value, axis):
    count = lax.axis_size(axis)
    return lax.ppermute(value, axis, [(i, i ^ 1) for i in range(count)])


def across(place, count):
    return (place + 1 if place % 2 else place - 1) % count


def swap_across(value, axis):
    count = lax.axis_size(axis)
    return lax.ppermute(value, axis, [(i, across(i, count)) for i in range(count)])


def swap_over(value, axis):
    count = lax.axis_size(axis)
    return lax.ppermute(value, axis, [(i, (i + 2) % count) for i in range(count)])


def is_corner(x, z, count_x, count_z):
    upper = x if x % 2 == 0 else across(x, count_x)
    return upper % (count_x // 2) == 0 and z in (0, count_z - 1)


def swap_corners(value):
    count_x, count_z = lax.axis_size("gx"), lax.axis_size("gz")
    pairs = []
    for x in range(count_x):
        for z in range(count_z):
            corner = is_corner(x, z, count_x, count_z)
            to_z = across(z, count_z) if corner else z
            pairs.append((x * count_z + z, across(x, count_x) * count_z + to_z))
    return lax.ppermute(value, ("gx", "gz"), pairs)


def swap_far_faces(value, corners):
    count_x, count_z = lax.axis_size("gx"), lax.axis_size("gz")
    pairs = [
        (x * count_z + z, across(x, count_x) * count_z + z)
        for x in range(count_x)
        for z in range(count_z)
        if is_corner(x, z, count_x, count_z) == corners
    ]
    return lax.ppermute(value, ("gx", "gz"), pairs)


def body(
    orbitals, potential, proj_values, point_cell, point_owner, point_slot, point_count, atom_energy
):
    sizes = tuple(lax.axis_size(axis) for axis in ("gx", "gy", "gz"))
    places = [lax.axis_index(axis) for axis in ("gx", "gy", "gz")]
    points = proj_values.shape[1]
    coord = jnp.stack(
        [p.astype(jnp.int32) for p in places]
        + [(p % 2).astype(jnp.int32) for p in places]
        + [point_count[0], jnp.int32(0)]
    )
    odd_x, odd_z = places[0] % 2 == 1, places[2] % 2 == 1
    some = point_count[0] > 0

    cells_shape = orbitals.shape
    x_shape = (NORB, HALO, SIDE, DEPTH)
    z_shape = (ROWS // 128, 8, 128)
    send_shapes = [
        ((SEGS // 3, 128), F32), ((2 * SEGS // 3, 128), F32), (x_shape, F32), (x_shape, F32), (z_shape, F32), (z_shape, F32)
    ]

    *sends, idx, wts = call(
        lambda *refs: first_kernel(sizes, *refs),
        send_shapes + [((8, points), jnp.int32), ((POS_Y * NPROJ, points), F32)],
        [], (600_000_000, 2_000_000),
        coord, orbitals, proj_values,
        point_cell.reshape(1, points), point_owner.reshape(1, points), point_slot.reshape(1, points),
    )
    def staged(trade, share, halo_trade, halo, finish, rest, otherwise, beside=tuple):
        come, extra = lax.optimization_barrier((trade(share), beside()))
        share, halo = lax.optimization_barrier((share, halo))
        arriving = halo_trade(halo)
        after = lax.cond(some, rest, otherwise, finish(come))
        return lax.optimization_barrier(((*after, *extra), arriving))

    def zeros_like_last(sums):
        return jnp.zeros((SEGS, 128), F32), jnp.zeros(z_shape, F32)

    def zeros_like_z(own):
        return (*zeros_like_last(own), jnp.zeros(x_shape, F32))

    def zeros_like_y(own):
        return (*zeros_like_z(own), jnp.zeros(cells_shape, F32))

    def energies():
        return call(
            lambda *refs: energy_kernel(sizes, *refs), [((SEGS, 128), F32)], [],
            (600_000_000, 200_000), coord, atom_energy,
        )

    def exchange(cells, give, keep, xa, xb, za, zb, energy):
        first = energy is None
        place = jnp.arange(2, dtype=jnp.int32)[:, None, None, None]

        def inside_again(sums):
            own, far = sums
            beyond_x = swap_inside(jnp.where(odd_x, own[0], own[1]), "gx")
            rows = jnp.where(
                odd_z,
                jnp.where(odd_x, jnp.stack([beyond_x[0], own[0, 0], own[1, 0]]),
                          jnp.stack([own[0, 0], own[1, 0], beyond_x[0]])),
                jnp.where(odd_x, jnp.stack([beyond_x[1], own[0, 1], own[1, 1]]),
                          jnp.stack([own[0, 1], own[1, 1], beyond_x[1]])),
            )
            return tuple(call(
                table_kernel, [((SEGS, 128), F32), (z_shape, F32)], [], (100_000, 300_000),
                coord, own, beyond_x, swap_inside(rows, "gz"), far,
            ))

        def along_z_across(own):
            rest, corner_in = staged(
                lambda v: swap_across(v, "gz"),
                jnp.concatenate([own.reshape(4, 8, 128), zb], axis=0),
                lambda v: swap_far_faces(v, True), xb,
                lambda far: (total(own, far[:4].reshape(2, 2, 8, 128)), far),
                inside_again, zeros_like_last,
            )
            return (*rest, corner_in)

        def along_y(own):
            rest, yb_in = staged(
                lambda v: (swap_inside(v, "gy"), swap_across(v, "gy"), swap_over(v, "gy")), own,
                lambda v: swap_across(v, "gy"), cells,
                lambda come: total(own, *come), along_z_across, zeros_like_z,
            )
            return (*rest, yb_in)

        cells, xa, give = lax.optimization_barrier((cells, xa, give))
        come = swap_inside(give, "gx").reshape(1, 3, 8, 128)
        pair = total(
            keep.reshape(2, 3, 8, 128), jnp.where(place == 1 - places[0] % 2, come, 0.0)
        )
        come = swap_inside(
            jnp.concatenate([jnp.where(odd_z, pair[:, 0], pair[:, 2]), za], axis=0), "gz"
        )
        za_in = come[2:]
        middle = pair[:, 1] + come[:2]
        own = jnp.where(
            odd_z,
            jnp.stack([middle, pair[:, 2]], axis=1),
            jnp.stack([pair[:, 0], middle], axis=1),
        )
        ya_in, xa_in = swap_inside(cells, "gy"), swap_inside(xa, "gx")
        rest, xb_in = staged(
            swap_corners, own, lambda v: swap_far_faces(v, False), xb,
            lambda come: total(own, come), along_y, zeros_like_y,
            lambda: (xa_in, ya_in, *(energies() if first else ())),
        )
        table, zb_in, corner_in, yb_in, xa_in, ya_in, *made = rest
        energy = made[0] if first else energy
        return energy, table, xa_in, xb_in, corner_in, ya_in, yb_in, za_in, zb_in

    half_width = (highest - cutoff) / 2.0
    middle = (highest + cutoff) / 2.0
    sigma_first = half_width / (lowest - middle)
    sigma_now = sigma_first
    previous, current, energy = None, orbitals, None
    scratch = [
        pltpu.VMEM((ROWS, DEPTH), F32),
        pltpu.VMEM((ROWS, DEPTH), F32),
        pltpu.VMEM((NORB, SIDE + 2 * HALO, SIDE, DEPTH), F32),
        pltpu.VMEM((3, NORB, SIDE, SIDE, DEPTH), F32),
    ]
    for degree_index in range(DEGREE):
        if degree_index == 0:
            scales = (sigma_first / half_width, middle, 0.0)
        else:
            sigma_next = 1.0 / (2.0 / sigma_first - sigma_now)
            scales = (2.0 * sigma_next / half_width, middle, sigma_now * sigma_next)
            sigma_now = sigma_next
        last = degree_index == DEGREE - 1
        came = exchange(current, *sends, energy)
        energy = came[0]
        before = [] if previous is None else [previous]
        results = call(
            lambda *refs, scales=scales, last=last: step_kernel(scales, last, *refs),
            [(cells_shape, F32)] + ([] if last else send_shapes),
            scratch, (1_500_000_000, 4_000_000),
            coord, current, *before, potential, idx, wts, *came,
        )
        previous, current = current, results[0]
        if not last:
            sends = results[1:]
    return current


def solution(mesh):
    return jax.shard_map(
        body,
        mesh=mesh,
        in_specs=(
            P(None, "gx", "gy", "gz"),
            P("gx", "gy", "gz"),
            P(None, ("gx", "gy", "gz")),
            P(("gx", "gy", "gz")),
            P(("gx", "gy", "gz")),
            P(("gx", "gy", "gz")),
            P(("gx", "gy", "gz")),
            P(),
        ),
        out_specs=P(None, "gx", "gy", "gz"),
        check_vma=False,
    )
```

```python
import jax
import jax.numpy as jnp
from jax import lax
from jax.experimental import pallas as pl
from jax.experimental.pallas import tpu as pltpu
from jax.sharding import PartitionSpec as P

DEGREE = 3
ATOM_DEV = 5
NORB = 8
NPROJ = 4
SIDE = 8
DEPTH = 128
HALO = 6
ROWS = NORB * SIDE * SIDE
PLANES = 9
SEGS = PLANES * 8
CHUNK = 1024
POS_Y = 4
VMEM_LIMIT = 20 * 1024 * 1024

stencil_terms = (
    -5369.0 / 1800.0,
    12.0 / 7.0,
    -15.0 / 56.0,
    10.0 / 189.0,
    -1.0 / 112.0,
    2.0 / 1925.0,
    -1.0 / 16632.0,
)
lowest = -3.5
cutoff = 1.5
highest = 13.0

F32 = jnp.float32
BF16 = jnp.bfloat16
LAST = (((1,), (1,)), ((), ()))
FIRST = (((0,), (0,)), ((), ()))


def iota(shape, dim):
    return lax.broadcasted_iota(jnp.int32, shape, dim)


def one_hot(index_row, rows, kind):
    hit = iota((rows, index_row.shape[1]), 0) == index_row
    return jnp.where(hit, 1.0, 0.0).astype(kind)


def split_two(value):
    upper = value.astype(BF16)
    return upper, (value - upper.astype(F32)).astype(BF16)


def sample_partials(cells, idx_ref, wts_ref):
    upper, lower = split_two(cells)
    both = jnp.concatenate([upper, lower], axis=1)
    points = idx_ref.shape[1]
    total = jnp.zeros((SEGS + 8, 128), F32)
    for first in range(0, points, CHUNK):
        span = slice(first, first + CHUNK)
        hot_z = one_hot(idx_ref[0:1, span], DEPTH, BF16)
        picked = jnp.dot(both, jnp.concatenate([hot_z, hot_z], axis=0), preferred_element_type=F32)
        mask = iota((SIDE * SIDE, CHUNK), 0) == idx_ref[1:2, span]
        picked = picked.reshape(NORB, SIDE * SIDE, CHUNK)
        sampled = jnp.sum(jnp.where(mask[None], picked, 0.0), axis=1)
        weights = wts_ref[:, span]
        parts = [weights[k : k + 1] * sampled for k in range(POS_Y * NPROJ)]
        upper_c, lower_c = split_two(jnp.concatenate(parts, axis=0))
        hot_seg = one_hot(idx_ref[2:3, span], SEGS + 8, BF16)
        total = total + lax.dot_general(hot_seg, upper_c, LAST, preferred_element_type=F32)
        total = total + lax.dot_general(hot_seg, lower_c, LAST, preferred_element_type=F32)
    return total[:SEGS]


def scatter_returned(coefs, idx_ref, wts_ref, nonlocal_ref):
    wide = jnp.concatenate([coefs, jnp.zeros((128 - SEGS, 128), F32)], axis=0)
    upper, lower = split_two(wide.T)
    both = jnp.concatenate([upper, lower], axis=1)
    points = idx_ref.shape[1]
    sums = []
    for first in range(0, points, CHUNK):
        span = slice(first, first + CHUNK)
        hot_seg = one_hot(idx_ref[2:3, span], 128, BF16)
        spread = jnp.dot(both, jnp.concatenate([hot_seg, hot_seg], axis=0), preferred_element_type=F32)
        weights = wts_ref[:, span]
        returned = weights[0:1] * spread[0:NORB]
        for k in range(1, POS_Y * NPROJ):
            returned = returned + weights[k : k + 1] * spread[k * NORB : (k + 1) * NORB]
        upper_r, lower_r = split_two(returned)
        hot_xy = one_hot(idx_ref[1:2, span], SIDE * SIDE, BF16)
        tall = jnp.concatenate(
            [
                jnp.concatenate([hot_xy * value[o : o + 1] for o in range(NORB)], axis=0)
                for value in (upper_r, lower_r)
            ],
            axis=1,
        )
        hot_z = one_hot(idx_ref[0:1, span], DEPTH, BF16)
        placed = lax.dot_general(
            tall, jnp.concatenate([hot_z, hot_z], axis=1), LAST, preferred_element_type=F32
        )
        sums.append(placed)
    nonlocal_ref[...] = sum(sums[1:], sums[0])


def write_parts(coord_ref, table, send_ref, keep_ref):
    rows = SEGS // 3
    odd_x = coord_ref[3] == 1
    below, same, above = table[:rows], table[rows : 2 * rows], table[2 * rows :]
    send_ref[...] = jnp.where(odd_x, below, above)
    kept = [jnp.where(odd_x, same, below), jnp.where(odd_x, above, same)]
    keep_ref[...] = jnp.concatenate(kept, axis=0)


def write_sends(coord_ref, cells_ref, xa_ref, xb_ref, za_ref, zb_ref):
    bx, bz = coord_ref[3], coord_ref[5]
    xa_ref[...] = cells_ref[:, pl.ds(2 - 2 * bx, HALO)]
    xb_ref[...] = cells_ref[:, pl.ds(2 * bx, HALO)]
    turned = cells_ref[...].reshape(ROWS, DEPTH).T
    near, far = turned[0:8], turned[DEPTH - 8 : DEPTH]
    to_a = jnp.where(bz == 1, near, far)
    to_b = jnp.where(bz == 1, far, near)
    for k in range(ROWS // 128):
        za_ref[k] = to_a[:, k * 128 : (k + 1) * 128]
        zb_ref[k] = to_b[:, k * 128 : (k + 1) * 128]


def offset_of(place, own, count):
    remain = (place - own) & (count - 1)
    return jnp.where(remain == 0, 1, jnp.where(remain == 1, 2, 0))


def first_kernel(
    sizes, coord_ref, cells_ref, proj_ref, cell_ref, owner_ref, slot_ref,
    give_ref, keep_ref, xa_ref, xb_ref, za_ref, zb_ref, idx_ref, wts_ref,
):
    size_x, size_y, size_z = sizes
    points = proj_ref.shape[1]
    shift_z = size_z.bit_length() - 1
    shift_x = shift_z + size_y.bit_length() - 1
    cell, owner = cell_ref[...], owner_ref[...]
    off_x = offset_of(owner >> shift_x, coord_ref[0], size_x)
    place_y = (owner >> shift_z) & (size_y - 1)
    off_z = offset_of(owner & (size_z - 1), coord_ref[2], size_z)
    idx_ref[0:1, :] = cell & (DEPTH - 1)
    idx_ref[1:2, :] = cell >> 7
    idx_ref[2:3, :] = (off_x * 3 + off_z) * 8 + slot_ref[...]
    idx_ref[3:8, :] = jnp.zeros((5, points), jnp.int32)
    live = iota((1, points), 1) < coord_ref[6]
    for position in range(POS_Y):
        here = jnp.logical_and(live, place_y == position)
        wts_ref[position * NPROJ : (position + 1) * NPROJ, :] = jnp.where(here, proj_ref[...], 0.0)
    table = sample_partials(cells_ref[...].reshape(ROWS, DEPTH), idx_ref, wts_ref)
    write_parts(coord_ref, table, give_ref, keep_ref)
    write_sends(coord_ref, cells_ref, xa_ref, xb_ref, za_ref, zb_ref)


def band(shape, distance):
    result = jnp.zeros(shape, F32)
    for k in range(1, HALO + 1):
        result = jnp.where(distance == k, stencil_terms[k], result)
    return result


def step_kernel(
    scales, last, coord_ref, cells_ref, *refs
):
    gain, middle, back = scales
    refs = list(refs)
    before_ref = refs.pop(0) if back else None
    (pot_ref, idx_ref, wts_ref, energy_ref, table_ref,
     xa_in, xb_in, corner_in, ya_in, yb_in, za_in, zb_in) = refs[:12]
    outs = refs[12:]
    if last:
        next_ref, nonlocal_ref, z_ref, xext, yext = outs
    else:
        (next_ref, give_ref, keep_ref, xa_ref, xb_ref, za_ref, zb_ref,
         nonlocal_ref, z_ref, xext, yext) = outs
    bx, by, bz = coord_ref[3], coord_ref[4], coord_ref[5]
    odd_z = bz == 1

    coefs = table_ref[...] * energy_ref[...]
    scatter_returned(coefs, idx_ref, wts_ref, nonlocal_ref)

    rows = cells_ref[...].reshape(ROWS, DEPTH)
    along = iota((DEPTH, DEPTH), 1) - iota((DEPTH, DEPTH), 0)
    z_part = jnp.dot(
        rows, band((DEPTH, DEPTH), jnp.abs(along)),
        precision=lax.Precision.HIGHEST, preferred_element_type=F32,
    )
    chunks = ROWS // 128
    from_a = jnp.concatenate([za_in[k] for k in range(chunks)], axis=1)
    from_b = jnp.concatenate([zb_in[k] for k in range(chunks)], axis=1)
    faces = jnp.concatenate(
        [jnp.where(odd_z, from_a, from_b), jnp.where(odd_z, from_b, from_a)], axis=0
    )
    face_row, face_col = iota((16, DEPTH), 0), iota((16, DEPTH), 1)
    distance = jnp.where(face_row < 8, face_col + 8 - face_row, DEPTH + face_row - 8 - face_col)
    z_ref[...] = z_part + jnp.dot(
        faces.T, band((16, DEPTH), distance),
        precision=lax.Precision.HIGHEST, preferred_element_type=F32,
    )

    xext[:, HALO : HALO + SIDE] = cells_ref[...]
    xext[:, pl.ds((1 - bx) * (HALO + SIDE), HALO)] = xa_in[...]
    xext[:, pl.ds(bx * (HALO + SIDE), HALO)] = xb_in[...] + corner_in[...]
    yext[1] = cells_ref[...]
    yext[2 - 2 * by] = ya_in[...]
    yext[2 * by] = yb_in[...]

    pot = pot_ref[...] - (middle + 1.5 * stencil_terms[0])
    row = iota((SIDE, SIDE, DEPTH), 1)
    for o in range(NORB):
        here = xext[o, HALO : HALO + SIDE]
        left, right = yext[0, o], yext[2, o]
        laplace = z_ref[o * 64 : (o + 1) * 64, :].reshape(SIDE, SIDE, DEPTH)
        for k in range(1, HALO + 1):
            pair = xext[o, HALO + k : HALO + k + SIDE] + xext[o, HALO - k : HALO - k + SIDE]
            up = pltpu.roll(jnp.where(row < k, right, here), SIDE - k, 1)
            down = pltpu.roll(jnp.where(row >= SIDE - k, left, here), k, 1)
            laplace = laplace + stencil_terms[k] * (pair + (up + down))
        nonlocal_part = nonlocal_ref[o * 64 : (o + 1) * 64, :].reshape(SIDE, SIDE, DEPTH)
        result = gain * (pot * here - 0.5 * laplace + nonlocal_part)
        if back:
            result = result - back * before_ref[o]
        next_ref[o] = result
    if not last:
        table = sample_partials(next_ref[...].reshape(ROWS, DEPTH), idx_ref, wts_ref)
        write_parts(coord_ref, table, give_ref, keep_ref)
        write_sends(coord_ref, next_ref, xa_ref, xb_ref, za_ref, zb_ref)


def table_kernel(coord_ref, own_ref, px_ref, pz_ref, far_ref, table_ref, face_ref):
    odd_x, odd_z = coord_ref[3] == 1, coord_ref[5] == 1
    own0, own1, other = own_ref[0], own_ref[1], px_ref[...]
    rows_x = (
        jnp.where(odd_x, other, own0),
        jnp.where(odd_x, own0, own1),
        jnp.where(odd_x, own1, other),
    )
    planes = []
    for k in range(3):
        low, high, beyond = rows_x[k][0], rows_x[k][1], pz_ref[k]
        planes += [
            jnp.where(odd_z, beyond, low),
            jnp.where(odd_z, low, high),
            jnp.where(odd_z, high, beyond),
        ]
    table_ref[...] = jnp.concatenate(planes, axis=0)
    face_ref[...] = far_ref[4:]


def energy_kernel(sizes, coord_ref, energy_ref, table_ref):
    size_x, size_y, size_z = sizes
    atoms = energy_ref.shape[1]
    values = jnp.concatenate(
        [jnp.broadcast_to(energy_ref[j : j + 1, :], (NORB, atoms)) for j in range(NPROJ)], axis=0
    )
    upper = values.astype(BF16)
    rest = values - upper.astype(F32)
    middle = rest.astype(BF16)
    lower = (rest - middle.astype(F32)).astype(BF16)
    row = iota((SEGS + 8, 1), 0)
    plane, slot = row >> 3, row & 7
    off_x = jnp.where(plane >= 6, 1, jnp.where(plane >= 3, 0, -1))
    off_z = plane - 3 * (off_x + 1) - 1
    place_x = (coord_ref[0] + off_x) & (size_x - 1)
    place_z = (coord_ref[2] + off_z) & (size_z - 1)
    used = jnp.logical_and(slot < ATOM_DEV, row < SEGS)
    columns = []
    for position in range(POS_Y):
        atom = ((place_x * size_y + position) * size_z + place_z) * ATOM_DEV + slot
        atom = jnp.where(used, atom, -1)
        hot = jnp.where(iota((SEGS + 8, atoms), 1) == atom, 1.0, 0.0).astype(BF16)
        column = lax.dot_general(hot, lower, LAST, preferred_element_type=F32)
        column = column + lax.dot_general(hot, middle, LAST, preferred_element_type=F32)
        columns.append(column + lax.dot_general(hot, upper, LAST, preferred_element_type=F32))
    table_ref[...] = jnp.concatenate(columns, axis=1)[:SEGS]


def in_vmem(count):
    return [pl.BlockSpec(memory_space=pltpu.VMEM)] * count


def call(kernel, shapes, scratch, cost, *operands):
    flops, traffic = cost
    return pl.pallas_call(
        kernel,
        out_shape=[jax.ShapeDtypeStruct(s, k) for s, k in shapes],
        in_specs=[pl.BlockSpec(memory_space=pltpu.SMEM)] + in_vmem(len(operands) - 1),
        out_specs=in_vmem(len(shapes)),
        scratch_shapes=scratch,
        compiler_params=pltpu.CompilerParams(vmem_limit_bytes=VMEM_LIMIT),
        cost_estimate=pl.CostEstimate(flops=flops, bytes_accessed=traffic, transcendentals=0),
    )(*operands)


def add_kernel(left_ref, right_ref, sum_ref):
    sum_ref[...] = left_ref[...] + right_ref[...]


def total(left, right):
    return pl.pallas_call(
        add_kernel,
        out_shape=jax.ShapeDtypeStruct(left.shape, F32),
        in_specs=in_vmem(2),
        out_specs=in_vmem(1)[0],
        compiler_params=pltpu.CompilerParams(vmem_limit_bytes=VMEM_LIMIT),
        cost_estimate=pl.CostEstimate(flops=8000000000, bytes_accessed=80000000, transcendentals=0),
    )(left, right)


def swap_inside(value, axis):
    count = lax.axis_size(axis)
    return lax.ppermute(value, axis, [(i, i ^ 1) for i in range(count)])


def across(place, count):
    return (place + 1 if place % 2 else place - 1) % count


def swap_across(value, axis):
    count = lax.axis_size(axis)
    return lax.ppermute(value, axis, [(i, across(i, count)) for i in range(count)])


def is_corner(x, z, count_x, count_z):
    upper = x if x % 2 == 0 else across(x, count_x)
    return upper % (count_x // 2) == 0 and z in (0, count_z - 1)


def swap_corners(value):
    count_x, count_z = lax.axis_size("gx"), lax.axis_size("gz")
    pairs = []
    for x in range(count_x):
        for z in range(count_z):
            corner = is_corner(x, z, count_x, count_z)
            to_z = across(z, count_z) if corner else z
            pairs.append((x * count_z + z, across(x, count_x) * count_z + to_z))
    return lax.ppermute(value, ("gx", "gz"), pairs)


def swap_far_faces(value, corners):
    count_x, count_z = lax.axis_size("gx"), lax.axis_size("gz")
    pairs = [
        (x * count_z + z, across(x, count_x) * count_z + z)
        for x in range(count_x)
        for z in range(count_z)
        if is_corner(x, z, count_x, count_z) == corners
    ]
    return lax.ppermute(value, ("gx", "gz"), pairs)


def body(
    orbitals, potential, proj_values, point_cell, point_owner, point_slot, point_count, atom_energy
):
    sizes = tuple(lax.axis_size(axis) for axis in ("gx", "gy", "gz"))
    places = [lax.axis_index(axis) for axis in ("gx", "gy", "gz")]
    points = proj_values.shape[1]
    coord = jnp.stack(
        [p.astype(jnp.int32) for p in places]
        + [(p % 2).astype(jnp.int32) for p in places]
        + [point_count[0], jnp.int32(0)]
    )
    odd_x, odd_z = places[0] % 2 == 1, places[2] % 2 == 1
    some = point_count[0] > 0

    cells_shape = orbitals.shape
    x_shape = (NORB, HALO, SIDE, DEPTH)
    z_shape = (ROWS // 128, 8, 128)
    send_shapes = [
        ((SEGS // 3, 128), F32), ((2 * SEGS // 3, 128), F32), (x_shape, F32), (x_shape, F32), (z_shape, F32), (z_shape, F32)
    ]

    *sends, idx, wts = call(
        lambda *refs: first_kernel(sizes, *refs),
        send_shapes + [((8, points), jnp.int32), ((POS_Y * NPROJ, points), F32)],
        [], (600_000_000, 2_000_000),
        coord, orbitals, proj_values,
        point_cell.reshape(1, points), point_owner.reshape(1, points), point_slot.reshape(1, points),
    )
    def staged(trade, share, halo_trade, halo, finish, rest, otherwise, beside=tuple):
        come, extra = lax.optimization_barrier((trade(share), beside()))
        share, halo = lax.optimization_barrier((share, halo))
        arriving = halo_trade(halo)
        after = lax.cond(some, rest, otherwise, finish(come))
        return lax.optimization_barrier(((*after, *extra), arriving))

    def energies():
        return call(
            lambda *refs: energy_kernel(sizes, *refs), [((SEGS, 128), F32)], [],
            (600_000_000, 200_000), coord, atom_energy,
        )

    def exchange(cells, give, keep, xa, xb, za, zb, energy):
        first = energy is None
        place = jnp.arange(2, dtype=jnp.int32)[:, None, None, None]

        def zeros_like_last(sums):
            made = (jnp.zeros((SEGS, 128), F32),) if first else ()
            return (jnp.zeros((SEGS, 128), F32), jnp.zeros(z_shape, F32), *made)

        def zeros_like_z(own):
            return (*zeros_like_last(own), jnp.zeros(x_shape, F32))

        def zeros_like_y(own):
            return (*zeros_like_z(own), jnp.zeros(cells_shape, F32))

        def zeros_like_x(own):
            return (*zeros_like_y(own), jnp.zeros(x_shape, F32))

        def inside_again(sums):
            own, far = sums
            beyond_x = swap_inside(jnp.where(odd_x, own[0], own[1]), "gx")
            made = energies() if first else ()
            beyond_x, made = lax.optimization_barrier((beyond_x, tuple(made)))
            rows = jnp.where(
                odd_z,
                jnp.where(odd_x, jnp.stack([beyond_x[0], own[0, 0], own[1, 0]]),
                          jnp.stack([own[0, 0], own[1, 0], beyond_x[0]])),
                jnp.where(odd_x, jnp.stack([beyond_x[1], own[0, 1], own[1, 1]]),
                          jnp.stack([own[0, 1], own[1, 1], beyond_x[1]])),
            )
            laid = call(
                table_kernel, [((SEGS, 128), F32), (z_shape, F32)], [], (100_000, 300_000),
                coord, own, beyond_x, swap_inside(rows, "gz"), far,
            )
            return (*laid, *made)

        def along_z_across(own):
            rest, corner_in = staged(
                lambda v: swap_across(v, "gz"),
                jnp.concatenate([own.reshape(4, 8, 128), zb], axis=0),
                lambda v: swap_far_faces(v, True), xb,
                lambda far: (total(own, far[:4].reshape(2, 2, 8, 128)), far),
                inside_again, zeros_like_last,
            )
            return (*rest, corner_in)

        def along_y_across(own):
            rest, yb_in = staged(
                lambda v: swap_across(v, "gy"), own, lambda v: swap_across(v, "gy"), cells,
                lambda come: total(own, come), along_z_across, zeros_like_z,
            )
            return (*rest, yb_in)

        def along_y_inside(own):
            rest, xa_in = staged(
                lambda v: swap_inside(v, "gy"), own, lambda v: swap_inside(v, "gx"), xa,
                lambda come: total(own, come), along_y_across, zeros_like_y,
            )
            return (*rest, xa_in)

        cells, give = lax.optimization_barrier((cells, give))
        come = swap_inside(give, "gx").reshape(1, 3, 8, 128)
        pair = total(
            keep.reshape(2, 3, 8, 128), jnp.where(place == 1 - places[0] % 2, come, 0.0)
        )
        come = swap_inside(
            jnp.concatenate([jnp.where(odd_z, pair[:, 0], pair[:, 2]), za], axis=0), "gz"
        )
        za_in = come[2:]
        middle = pair[:, 1] + come[:2]
        own = jnp.where(
            odd_z,
            jnp.stack([middle, pair[:, 2]], axis=1),
            jnp.stack([pair[:, 0], middle], axis=1),
        )
        ya_in = swap_inside(cells, "gy")
        rest, xb_in = staged(
            swap_corners, own, lambda v: swap_far_faces(v, False), xb,
            lambda come: total(own, come), along_y_inside, zeros_like_x,
            lambda: (ya_in,),
        )
        table, zb_in, *made, corner_in, yb_in, xa_in, ya_in = rest
        energy = made[0] if first else energy
        return energy, table, xa_in, xb_in, corner_in, ya_in, yb_in, za_in, zb_in

    half_width = (highest - cutoff) / 2.0
    middle = (highest + cutoff) / 2.0
    sigma_first = half_width / (lowest - middle)
    sigma_now = sigma_first
    previous, current, energy = None, orbitals, None
    scratch = [
        pltpu.VMEM((ROWS, DEPTH), F32),
        pltpu.VMEM((ROWS, DEPTH), F32),
        pltpu.VMEM((NORB, SIDE + 2 * HALO, SIDE, DEPTH), F32),
        pltpu.VMEM((3, NORB, SIDE, SIDE, DEPTH), F32),
    ]
    for degree_index in range(DEGREE):
        if degree_index == 0:
            scales = (sigma_first / half_width, middle, 0.0)
        else:
            sigma_next = 1.0 / (2.0 / sigma_first - sigma_now)
            scales = (2.0 * sigma_next / half_width, middle, sigma_now * sigma_next)
            sigma_now = sigma_next
        last = degree_index == DEGREE - 1
        came = exchange(current, *sends, energy)
        energy = came[0]
        before = [] if previous is None else [previous]
        results = call(
            lambda *refs, scales=scales, last=last: step_kernel(scales, last, *refs),
            [(cells_shape, F32)] + ([] if last else send_shapes),
            scratch, (1_500_000_000, 4_000_000),
            coord, current, *before, potential, idx, wts, *came,
        )
        previous, current = current, results[0]
        if not last:
            sends = results[1:]
    return current


def solution(mesh):
    return jax.shard_map(
        body,
        mesh=mesh,
        in_specs=(
            P(None, "gx", "gy", "gz"),
            P("gx", "gy", "gz"),
            P(None, ("gx", "gy", "gz")),
            P(("gx", "gy", "gz")),
            P(("gx", "gy", "gz")),
            P(("gx", "gy", "gz")),
            P(("gx", "gy", "gz")),
            P(),
        ),
        out_specs=P(None, "gx", "gy", "gz"),
        check_vma=False,
    )
```
